512 devices in a mesh: remap: 32 (over z, x), depth: 16 (over y, core).
Axes of the slice: x: 4, y: 8, z: 8, core: 2. Of those that a mesh axis runs over, the one named last changes fastest.
Arguments:
- wavefunction: bfloat16 [512, 256, 256], P('remap'), may hold values from -6 to 6
- right_home: int32 [512], P('remap'), may hold values from 0 to 511, as said below
- term_links: int32 [32, 512], P('depth', 'remap'), may hold values from 0 to 511, as said below
- sector_rows: int32 [128], P('remap'), may hold values from 64 to 256, as said below
- sector_cols: int32 [128], P('remap'), may hold values from 64 to 256, as said below
- left_env: bfloat16 [32, 128, 256, 256], P('depth', 'remap'), may hold values from -0.0625 to 0.0625
- right_env: bfloat16 [32, 128, 256, 256], P('depth', 'remap'), may hold values from -0.375 to 0.375
Outputs:
- applied: bfloat16 [512, 256, 256], P('remap', 'depth')
The draws below stay inside these ranges and needn't reach their ends.
Inputs may be any that keep to these rules, and one draw needn't show every extreme that they name: `right_home`: A permutation of the 512 blocks. Remap device i holds positions i * 16 to (i + 1) * 16 - 1 in both groupings; from one remap device to another go at most 1 block, and some pair of devices carries exactly 1 in every draw. `term_links`: for each term a permutation of the 512 blocks; from one remap device to another go at most 1 block of one term, and some pair carries exactly 1 for every term. `sector_rows`: some sector has all 256 rows. `sector_cols`: some sector has all 256 columns.
All inputs are finite; a program needn't handle non-finite values.
Results may differ from the reference program's by a relative error of at most 0.022.
Values may be sent and summed in bfloat16 or wider, within the bound.
No kernel may reach another device: no remote copies, remote signals or barrier semaphores. Data moves between devices by JAX's collectives and lax.ppermute only.
A program may use at most 64 MiB of HBM per device.

```python
import jax
import jax.numpy as jnp
from jax import lax

DB = 256
GROUP = 4
TERMS_DEV = 2
NB_DEV = 16
NSEC = 128
NB = 512
TERMS = 32
CAP = 1
N_REMAP = 32
N_DEPTH = 16


def spread(key, peers, per_device, capacity):
    key_full, key_rank, key_shuffle, key_slots = jax.random.split(key, 4)
    full_offset = jax.random.randint(key_full, (), 0, peers)
    half_offset = peers // 2
    owners = jnp.arange(peers * capacity) // capacity
    copies = jnp.arange(peers * capacity) % capacity
    ranking = jax.random.permutation(key_rank, peers * capacity)
    ranking = jnp.where(owners == full_offset, -1 - copies, ranking)
    ranking = jnp.where((owners == half_offset) & (copies == 0), -2 - capacity, ranking)
    chosen = owners[jnp.argsort(ranking)[:per_device]]
    offsets = chosen[jax.random.permutation(key_shuffle, per_device)]
    scores = jax.random.randint(key_slots, (peers, per_device), 0, 1 << 20) * per_device
    scores = scores + jnp.arange(per_device)[None, :]
    places = jnp.argsort(scores, axis=1)
    sources = jnp.arange(peers)[:, None]
    targets = (sources + offsets[None, :]) % peers
    target_slot = places[targets, jnp.arange(per_device)[None, :]]
    return (targets * per_device + target_slot).reshape(-1).astype(jnp.int32)


def draw_right_home(key, part):
    key = jax.random.fold_in(key, 11)
    return spread(key, N_REMAP, NB_DEV, CAP)


def draw_term_links(key, part):
    key = jax.random.fold_in(key, 12)
    return jax.vmap(lambda term_index: spread(jax.random.fold_in(key, term_index), N_REMAP, NB_DEV, CAP))(jnp.arange(TERMS))


def draw_sector_rows(key, part):
    key = jax.random.fold_in(key, 21)
    key_sizes, key_full = jax.random.split(key)
    sizes = jax.random.randint(key_sizes, (NSEC,), DB // 4, DB + 1)
    return sizes.at[jax.random.randint(key_full, (), 0, NSEC)].set(DB).astype(jnp.int32)


def draw_sector_cols(key, part):
    key = jax.random.fold_in(key, 22)
    key_sizes, key_full = jax.random.split(key)
    sizes = jax.random.randint(key_sizes, (NSEC,), DB // 4, DB + 1)
    return sizes.at[jax.random.randint(key_full, (), 0, NSEC)].set(DB).astype(jnp.int32)


def levels(stream_key, dims, cuts, smallest, top_value):
    gain, own = 1.0, jax.random.fold_in(stream_key, 6)
    for position, blocks in cuts:
        heights = jnp.exp(jax.random.uniform(jax.random.fold_in(own, position), (blocks,), jnp.float32, smallest / len(cuts), top_value / len(cuts)))
        gain = gain * jnp.repeat(heights, dims[position] // blocks).reshape([-1 if axis == position else 1 for axis in range(len(dims))])
    return gain


def gaussian(key, extent, deviation, bound, pieces=(), kind=jnp.bfloat16):
    result = deviation * jax.random.normal(key, extent, jnp.float32)
    if pieces:
        result = result * levels(key, extent, pieces, -0.22, 0.18)
    return jnp.clip(result, -bound, bound).astype(kind)


def setup_inputs(seed: int = 0) -> dict:
    keys = jax.random.split(jax.random.key(seed), 8)
    wavefunction = gaussian(keys[0], (NB, DB, DB), 1.0, 6.0, ((0, 32),))
    right_home = draw_right_home(jax.random.fold_in(keys[7], 71), 0)
    term_links = draw_term_links(jax.random.fold_in(keys[7], 71), 0)
    sector_rows = draw_sector_rows(jax.random.fold_in(keys[7], 71), 0)
    sector_cols = draw_sector_cols(jax.random.fold_in(keys[7], 71), 0)
    left_env = gaussian(keys[5], (TERMS, NSEC, DB, DB), (DB * TERMS) ** -0.5, 0.0625, ((0, 16), (1, 32)))
    right_env = gaussian(keys[6], (TERMS, NSEC, DB, DB), DB ** -0.5, 0.375, ((0, 16), (1, 32)))
    return dict(wavefunction=wavefunction, right_home=right_home, term_links=term_links, sector_rows=sector_rows, sector_cols=sector_cols, left_env=left_env, right_env=right_env)


def reference(wavefunction, right_home, term_links, sector_rows, sector_cols, left_env, right_env):
    positions = jnp.arange(DB, dtype=jnp.int32)
    row_keep = (positions[None, :] < jnp.repeat(sector_rows, GROUP)[:, None]).astype(jnp.bfloat16)
    masked = wavefunction * row_keep[:, :, None]
    moved = jnp.zeros_like(masked).at[right_home].set(masked)
    col_keep = (positions[None, :] < jnp.repeat(sector_cols, GROUP)[:, None]).astype(jnp.bfloat16)
    moved = (moved * col_keep[:, None, :]).reshape(NSEC, GROUP, DB, DB).astype(jnp.float32)

    def depth_group(accumulated, depth_index):
        left_part = lax.dynamic_slice_in_dim(left_env, depth_index * TERMS_DEV, TERMS_DEV, 0)
        right_part = lax.dynamic_slice_in_dim(right_env, depth_index * TERMS_DEV, TERMS_DEV, 0)
        link_part = lax.dynamic_slice_in_dim(term_links, depth_index * TERMS_DEV, TERMS_DEV, 0)
        partial_value = jnp.zeros((NB, DB, DB), jnp.float32)
        for term_index in range(TERMS_DEV):
            product = jnp.einsum("sgij,sjk->sgik", moved, right_part[term_index].astype(jnp.float32),
                                 precision=lax.Precision.HIGHEST)
            product = product.reshape(NB, DB, DB).astype(jnp.bfloat16)
            placed = jnp.zeros_like(product).at[link_part[term_index]].set(product)
            contrib = jnp.einsum("sij,sgjk->sgik", left_part[term_index].astype(jnp.float32),
                                 placed.reshape(NSEC, GROUP, DB, DB).astype(jnp.float32),
                                 precision=lax.Precision.HIGHEST)
            partial_value = partial_value + contrib.reshape(NB, DB, DB)
        rounded = lax.optimization_barrier(partial_value.astype(jnp.bfloat16)).astype(jnp.float32)
        return accumulated + rounded, None

    total, _ = lax.scan(depth_group, jnp.zeros((NB, DB, DB), jnp.float32),
                        jnp.arange(N_DEPTH, dtype=jnp.int32))
    return (total * row_keep[:, :, None].astype(jnp.float32)).astype(jnp.bfloat16)
```

```python
import functools

import jax
import jax.numpy as jnp
from jax import lax
from jax.experimental import pallas as pl
from jax.experimental.pallas import tpu as pltpu
from jax.sharding import Mesh, PartitionSpec as P

LABEL_ROWS = 16
CHUNK = 128
VMEM_LIMIT = 48 * 1024 * 1024


def spread_kernel(count, core_ref, home_ref, links_ref, rows_ref, wave_ref, out_ref, label_ref):
    slots, half = out_ref.shape[0], wave_ref.shape[1]
    terms = links_ref.shape[0]
    per_sector = count // rows_ref.shape[0]
    core = core_ref[0]

    def clear(peer, carry):
        for kind in range(1 + terms):
            label_ref[kind, peer] = count
        return carry

    lax.fori_loop(0, slots, clear, 0)

    def fill(block, carry):
        home = home_ref[block]
        label_ref[0, lax.div(home, count)] = lax.rem(home, count)
        for term in range(terms):
            link = links_ref[term, block]
            label_ref[1 + term, lax.div(link, count)] = lax.rem(link, count)
        return carry

    lax.fori_loop(0, count, fill, 0)

    lane = lax.broadcasted_iota(jnp.int32, (LABEL_ROWS, out_ref.shape[2]), 1)

    def mark(peer, carry):
        tile = jnp.full(lane.shape, label_ref[0, peer], jnp.int32)
        for term in range(terms):
            tile = jnp.where(lane == 1 + term, label_ref[1 + term, peer], tile)
        out_ref[peer, half:, :] = tile.astype(jnp.float32).astype(jnp.bfloat16)
        return carry

    lax.fori_loop(0, slots, mark, 0)

    row = lax.broadcasted_iota(jnp.int32, wave_ref.shape[1:], 0) + core * half

    def put(block, carry):
        owner = lax.div(home_ref[block], count)
        keep = row < rows_ref[lax.div(block, per_sector)]
        value = wave_ref[block]
        out_ref[owner, 0:half, :] = jnp.where(keep, value, jnp.zeros_like(value))
        return carry

    lax.fori_loop(0, count, put, 0)


def spread(core, right_home, term_links, sector_rows, wavefunction, slots):
    count, extent, width = wavefunction.shape
    half = extent // 2
    smem = pl.BlockSpec(memory_space=pltpu.SMEM)
    return pl.pallas_call(
        functools.partial(spread_kernel, count),
        grid_spec=pltpu.PrefetchScalarGridSpec(
            num_scalar_prefetch=1,
            grid=(1,),
            in_specs=[
                smem,
                smem,
                smem,
                pl.BlockSpec((count, half, width), lambda i, core: (0, core[0], 0)),
            ],
            out_specs=pl.BlockSpec((slots, half + LABEL_ROWS, width), lambda i, core: (0, 0, 0)),
            scratch_shapes=[pltpu.SMEM((1 + term_links.shape[0], slots), jnp.int32)],
        ),
        out_shape=jax.ShapeDtypeStruct((slots, half + LABEL_ROWS, width), jnp.bfloat16),
        compiler_params=pltpu.CompilerParams(vmem_limit_bytes=VMEM_LIMIT),
        name="spread_blocks",
    )(core, right_home, term_links, sector_rows, wavefunction)


def right_kernel(core_ref, from_ref, links_ref, cols_ref, own_ref, other_ref, env_ref, out_ref):
    count = from_ref.shape[0]
    sectors = cols_ref.shape[0]
    per_sector = count // sectors
    terms = links_ref.shape[0]
    half = out_ref.shape[2] // 2
    core = core_ref[0]
    sector = pl.program_id(0)
    own_row = pl.multiple_of(core * half, half)
    other_row = pl.multiple_of((1 - core) * half, half)
    column = lax.broadcasted_iota(jnp.int32, (2 * half, own_ref.shape[2]), 1)
    keep = column < cols_ref[sector]
    for place in range(per_sector):
        block = sector * per_sector + place
        slot = from_ref[block]
        moved = jnp.concatenate([own_ref[slot, 0:half, :], other_ref[slot, 0:half, :]], axis=0)
        moved = jnp.where(keep, moved, jnp.zeros_like(moved))
        for term in range(terms):
            product = jnp.dot(
                moved, env_ref[term, 0], preferred_element_type=jnp.float32
            ).astype(jnp.bfloat16)
            owner = lax.div(links_ref[term, block], count)
            out_ref[owner, term, pl.ds(own_row, half), :] = product[0:half]
            out_ref[owner, term, pl.ds(other_row, half), :] = product[half:]


def right_products(core, source, term_links, sector_cols, own, other, right_env, chunk):
    slots, tall, width = own.shape
    terms, sectors, extent, _ = right_env.shape
    smem = pl.BlockSpec(memory_space=pltpu.SMEM)
    whole = pl.BlockSpec((slots, tall, width), lambda i: (0, 0, 0))
    return pl.pallas_call(
        right_kernel,
        grid=(sectors,),
        in_specs=[
            smem,
            smem,
            smem,
            smem,
            whole,
            whole,
            pl.BlockSpec((terms, 1, extent, CHUNK), lambda i: (0, i, 0, chunk)),
        ],
        out_specs=pl.BlockSpec((slots, terms, extent, CHUNK), lambda i: (0, 0, 0, 0)),
        out_shape=jax.ShapeDtypeStruct((slots, terms, extent, CHUNK), jnp.bfloat16),
        compiler_params=pltpu.CompilerParams(vmem_limit_bytes=VMEM_LIMIT),
        name="right_products",
    )(core, source, term_links, sector_cols, own, other, right_env)


def left_kernel(core_ref, from_ref, placed_ref, env_ref, keep_ref, send_ref):
    terms, count = from_ref.shape
    per_sector = count // pl.num_programs(0)
    chips, _, share, _ = keep_ref.shape
    core = core_ref[0]
    sector = pl.program_id(0)
    left = jnp.concatenate([env_ref[term, 0] for term in range(terms)], axis=1)
    for place in range(per_sector):
        block = sector * per_sector + place
        placed = jnp.concatenate(
            [placed_ref[from_ref[term, block], term] for term in range(terms)], axis=0
        )
        partial = jnp.dot(left, placed, preferred_element_type=jnp.float32).astype(jnp.bfloat16)
        halves = [
            jnp.stack([partial[(2 * c + k) * share : (2 * c + k + 1) * share] for c in range(chips)])
            for k in range(2)
        ]
        keep_ref[:, place] = jnp.where(core == 0, halves[0], halves[1])
        send_ref[:, place] = jnp.where(core == 0, halves[1], halves[0])


def left_products(core, source, arrived, left_env, chips):
    slots, terms, extent, width = arrived.shape
    _, sectors, _, _ = left_env.shape
    count = source.shape[1]
    share = extent // (2 * chips)
    smem = pl.BlockSpec(memory_space=pltpu.SMEM)
    out_spec = pl.BlockSpec((chips, count // sectors, share, width), lambda i: (0, i, 0, 0))
    shape = jax.ShapeDtypeStruct((chips, count, share, width), jnp.bfloat16)
    return pl.pallas_call(
        left_kernel,
        grid=(sectors,),
        in_specs=[
            smem,
            smem,
            pl.BlockSpec((slots, terms, extent, width), lambda i: (0, 0, 0, 0)),
            pl.BlockSpec((terms, 1, extent, extent), lambda i: (0, i, 0, 0)),
        ],
        out_specs=[out_spec, out_spec],
        out_shape=[shape, shape],
        compiler_params=pltpu.CompilerParams(vmem_limit_bytes=VMEM_LIMIT),
        name="left_products",
    )(core, source, arrived, left_env)


def local(wavefunction, right_home, term_links, sector_rows, sector_cols, left_env, right_env):
    count, extent, width = wavefunction.shape
    per_sector = count // sector_rows.shape[0]
    slots = lax.axis_size("remap")
    chips = lax.axis_size("y")
    core_index = lax.axis_index("core")
    core = core_index.reshape(1)

    buffer = spread(core, right_home, term_links, sector_rows, wavefunction, slots)
    own = lax.all_to_all(buffer, "remap", 0, 0, tiled=True)
    other = lax.ppermute(own, "core", [(0, 1), (1, 0)])
    labels = own[:, extent // 2, : 1 + term_links.shape[0]].astype(jnp.int32)
    match = labels.T[:, None, :] == jnp.arange(count, dtype=jnp.int32)[None, :, None]
    source = jnp.sum(jnp.where(match, jnp.arange(slots, dtype=jnp.int32), 0), axis=2)

    pieces = []
    for chunk in range(width // CHUNK):
        products = right_products(
            core, source[0], term_links, sector_cols, own, other, right_env, chunk
        )
        arrived = lax.all_to_all(products, "remap", 0, 0, tiled=True)
        keep, send = left_products(core, source[1:], arrived, left_env, chips)
        received = lax.ppermute(send, "core", [(0, 1), (1, 0)])
        pair = (keep.astype(jnp.float32) + received.astype(jnp.float32)).astype(jnp.bfloat16)
        if chunk + 1 < width // CHUNK:
            summed = lax.psum_scatter(pair, "y", scatter_dimension=0, tiled=False)
        else:
            gathered = lax.all_to_all(pair, "y", 0, 0, tiled=True)
            summed = jnp.sum(gathered.astype(jnp.float32), axis=0)
        pieces.append(summed.astype(jnp.float32))
    total = jnp.concatenate(pieces, axis=2)
    share = total.shape[1]
    first = (lax.axis_index("y") * 2 + core_index) * share
    row = first + jnp.arange(share, dtype=jnp.int32)
    keep_rows = row[None, :] < jnp.repeat(sector_rows, per_sector)[:, None]
    return jnp.where(keep_rows[:, :, None], total, 0.0).astype(jnp.bfloat16)


def solution(mesh):
    slots, depth = mesh.devices.shape
    split = Mesh(mesh.devices.reshape(slots, depth // 2, 2), ("remap", "y", "core"))
    deep = ("y", "core")
    return jax.shard_map(
        local,
        mesh=split,
        in_specs=(
            P("remap", None, None),
            P("remap"),
            P(deep, "remap"),
            P("remap"),
            P("remap"),
            P(deep, "remap", None, None),
            P(deep, "remap", None, None),
        ),
        out_specs=P("remap", deep, None),
        check_vma=False,
    )
```

```python
import functools

import jax
import jax.numpy as jnp
from jax import lax
from jax.experimental import pallas as pl
from jax.experimental.pallas import tpu as pltpu
from jax.sharding import Mesh, PartitionSpec as P

SHARE = 16
LANES = 128
VMEM_LIMIT = 48 * 1024 * 1024
REMAP = ("zh", "zl", "x")
GROUP = ("zl", "x")
SMEM = pl.BlockSpec(memory_space=pltpu.SMEM)


def spread_kernel(count, depth_ref, home_ref, links_ref, rows_ref, wave_ref, out_ref, label_ref):
    slots = out_ref.shape[0]
    terms = links_ref.shape[0]
    per_sector = count // rows_ref.shape[0]

    def clear(peer, carry):
        for kind in range(1 + terms):
            label_ref[kind, peer] = count
        return carry

    lax.fori_loop(0, slots, clear, 0)

    def fill(block, carry):
        home = home_ref[block]
        label_ref[0, lax.div(home, count)] = lax.rem(home, count)
        for term in range(terms):
            link = links_ref[term, block]
            label_ref[1 + term, lax.div(link, count)] = lax.rem(link, count)
        return carry

    lax.fori_loop(0, count, fill, 0)
    lane = lax.broadcasted_iota(jnp.int32, (SHARE, LANES), 1)

    def mark(peer, carry):
        tile = jnp.full(lane.shape, label_ref[0, peer], jnp.int32)
        for term in range(terms):
            tile = jnp.where(lane == 1 + term, label_ref[1 + term, peer], tile)
        out_ref[peer, 2 * SHARE :, :] = tile.astype(jnp.float32).astype(jnp.bfloat16)
        return carry

    lax.fori_loop(0, slots, mark, 0)
    row = lax.broadcasted_iota(jnp.int32, wave_ref.shape[1:], 0) + depth_ref[0] * SHARE

    def put(block, carry):
        owner = lax.div(home_ref[block], count)
        keep = row < rows_ref[lax.div(block, per_sector)]
        value = wave_ref[block]
        value = jnp.where(keep, value, jnp.zeros_like(value))
        out_ref[owner, 0:SHARE, :] = value[:, :LANES]
        out_ref[owner, SHARE : 2 * SHARE, :] = value[:, LANES:]
        return carry

    lax.fori_loop(0, count, put, 0)


def spread(depth, right_home, term_links, sector_rows, wavefunction, slots):
    count, _, width = wavefunction.shape
    return pl.pallas_call(
        functools.partial(spread_kernel, count),
        grid_spec=pltpu.PrefetchScalarGridSpec(
            num_scalar_prefetch=1,
            grid=(1,),
            in_specs=[
                SMEM,
                SMEM,
                SMEM,
                pl.BlockSpec((count, SHARE, width), lambda i, depth: (0, depth[0], 0)),
            ],
            out_specs=pl.BlockSpec((slots, 3 * SHARE, LANES), lambda i, depth: (0, 0, 0)),
            scratch_shapes=[pltpu.SMEM((1 + term_links.shape[0], slots), jnp.int32)],
        ),
        out_shape=jax.ShapeDtypeStruct((slots, 3 * SHARE, LANES), jnp.bfloat16),
        name="spread_blocks",
    )(depth, right_home, term_links, sector_rows, wavefunction)


def order_kernel(from_ref, links_ref, cols_ref, in_ref, out_ref):
    terms, count = links_ref.shape
    per_sector = count // cols_ref.shape[0]
    lane = lax.broadcasted_iota(jnp.int32, (SHARE, LANES), 1)
    targets = jnp.zeros(lane.shape, jnp.int32)
    for block in range(count):
        slot = from_ref[block]
        cols = cols_ref[block // per_sector]
        for part in range(2):
            value = in_ref[slot, part * SHARE : (part + 1) * SHARE, :]
            out_ref[block, part * SHARE : (part + 1) * SHARE, :] = jnp.where(
                lane + part * LANES < cols, value, jnp.zeros_like(value)
            )
        for term in range(terms):
            owner = lax.div(links_ref[term, block], count)
            targets = jnp.where(lane == term * count + block, owner, targets)
    targets = targets.astype(jnp.float32).astype(jnp.bfloat16)
    out_ref[count, 0:SHARE, :] = targets
    out_ref[count, SHARE:, :] = targets


def order(source, term_links, sector_cols, arrived):
    count = source.shape[0]
    return pl.pallas_call(
        order_kernel,
        in_specs=[SMEM, SMEM, SMEM, pl.BlockSpec(memory_space=pltpu.VMEM)],
        out_specs=pl.BlockSpec(memory_space=pltpu.VMEM),
        out_shape=jax.ShapeDtypeStruct((count + 1, 2 * SHARE, LANES), jnp.bfloat16),
        name="order_blocks",
    )(source, term_links, sector_cols, arrived)


def right_kernel(steps, place_ref, targets_ref, *refs):
    slices, (env_ref, out_ref, moved_ref) = refs[: 2 * len(steps)], refs[2 * len(steps) :]
    group, layers, terms, extent, width = out_ref.shape
    sectors = env_ref.shape[2]
    count = slices[0].shape[1] - 1
    per_sector = count // sectors
    chips = len(steps)
    layer, chip, core = place_ref[0], place_ref[1], place_ref[2]
    turn = pl.program_id(0)
    from_layer = lax.rem(layer + turn, layers)
    for sector in range(sectors):
        for index, step in enumerate(steps):
            from_chip = lax.rem(chip + step + chips, chips)
            for other in range(2):
                from_core = core if other == 0 else 1 - core
                row = (from_chip * 2 + from_core) * SHARE
                source = slices[2 * index + other]
                for place in range(per_sector):
                    at = pl.ds(pl.multiple_of(place * extent + row, SHARE), SHARE)
                    block = sector * per_sector + place
                    moved_ref[sector % 2, at, 0:LANES] = source[0, block, 0:SHARE, :]
                    moved_ref[sector % 2, at, LANES:] = source[0, block, SHARE:, :]
        env = jnp.concatenate([env_ref[0, term, sector] for term in range(terms)], axis=1)
        product = jnp.dot(moved_ref[sector % 2], env, preferred_element_type=jnp.float32)
        product = product.astype(jnp.bfloat16)
        for place in range(per_sector):
            for term in range(terms):
                owner = targets_ref[turn, term * count + sector * per_sector + place]

                @pl.when(lax.div(owner, group) == layer)
                def _(place=place, term=term, owner=owner):
                    out_ref[lax.rem(owner, group), from_layer, term] = product[
                        place * extent : (place + 1) * extent, term * width : (term + 1) * width
                    ]


def right_products(place, targets, steps, slices, env, group):
    layers, terms, sectors, extent, width = env.shape
    _, blocks, tall, lanes = slices[0].shape
    per_sector = (blocks - 1) // sectors
    slice_spec = pl.BlockSpec((1, blocks, tall, lanes), lambda i, place, targets: (i, 0, 0, 0))
    return pl.pallas_call(
        functools.partial(right_kernel, steps),
        grid_spec=pltpu.PrefetchScalarGridSpec(
            num_scalar_prefetch=2,
            grid=(layers,),
            in_specs=[slice_spec] * len(slices)
            + [
                pl.BlockSpec(
                    (1, terms, sectors, extent, width),
                    lambda i, place, targets: (lax.rem(place[0] + i, layers), 0, 0, 0, 0),
                ),
            ],
            out_specs=pl.BlockSpec(
                (group, layers, terms, extent, width), lambda i, place, targets: (0, 0, 0, 0, 0)
            ),
            scratch_shapes=[pltpu.VMEM((2, per_sector * extent, extent), jnp.bfloat16)],
        ),
        out_shape=jax.ShapeDtypeStruct((group, layers, terms, extent, width), jnp.bfloat16),
        compiler_params=pltpu.CompilerParams(vmem_limit_bytes=VMEM_LIMIT),
        name="right_products",
    )(place, targets, *slices, env)


def left_partials(from_ref, placed_ref, env_ref):
    terms, count = from_ref.shape
    group = placed_ref.shape[0]
    per_sector = count // pl.num_programs(0)
    sector = pl.program_id(0)
    left = jnp.concatenate([env_ref[term, 0] for term in range(terms)], axis=1)
    for place in range(per_sector):
        parts = []
        for term in range(terms):
            device = from_ref[term, sector * per_sector + place]
            parts.append(placed_ref[lax.rem(device, group), lax.div(device, group), term])
        placed = jnp.concatenate(parts, axis=0)
        partial = jnp.dot(left, placed, preferred_element_type=jnp.float32)
        yield place, partial.astype(jnp.bfloat16)


def left_kernel(from_ref, placed_ref, env_ref, out_ref):
    for place, partial in left_partials(from_ref, placed_ref, env_ref):
        out_ref[:, place] = partial.reshape(out_ref.shape[0], SHARE, partial.shape[1])


def left_split_kernel(core_ref, from_ref, placed_ref, env_ref, keep_ref, send_ref):
    chips = keep_ref.shape[0]
    core = core_ref[0]
    for place, partial in left_partials(from_ref, placed_ref, env_ref):
        halves = [
            jnp.stack(
                [partial[(2 * c + k) * SHARE : (2 * c + k + 1) * SHARE] for c in range(chips)]
            )
            for k in range(2)
        ]
        keep_ref[:, place] = jnp.where(core == 0, halves[0], halves[1])
        send_ref[:, place] = jnp.where(core == 0, halves[1], halves[0])


def left_products(core, source, arrived, left_env, split):
    _, sectors, extent, _ = left_env.shape
    terms, count = source.shape
    width = arrived.shape[-1]
    pieces = extent // SHARE // (2 if split else 1)
    out_spec = pl.BlockSpec((pieces, count // sectors, SHARE, width), lambda i: (0, i, 0, 0))
    shape = jax.ShapeDtypeStruct((pieces, count, SHARE, width), jnp.bfloat16)
    specs = [
        SMEM,
        pl.BlockSpec(arrived.shape, lambda i: (0,) * arrived.ndim),
        pl.BlockSpec((terms, 1, extent, extent), lambda i: (0, i, 0, 0)),
    ]
    operands = [source, arrived, left_env]
    return pl.pallas_call(
        left_split_kernel if split else left_kernel,
        grid=(sectors,),
        in_specs=[SMEM] + specs if split else specs,
        out_specs=[out_spec, out_spec] if split else out_spec,
        out_shape=[shape, shape] if split else shape,
        compiler_params=pltpu.CompilerParams(vmem_limit_bytes=VMEM_LIMIT),
        name="left_products",
    )(*([core] + operands if split else operands))


def shift(array, axis, step):
    size = lax.axis_size(axis)
    return lax.ppermute(array, axis, [(i, (i + step) % size) for i in range(size)])


def gather_ring(own, axis):
    size = lax.axis_size(axis)
    found = [(0, own)]
    up = down = own
    for step in range(1, size // 2):
        up, down = shift(up, axis, 1), shift(down, axis, -1)
        found += [(-step, up), (step, down)]
    middle = own.shape[0] // 2
    last = jnp.concatenate([shift(up[:middle], axis, 1), shift(down[middle:], axis, -1)])
    return found + [(size // 2, last)]


def local(wavefunction, right_home, term_links, sector_rows, sector_cols, left_env, right_env):
    count, _, width = wavefunction.shape
    per_sector = count // sector_rows.shape[0]
    slots = lax.axis_size(REMAP)
    layers = lax.axis_size("zh")
    terms = term_links.shape[0]
    core_index = lax.axis_index("core")
    depth_index = lax.axis_index("y") * 2 + core_index
    core = core_index.reshape(1)
    place = jnp.stack([lax.axis_index("zh"), lax.axis_index("y"), core_index])
    chunks = [slice(at, at + LANES) for at in range(0, width, LANES)]

    envs = [lax.all_gather(right_env[..., chunk], "zh") for chunk in chunks]
    buffer = spread(depth_index.reshape(1), right_home, term_links, sector_rows, wavefunction, slots)
    arrived = lax.all_to_all(buffer, REMAP, 0, 0, tiled=True)
    labels = arrived[:, 2 * SHARE, : 1 + terms].astype(jnp.int32)
    match = labels.T[:, None, :] == jnp.arange(count, dtype=jnp.int32)[None, :, None]
    source = jnp.sum(jnp.where(match, jnp.arange(slots, dtype=jnp.int32), 0), axis=2)

    ordered = order(source[0], term_links, sector_cols, arrived)
    mine = jnp.stack([ordered] + [shift(ordered, "zh", -step) for step in range(1, layers)])
    targets = mine[:, count, 0, : terms * count].astype(jnp.int32)
    steps, slices = [], []
    for step, shard in gather_ring(mine, "y"):
        steps.append(step)
        slices += [shard, shift(shard, "core", 1)]

    pieces = []
    for env in envs:
        products = right_products(place, targets, steps, slices, env, slots // layers)
        arrived = lax.all_to_all(products, GROUP, 0, 0, tiled=True)
        if len(pieces) + 1 < len(envs):
            partial = left_products(core, source[1:], arrived, left_env, False)
            summed = lax.psum_scatter(partial, ("y", "core"), scatter_dimension=0, tiled=False)
            pieces.append(summed.astype(jnp.float32))
        else:
            keep, send = left_products(core, source[1:], arrived, left_env, True)
            pair = keep.astype(jnp.float32) + shift(send, "core", 1).astype(jnp.float32)
            gathered = lax.all_to_all(pair.astype(jnp.bfloat16), "y", 0, 0, tiled=True)
            pieces.append(jnp.sum(gathered.astype(jnp.float32), axis=0))
    total = jnp.concatenate(pieces, axis=2)
    row = depth_index * SHARE + jnp.arange(SHARE, dtype=jnp.int32)
    keep_rows = row[None, :] < jnp.repeat(sector_rows, per_sector)[:, None]
    return jnp.where(keep_rows[:, :, None], total, 0.0).astype(jnp.bfloat16)


def solution(mesh):
    slots, depth = mesh.devices.shape
    split = Mesh(
        mesh.devices.reshape(4, 2, slots // 8, depth // 2, 2), ("zh", "zl", "x", "y", "core")
    )
    deep = ("y", "core")
    return jax.shard_map(
        local,
        mesh=split,
        in_specs=(
            P(REMAP, None, None),
            P(REMAP),
            P(deep, REMAP),
            P(REMAP),
            P(REMAP),
            P(deep, REMAP, None, None),
            P(deep, REMAP, None, None),
        ),
        out_specs=P(REMAP, deep, None),
        check_vma=False,
    )
```

```python
import functools

import jax
import jax.numpy as jnp
from jax import lax
from jax.experimental import pallas as pl
from jax.experimental.pallas import tpu as pltpu
from jax.sharding import Mesh, PartitionSpec as P

SHARE = 16
LANES = 128
VMEM_LIMIT = 48 * 1024 * 1024
REMAP = ("zh", "zl", "x")
GROUP = ("zl", "x")
DEPTH = ("y", "core")
SMEM = pl.BlockSpec(memory_space=pltpu.SMEM)


def spread_kernel(count, depth_ref, home_ref, links_ref, rows_ref, wave_ref, out_ref, label_ref):
    slots = out_ref.shape[0]
    terms = links_ref.shape[0]
    per_sector = count // rows_ref.shape[0]

    def clear(peer, carry):
        for kind in range(1 + terms):
            label_ref[kind, peer] = count
        return carry

    lax.fori_loop(0, slots, clear, 0)

    def fill(block, carry):
        home = home_ref[block]
        label_ref[0, lax.div(home, count)] = lax.rem(home, count)
        for term in range(terms):
            link = links_ref[term, block]
            label_ref[1 + term, lax.div(link, count)] = lax.rem(link, count)
        return carry

    lax.fori_loop(0, count, fill, 0)
    lane = lax.broadcasted_iota(jnp.int32, (SHARE, LANES), 1)

    def mark(peer, carry):
        tile = jnp.full(lane.shape, label_ref[0, peer], jnp.int32)
        for term in range(terms):
            tile = jnp.where(lane == 1 + term, label_ref[1 + term, peer], tile)
        out_ref[peer, 2 * SHARE :, :] = tile.astype(jnp.float32).astype(jnp.bfloat16)
        return carry

    lax.fori_loop(0, slots, mark, 0)
    row = lax.broadcasted_iota(jnp.int32, wave_ref.shape[1:], 0) + depth_ref[0] * SHARE

    def put(block, carry):
        owner = lax.div(home_ref[block], count)
        keep = row < rows_ref[lax.div(block, per_sector)]
        value = wave_ref[block]
        value = jnp.where(keep, value, jnp.zeros_like(value))
        out_ref[owner, 0:SHARE, :] = value[:, :LANES]
        out_ref[owner, SHARE : 2 * SHARE, :] = value[:, LANES:]
        return carry

    lax.fori_loop(0, count, put, 0)


def spread(depth, right_home, term_links, sector_rows, wavefunction, slots):
    count, _, width = wavefunction.shape
    return pl.pallas_call(
        functools.partial(spread_kernel, count),
        grid_spec=pltpu.PrefetchScalarGridSpec(
            num_scalar_prefetch=1,
            grid=(1,),
            in_specs=[
                SMEM,
                SMEM,
                SMEM,
                pl.BlockSpec((count, SHARE, width), lambda i, depth: (0, depth[0], 0)),
            ],
            out_specs=pl.BlockSpec((slots, 3 * SHARE, LANES), lambda i, depth: (0, 0, 0)),
            scratch_shapes=[pltpu.SMEM((1 + term_links.shape[0], slots), jnp.int32)],
        ),
        out_shape=jax.ShapeDtypeStruct((slots, 3 * SHARE, LANES), jnp.bfloat16),
        name="spread_blocks",
    )(depth, right_home, term_links, sector_rows, wavefunction)


def order_kernel(from_ref, links_ref, cols_ref, in_ref, out_ref):
    terms, count = links_ref.shape
    per_sector = count // cols_ref.shape[0]
    lane = lax.broadcasted_iota(jnp.int32, (SHARE, LANES), 1)
    targets = jnp.zeros(lane.shape, jnp.int32)
    for block in range(count):
        slot = from_ref[block]
        cols = cols_ref[block // per_sector]
        for part in range(2):
            value = in_ref[slot, part * SHARE : (part + 1) * SHARE, :]
            out_ref[block, part * SHARE : (part + 1) * SHARE, :] = jnp.where(
                lane + part * LANES < cols, value, jnp.zeros_like(value)
            )
        for term in range(terms):
            owner = lax.div(links_ref[term, block], count)
            targets = jnp.where(lane == term * count + block, owner, targets)
    targets = targets.astype(jnp.float32).astype(jnp.bfloat16)
    out_ref[count, 0:SHARE, :] = targets
    out_ref[count, SHARE:, :] = targets


def order(source, term_links, sector_cols, arrived):
    count = source.shape[0]
    return pl.pallas_call(
        order_kernel,
        in_specs=[SMEM, SMEM, SMEM, pl.BlockSpec(memory_space=pltpu.VMEM)],
        out_specs=pl.BlockSpec(memory_space=pltpu.VMEM),
        out_shape=jax.ShapeDtypeStruct((count + 1, 2 * SHARE, LANES), jnp.bfloat16),
        name="order_blocks",
    )(source, term_links, sector_cols, arrived)


def right_kernel(place_ref, targets_ref, slices_ref, *refs):
    envs, (out_ref, moved_ref, env_ref) = refs[:-3], refs[-3:]
    group, _, terms, extent, width = out_ref.shape
    sectors = env_ref.shape[0]
    depth, count = slices_ref.shape[0], slices_ref.shape[2] - 1
    per_sector = count // sectors
    turn = pl.program_id(0)
    for index in range(len(envs) // terms):

        @pl.when(turn == index)
        def _(index=index):
            for term in range(terms):
                env = envs[index * terms + term][0]
                env_ref[:, :, term * width : (term + 1) * width] = env

    for sector in range(sectors):
        half = sector % 2
        for share in range(depth):
            for place in range(per_sector):
                at = slice(place * extent + share * SHARE, place * extent + (share + 1) * SHARE)
                block = sector * per_sector + place
                moved_ref[half, at, 0:LANES] = slices_ref[share, 0, block, 0:SHARE, :]
                moved_ref[half, at, LANES:] = slices_ref[share, 0, block, SHARE:, :]
        product = jnp.dot(moved_ref[half], env_ref[sector], preferred_element_type=jnp.float32)
        product = product.astype(jnp.bfloat16)
        for place in range(per_sector):
            for term in range(terms):
                owner = targets_ref[turn, term * count + sector * per_sector + place]

                @pl.when(lax.div(owner, group) == place_ref[0])
                def _(place=place, term=term, owner=owner):
                    out_ref[lax.rem(owner, group), 0, term] = product[
                        place * extent : (place + 1) * extent, term * width : (term + 1) * width
                    ]


def right_products(place, targets, slices, envs, group, chunk, width):
    depth, layers, blocks, tall, lanes = slices.shape
    terms = len(envs[0])
    sectors, extent = envs[0][0][0].shape[1:3]
    per_sector = (blocks - 1) // sectors
    flat = [pair for layer in envs for pair in layer]
    shape = (group, layers, terms, extent, width)
    return pl.pallas_call(
        right_kernel,
        grid_spec=pltpu.PrefetchScalarGridSpec(
            num_scalar_prefetch=2,
            grid=(layers,),
            in_specs=[pl.BlockSpec((depth, 1, blocks, tall, lanes), lambda i, p, t: (0, i, 0, 0, 0))]
            + [
                pl.BlockSpec(
                    (1, sectors, extent, width), lambda i, p, t, term=term: (term, 0, 0, chunk)
                )
                for _, term in flat
            ],
            out_specs=pl.BlockSpec((group, 1, terms, extent, width), lambda i, p, t: (0, i, 0, 0, 0)),
            scratch_shapes=[
                pltpu.VMEM((2, per_sector * extent, extent), jnp.bfloat16),
                pltpu.VMEM((sectors, extent, terms * width), jnp.bfloat16),
            ],
        ),
        out_shape=jax.ShapeDtypeStruct(shape, jnp.bfloat16),
        compiler_params=pltpu.CompilerParams(vmem_limit_bytes=VMEM_LIMIT),
        name="right_products",
    )(place, targets, slices, *[array for array, _ in flat])


def left_partials(place_ref, from_ref, own_ref, far_ref, env_ref, placed_ref):
    terms, count = from_ref.shape
    group, _, _, extent, _ = own_ref.shape
    layers = far_ref.shape[1] + 1
    per_sector = count // pl.num_programs(0)
    sector = pl.program_id(0)
    left = jnp.concatenate([env_ref[term, 0] for term in range(terms)], axis=1)
    for place in range(per_sector):
        for term in range(terms):
            device = from_ref[term, sector * per_sector + place]
            peer = lax.rem(device, group)
            step = lax.rem(lax.div(device, group) + layers - place_ref[0], layers)
            at = slice(term * extent, (term + 1) * extent)

            @pl.when(step == 0)
            def _(place=place, term=term, peer=peer, at=at):
                placed_ref[place, at, :] = own_ref[peer, 0, term]

            @pl.when(step > 0)
            def _(place=place, term=term, peer=peer, at=at, step=step):
                placed_ref[place, at, :] = far_ref[peer, jnp.maximum(step - 1, 0), term]

        partial = jnp.dot(left, placed_ref[place], preferred_element_type=jnp.float32)
        yield place, partial.astype(jnp.bfloat16)


def left_kernel(place_ref, from_ref, own_ref, far_ref, env_ref, out_ref, placed_ref):
    for place, partial in left_partials(place_ref, from_ref, own_ref, far_ref, env_ref, placed_ref):
        out_ref[:, place] = partial.reshape(out_ref.shape[0], SHARE, partial.shape[1])


def left_split_kernel(place_ref, from_ref, own_ref, far_ref, env_ref, keep_ref, send_ref, placed_ref):
    chips = keep_ref.shape[0]
    core = place_ref[2]
    for place, partial in left_partials(place_ref, from_ref, own_ref, far_ref, env_ref, placed_ref):
        halves = [
            jnp.stack(
                [partial[(2 * c + k) * SHARE : (2 * c + k + 1) * SHARE] for c in range(chips)]
            )
            for k in range(2)
        ]
        keep_ref[:, place] = jnp.where(core == 0, halves[0], halves[1])
        send_ref[:, place] = jnp.where(core == 0, halves[1], halves[0])


def left_products(place, source, own, far, left_env, chunk, split):
    _, sectors, extent, _ = left_env.shape
    terms, count = source.shape
    width = far.shape[-1]
    per_sector = count // sectors
    pieces = extent // SHARE // (2 if split else 1)
    out_spec = pl.BlockSpec((pieces, per_sector, SHARE, width), lambda i: (0, i, 0, 0))
    shape = jax.ShapeDtypeStruct((pieces, count, SHARE, width), jnp.bfloat16)
    return pl.pallas_call(
        left_split_kernel if split else left_kernel,
        grid=(sectors,),
        in_specs=[
            SMEM,
            SMEM,
            pl.BlockSpec(own.shape[:-1] + (width,), lambda i: (0, 0, 0, 0, chunk)),
            pl.BlockSpec(far.shape, lambda i: (0, 0, 0, 0, 0)),
            pl.BlockSpec((terms, 1, extent, extent), lambda i: (0, i, 0, 0)),
        ],
        out_specs=[out_spec, out_spec] if split else out_spec,
        out_shape=[shape, shape] if split else shape,
        scratch_shapes=[pltpu.VMEM((per_sector, terms * extent, width), jnp.bfloat16)],
        compiler_params=pltpu.CompilerParams(vmem_limit_bytes=VMEM_LIMIT),
        name="left_products",
    )(place, source, own, far, left_env)


def shift(array, axis, step):
    size = lax.axis_size(axis)
    return lax.ppermute(array, axis, [(i, (i + step) % size) for i in range(size)])


def local(wavefunction, right_home, term_links, sector_rows, sector_cols, left_env, right_env):
    count, _, width = wavefunction.shape
    per_sector = count // sector_rows.shape[0]
    slots = lax.axis_size(REMAP)
    layers = lax.axis_size("zh")
    group = slots // layers
    terms = term_links.shape[0]
    layer = lax.axis_index("zh")
    core_index = lax.axis_index("core")
    depth_index = lax.axis_index("y") * 2 + core_index
    place = jnp.stack([layer, lax.axis_index("y"), core_index])

    buffer = spread(depth_index.reshape(1), right_home, term_links, sector_rows, wavefunction, slots)
    arrived = lax.all_to_all(buffer, REMAP, 0, 0, tiled=True)
    labels = arrived[:, 2 * SHARE, : 1 + terms].astype(jnp.int32)
    match = labels.T[:, None, :] == jnp.arange(count, dtype=jnp.int32)[None, :, None]
    source = jnp.sum(jnp.where(match, jnp.arange(slots, dtype=jnp.int32), 0), axis=2)
    ordered = order(source[0], term_links, sector_cols, arrived)

    parts = [right_env[..., at : at + LANES] for at in range(0, width, LANES)]
    above = [shift(part, "zh", -1) for part in parts]
    below = [shift(part, "zh", 1) for part in parts]

    slices = lax.all_gather(ordered[None], DEPTH)
    targets = (term_links // count).reshape(1, terms * count)
    envs = [[(right_env, term) for term in range(terms)]]
    products = right_products(place, targets, slices, envs, group, 0, width)
    products, above[0], below[0] = lax.optimization_barrier((products, above[0], below[0]))
    own = lax.all_to_all(products, GROUP, 0, 0, tiled=True)

    around = lax.all_gather(ordered, "zh")
    others = lax.dynamic_slice_in_dim(jnp.concatenate([around, around]), layer + 1, layers - 1)
    targets = others[:, count, 0, : terms * count].astype(jnp.int32)
    slices = lax.all_gather(others, DEPTH)
    pieces = []
    for chunk in range(width // LANES):
        up, down = above[chunk], below[chunk]
        across = [shift(up[:1], "zh", -1), shift(down[1:], "zh", 1)]
        envs = [[(up, 0), (up, 1)], [(across[0], 0), (across[1], 0)], [(down, 0), (down, 1)]]
        products = right_products(place, targets, slices, envs, group, 0, LANES)
        slices, products = lax.optimization_barrier((slices, products))
        far = lax.all_to_all(products, GROUP, 0, 0, tiled=True)
        last = (chunk + 1) * LANES == width
        partial = left_products(place, source[1:], own, far, left_env, chunk, last)
        if last:
            keep, send = partial
            pair = keep.astype(jnp.float32) + shift(send, "core", 1).astype(jnp.float32)
            gathered = lax.all_to_all(pair.astype(jnp.bfloat16), "y", 0, 0, tiled=True)
            pieces.append(jnp.sum(gathered.astype(jnp.float32), axis=0))
        else:
            summed = lax.psum_scatter(partial, DEPTH, scatter_dimension=0, tiled=False)
            pieces.append(summed.astype(jnp.float32))
    total = jnp.concatenate(pieces, axis=2)
    row = depth_index * SHARE + jnp.arange(SHARE, dtype=jnp.int32)
    keep_rows = row[None, :] < jnp.repeat(sector_rows, per_sector)[:, None]
    return jnp.where(keep_rows[:, :, None], total, 0.0).astype(jnp.bfloat16)


def solution(mesh):
    slots, depth = mesh.devices.shape
    split = Mesh(
        mesh.devices.reshape(4, 2, slots // 8, depth // 2, 2), ("zh", "zl", "x", "y", "core")
    )
    return jax.shard_map(
        local,
        mesh=split,
        in_specs=(
            P(REMAP, None, None),
            P(REMAP),
            P(DEPTH, REMAP),
            P(REMAP),
            P(REMAP),
            P(DEPTH, REMAP, None, None),
            P(DEPTH, REMAP, None, None),
        ),
        out_specs=P(REMAP, DEPTH, None),
        check_vma=False,
    )
```

```python
import functools

import jax
import jax.numpy as jnp
from jax import lax
from jax.experimental import pallas as pl
from jax.experimental.pallas import tpu as pltpu
from jax.sharding import Mesh, PartitionSpec as P

SHARE = 16
LANES = 128
VMEM_LIMIT = 40 * 1024 * 1024
REMAP = ("zh", "zl", "x")
GROUP = ("zl", "x")
DEPTH = ("y", "core")
SMEM = pl.BlockSpec(memory_space=pltpu.SMEM)


def in_hbm(array):
    return pltpu.with_memory_space_constraint(array, pltpu.HBM)


def spread_kernel(count, depth_ref, home_ref, links_ref, rows_ref, wave_ref, out_ref, label_ref):
    slots = out_ref.shape[0]
    terms = links_ref.shape[0]
    per_sector = count // rows_ref.shape[0]

    def clear(peer, carry):
        for kind in range(1 + terms):
            label_ref[kind, peer] = count
        return carry

    lax.fori_loop(0, slots, clear, 0)

    def fill(block, carry):
        home = home_ref[block]
        label_ref[0, lax.div(home, count)] = lax.rem(home, count)
        for term in range(terms):
            link = links_ref[term, block]
            label_ref[1 + term, lax.div(link, count)] = lax.rem(link, count)
        return carry

    lax.fori_loop(0, count, fill, 0)
    lane = lax.broadcasted_iota(jnp.int32, (SHARE, LANES), 1)

    def mark(peer, carry):
        tile = jnp.full(lane.shape, label_ref[0, peer], jnp.int32)
        for term in range(terms):
            tile = jnp.where(lane == 1 + term, label_ref[1 + term, peer], tile)
        out_ref[peer, 2 * SHARE :, :] = tile.astype(jnp.float32).astype(jnp.bfloat16)
        return carry

    lax.fori_loop(0, slots, mark, 0)
    row = lax.broadcasted_iota(jnp.int32, wave_ref.shape[1:], 0) + depth_ref[0] * SHARE

    def put(block, carry):
        owner = lax.div(home_ref[block], count)
        keep = row < rows_ref[lax.div(block, per_sector)]
        value = wave_ref[block]
        value = jnp.where(keep, value, jnp.zeros_like(value))
        out_ref[owner, 0:SHARE, :] = value[:, :LANES]
        out_ref[owner, SHARE : 2 * SHARE, :] = value[:, LANES:]
        return carry

    lax.fori_loop(0, count, put, 0)


def spread(depth, right_home, term_links, sector_rows, wavefunction, slots):
    count, _, width = wavefunction.shape
    return pl.pallas_call(
        functools.partial(spread_kernel, count),
        grid_spec=pltpu.PrefetchScalarGridSpec(
            num_scalar_prefetch=1,
            grid=(1,),
            in_specs=[
                SMEM,
                SMEM,
                SMEM,
                pl.BlockSpec((count, SHARE, width), lambda i, depth: (0, depth[0], 0)),
            ],
            out_specs=pl.BlockSpec((slots, 3 * SHARE, LANES), lambda i, depth: (0, 0, 0)),
            scratch_shapes=[pltpu.SMEM((1 + term_links.shape[0], slots), jnp.int32)],
        ),
        out_shape=pltpu.HBM((slots, 3 * SHARE, LANES), jnp.bfloat16),
        name="spread_blocks",
    )(depth, right_home, term_links, sector_rows, in_hbm(wavefunction))


def order_kernel(from_ref, links_ref, cols_ref, in_ref, out_ref):
    terms, count = links_ref.shape
    per_sector = count // cols_ref.shape[0]
    lane = lax.broadcasted_iota(jnp.int32, (SHARE, LANES), 1)
    targets = jnp.zeros(lane.shape, jnp.int32)
    for block in range(count):
        slot = from_ref[block]
        cols = cols_ref[block // per_sector]
        for part in range(2):
            value = in_ref[slot, part * SHARE : (part + 1) * SHARE, :]
            out_ref[block, part * SHARE : (part + 1) * SHARE, :] = jnp.where(
                lane + part * LANES < cols, value, jnp.zeros_like(value)
            )
        for term in range(terms):
            owner = lax.div(links_ref[term, block], count)
            targets = jnp.where(lane == term * count + block, owner, targets)
    targets = targets.astype(jnp.float32).astype(jnp.bfloat16)
    out_ref[count, 0:SHARE, :] = targets
    out_ref[count, SHARE:, :] = targets


def order(source, term_links, sector_cols, arrived):
    count = source.shape[0]
    return pl.pallas_call(
        order_kernel,
        in_specs=[SMEM, SMEM, SMEM, pl.BlockSpec(memory_space=pltpu.VMEM)],
        out_specs=pl.BlockSpec(memory_space=pltpu.VMEM),
        out_shape=jax.ShapeDtypeStruct((count + 1, 2 * SHARE, LANES), jnp.bfloat16),
        name="order_blocks",
    )(source, term_links, sector_cols, arrived)


def right_kernel(place_ref, targets_ref, slices_ref, *refs):
    envs, (out_ref, moved_ref, env_ref) = refs[:-3], refs[-3:]
    group, _, terms, extent, width = out_ref.shape
    sectors = env_ref.shape[0]
    depth, count = slices_ref.shape[0], slices_ref.shape[2] - 1
    per_sector = count // sectors
    turn = pl.program_id(0)
    for index in range(len(envs) // terms):

        @pl.when(turn == index)
        def _(index=index):
            for term in range(terms):
                env = envs[index * terms + term][0]
                env_ref[:, :, term * width : (term + 1) * width] = env

    for sector in range(sectors):
        half = sector % 2
        for share in range(depth):
            for place in range(per_sector):
                at = slice(place * extent + share * SHARE, place * extent + (share + 1) * SHARE)
                block = sector * per_sector + place
                moved_ref[half, at, 0:LANES] = slices_ref[share, 0, block, 0:SHARE, :]
                moved_ref[half, at, LANES:] = slices_ref[share, 0, block, SHARE:, :]
        product = jnp.dot(moved_ref[half], env_ref[sector], preferred_element_type=jnp.float32)
        product = product.astype(jnp.bfloat16)
        for place in range(per_sector):
            for term in range(terms):
                owner = targets_ref[turn, term * count + sector * per_sector + place]

                @pl.when(lax.div(owner, group) == place_ref[0])
                def _(place=place, term=term, owner=owner):
                    out_ref[lax.rem(owner, group), 0, term] = product[
                        place * extent : (place + 1) * extent, term * width : (term + 1) * width
                    ]


def right_products(place, targets, slices, envs, group, chunk, width):
    depth, layers, blocks, tall, lanes = slices.shape
    terms = len(envs[0])
    sectors, extent = envs[0][0][0].shape[1:3]
    per_sector = (blocks - 1) // sectors
    flat = [pair for layer in envs for pair in layer]
    shape = (group, layers, terms, extent, width)
    return pl.pallas_call(
        right_kernel,
        grid_spec=pltpu.PrefetchScalarGridSpec(
            num_scalar_prefetch=2,
            grid=(layers,),
            in_specs=[pl.BlockSpec((depth, 1, blocks, tall, lanes), lambda i, p, t: (0, i, 0, 0, 0))]
            + [
                pl.BlockSpec(
                    (1, sectors, extent, width), lambda i, p, t, term=term: (term, 0, 0, chunk)
                )
                for _, term in flat
            ],
            out_specs=pl.BlockSpec((group, 1, terms, extent, width), lambda i, p, t: (0, i, 0, 0, 0)),
            scratch_shapes=[
                pltpu.VMEM((2, per_sector * extent, extent), jnp.bfloat16),
                pltpu.VMEM((sectors, extent, terms * width), jnp.bfloat16),
            ],
        ),
        out_shape=pltpu.HBM(shape, jnp.bfloat16),
        compiler_params=pltpu.CompilerParams(vmem_limit_bytes=VMEM_LIMIT),
        name="right_products",
    )(place, targets, in_hbm(slices), *[array for array, _ in flat])


def left_partials(place_ref, from_ref, own_ref, far_ref, env_ref, placed_ref):
    terms, count = from_ref.shape
    group, _, _, extent, _ = own_ref.shape
    layers = far_ref.shape[1] + 1
    per_sector = count // pl.num_programs(0)
    sector = pl.program_id(0)
    left = jnp.concatenate([env_ref[term, 0] for term in range(terms)], axis=1)
    for place in range(per_sector):
        for term in range(terms):
            device = from_ref[term, sector * per_sector + place]
            peer = lax.rem(device, group)
            step = lax.rem(lax.div(device, group) + layers - place_ref[0], layers)
            at = slice(term * extent, (term + 1) * extent)

            @pl.when(step == 0)
            def _(place=place, term=term, peer=peer, at=at):
                placed_ref[place, at, :] = own_ref[peer, 0, term]

            @pl.when(step > 0)
            def _(place=place, term=term, peer=peer, at=at, step=step):
                placed_ref[place, at, :] = far_ref[peer, jnp.maximum(step - 1, 0), term]

        partial = jnp.dot(left, placed_ref[place], preferred_element_type=jnp.float32)
        yield place, partial.astype(jnp.bfloat16)


def left_kernel(place_ref, from_ref, own_ref, far_ref, env_ref, out_ref, placed_ref):
    for place, partial in left_partials(place_ref, from_ref, own_ref, far_ref, env_ref, placed_ref):
        out_ref[:, place] = partial.reshape(out_ref.shape[0], SHARE, partial.shape[1])


def left_split_kernel(place_ref, from_ref, own_ref, far_ref, env_ref, keep_ref, send_ref, placed_ref):
    chips = keep_ref.shape[0]
    core = place_ref[2]
    for place, partial in left_partials(place_ref, from_ref, own_ref, far_ref, env_ref, placed_ref):
        halves = [
            jnp.stack(
                [partial[(2 * c + k) * SHARE : (2 * c + k + 1) * SHARE] for c in range(chips)]
            )
            for k in range(2)
        ]
        keep_ref[:, place] = jnp.where(core == 0, halves[0], halves[1])
        send_ref[:, place] = jnp.where(core == 0, halves[1], halves[0])


def left_products(place, source, own, far, left_env, chunk, split):
    _, sectors, extent, _ = left_env.shape
    terms, count = source.shape
    width = far.shape[-1]
    per_sector = count // sectors
    pieces = extent // SHARE // (2 if split else 1)
    out_spec = pl.BlockSpec((pieces, per_sector, SHARE, width), lambda i: (0, i, 0, 0))
    shape = jax.ShapeDtypeStruct((pieces, count, SHARE, width), jnp.bfloat16)
    return pl.pallas_call(
        left_split_kernel if split else left_kernel,
        grid=(sectors,),
        in_specs=[
            SMEM,
            SMEM,
            pl.BlockSpec(own.shape[:-1] + (width,), lambda i: (0, 0, 0, 0, chunk)),
            pl.BlockSpec(far.shape, lambda i: (0, 0, 0, 0, 0)),
            pl.BlockSpec((terms, 1, extent, extent), lambda i: (0, i, 0, 0)),
        ],
        out_specs=[out_spec, out_spec] if split else out_spec,
        out_shape=[shape, shape] if split else shape,
        scratch_shapes=[pltpu.VMEM((per_sector, terms * extent, width), jnp.bfloat16)],
        compiler_params=pltpu.CompilerParams(vmem_limit_bytes=VMEM_LIMIT),
        name="left_products",
    )(place, source, own, far, left_env)


def shift(array, axis, step):
    size = lax.axis_size(axis)
    return lax.ppermute(array, axis, [(i, (i + step) % size) for i in range(size)])


def local(wavefunction, right_home, term_links, sector_rows, sector_cols, left_env, right_env):
    count, _, width = wavefunction.shape
    per_sector = count // sector_rows.shape[0]
    slots = lax.axis_size(REMAP)
    layers = lax.axis_size("zh")
    group = slots // layers
    terms = term_links.shape[0]
    layer = lax.axis_index("zh")
    core_index = lax.axis_index("core")
    depth_index = lax.axis_index("y") * 2 + core_index
    place = jnp.stack([layer, lax.axis_index("y"), core_index])

    buffer = spread(depth_index.reshape(1), right_home, term_links, sector_rows, wavefunction, slots)
    arrived = lax.all_to_all(buffer, REMAP, 0, 0, tiled=True)
    labels = arrived[:, 2 * SHARE, : 1 + terms].astype(jnp.int32)
    match = labels.T[:, None, :] == jnp.arange(count, dtype=jnp.int32)[None, :, None]
    source = jnp.sum(jnp.where(match, jnp.arange(slots, dtype=jnp.int32), 0), axis=2)
    ordered = order(source[0], term_links, sector_cols, arrived)

    parts = [right_env[..., at : at + LANES] for at in range(0, width, LANES)]
    above = [shift(part, "zh", -1) for part in parts]
    below = [shift(part, "zh", 1) for part in parts]

    slices = lax.all_gather(ordered[None], DEPTH)
    targets = (term_links // count).reshape(1, terms * count)
    envs = [[(right_env, term) for term in range(terms)]]
    products = right_products(place, targets, slices, envs, group, 0, width)
    products, above[0], below[0] = lax.optimization_barrier((products, above[0], below[0]))
    own = lax.all_to_all(products, GROUP, 0, 0, tiled=True)

    around = lax.all_gather(ordered, "zh")
    others = lax.dynamic_slice_in_dim(jnp.concatenate([around, around]), layer + 1, layers - 1)
    targets = others[:, count, 0, : terms * count].astype(jnp.int32)
    slices = lax.all_gather(others, DEPTH)
    pieces = []
    for chunk in range(width // LANES):
        up, down = above[chunk], below[chunk]
        across = [shift(up[:1], "zh", -1), shift(down[1:], "zh", 1)]
        envs = [[(up, 0), (up, 1)], [(across[0], 0), (across[1], 0)], [(down, 0), (down, 1)]]
        products = right_products(place, targets, slices, envs, group, 0, LANES)
        if chunk + 1 < len(parts):
            after = slices, products, above[chunk + 1], below[chunk + 1]
            slices, products, above[chunk + 1], below[chunk + 1] = lax.optimization_barrier(after)
        far = lax.all_to_all(products, GROUP, 0, 0, tiled=True)
        last = (chunk + 1) * LANES == width
        partial = left_products(place, source[1:], own, far, left_env, chunk, last)
        if last:
            keep, send = partial
            pair = keep.astype(jnp.float32) + shift(send, "core", 1).astype(jnp.float32)
            gathered = lax.all_to_all(pair.astype(jnp.bfloat16), "y", 0, 0, tiled=True)
            pieces.append(jnp.sum(gathered.astype(jnp.float32), axis=0))
        else:
            summed = lax.psum_scatter(partial, DEPTH, scatter_dimension=0, tiled=False)
            pieces.append(summed.astype(jnp.float32))
    total = jnp.concatenate(pieces, axis=2)
    row = depth_index * SHARE + jnp.arange(SHARE, dtype=jnp.int32)
    keep_rows = row[None, :] < jnp.repeat(sector_rows, per_sector)[:, None]
    return jnp.where(keep_rows[:, :, None], total, 0.0).astype(jnp.bfloat16)


def solution(mesh):
    slots, depth = mesh.devices.shape
    split = Mesh(
        mesh.devices.reshape(4, 2, slots // 8, depth // 2, 2), ("zh", "zl", "x", "y", "core")
    )
    return jax.shard_map(
        local,
        mesh=split,
        in_specs=(
            P(REMAP, None, None),
            P(REMAP),
            P(DEPTH, REMAP),
            P(REMAP),
            P(REMAP),
            P(DEPTH, REMAP, None, None),
            P(DEPTH, REMAP, None, None),
        ),
        out_specs=P(REMAP, DEPTH, None),
        check_vma=False,
    )
```

```python
import functools

import jax
import jax.numpy as jnp
from jax import lax
from jax.experimental import pallas as pl
from jax.experimental.pallas import tpu as pltpu
from jax.sharding import Mesh, PartitionSpec as P

SHARE = 16
LANES = 128
NEAR = 2
VMEM_LIMIT = 40 * 1024 * 1024
REMAP = ("zh", "zl", "x")
GROUP = ("zl", "x")
DEPTH = ("y", "core")
SMEM = pl.BlockSpec(memory_space=pltpu.SMEM)


def in_hbm(array):
    return pltpu.with_memory_space_constraint(array, pltpu.HBM)


def spread_kernel(count, depth_ref, home_ref, links_ref, rows_ref, wave_ref, out_ref, label_ref):
    slots = out_ref.shape[0]
    terms = links_ref.shape[0]
    per_sector = count // rows_ref.shape[0]

    def clear(peer, carry):
        for kind in range(1 + terms):
            label_ref[kind, peer] = count
        return carry

    lax.fori_loop(0, slots, clear, 0)

    def fill(block, carry):
        home = home_ref[block]
        label_ref[0, lax.div(home, count)] = lax.rem(home, count)
        for term in range(terms):
            link = links_ref[term, block]
            label_ref[1 + term, lax.div(link, count)] = lax.rem(link, count)
        return carry

    lax.fori_loop(0, count, fill, 0)
    lane = lax.broadcasted_iota(jnp.int32, (SHARE, LANES), 1)

    def mark(peer, carry):
        tile = jnp.full(lane.shape, label_ref[0, peer], jnp.int32)
        for term in range(terms):
            tile = jnp.where(lane == 1 + term, label_ref[1 + term, peer], tile)
        out_ref[peer, 2 * SHARE :, :] = tile.astype(jnp.float32).astype(jnp.bfloat16)
        return carry

    lax.fori_loop(0, slots, mark, 0)
    row = lax.broadcasted_iota(jnp.int32, wave_ref.shape[1:], 0) + depth_ref[0] * SHARE

    def put(block, carry):
        owner = lax.div(home_ref[block], count)
        keep = row < rows_ref[lax.div(block, per_sector)]
        value = wave_ref[block]
        value = jnp.where(keep, value, jnp.zeros_like(value))
        out_ref[owner, 0:SHARE, :] = value[:, :LANES]
        out_ref[owner, SHARE : 2 * SHARE, :] = value[:, LANES:]
        return carry

    lax.fori_loop(0, count, put, 0)


def spread(depth, right_home, term_links, sector_rows, wavefunction, slots):
    count, _, width = wavefunction.shape
    return pl.pallas_call(
        functools.partial(spread_kernel, count),
        grid_spec=pltpu.PrefetchScalarGridSpec(
            num_scalar_prefetch=1,
            grid=(1,),
            in_specs=[
                SMEM,
                SMEM,
                SMEM,
                pl.BlockSpec((count, SHARE, width), lambda i, depth: (0, depth[0], 0)),
            ],
            out_specs=pl.BlockSpec((slots, 3 * SHARE, LANES), lambda i, depth: (0, 0, 0)),
            scratch_shapes=[pltpu.SMEM((1 + term_links.shape[0], slots), jnp.int32)],
        ),
        out_shape=pltpu.HBM((slots, 3 * SHARE, LANES), jnp.bfloat16),
        name="spread_blocks",
    )(depth, right_home, term_links, sector_rows, in_hbm(wavefunction))


def order_kernel(from_ref, links_ref, cols_ref, in_ref, out_ref):
    terms, count = links_ref.shape
    per_sector = count // cols_ref.shape[0]
    lane = lax.broadcasted_iota(jnp.int32, (SHARE, LANES), 1)
    targets = jnp.zeros(lane.shape, jnp.int32)
    for block in range(count):
        slot = from_ref[block]
        cols = cols_ref[block // per_sector]
        for part in range(2):
            value = in_ref[slot, part * SHARE : (part + 1) * SHARE, :]
            out_ref[block, part * SHARE : (part + 1) * SHARE, :] = jnp.where(
                lane + part * LANES < cols, value, jnp.zeros_like(value)
            )
        for term in range(terms):
            owner = lax.div(links_ref[term, block], count)
            targets = jnp.where(lane == term * count + block, owner, targets)
    targets = targets.astype(jnp.float32).astype(jnp.bfloat16)
    out_ref[count, 0:SHARE, :] = targets
    out_ref[count, SHARE:, :] = targets


def order(source, term_links, sector_cols, arrived):
    count = source.shape[0]
    return pl.pallas_call(
        order_kernel,
        in_specs=[SMEM, SMEM, SMEM, pl.BlockSpec(memory_space=pltpu.VMEM)],
        out_specs=pl.BlockSpec(memory_space=pltpu.VMEM),
        out_shape=jax.ShapeDtypeStruct((count + 1, 2 * SHARE, LANES), jnp.bfloat16),
        name="order_blocks",
    )(source, term_links, sector_cols, arrived)


def right_kernel(place_ref, targets_ref, slices_ref, *refs):
    envs, (out_ref, moved_ref, env_ref) = refs[:-3], refs[-3:]
    group, _, terms, extent, width = out_ref.shape
    sectors = env_ref.shape[0]
    depth, count = slices_ref.shape[0], slices_ref.shape[2] - 1
    per_sector = count // sectors
    turn = pl.program_id(0)
    for index in range(len(envs) // terms):

        @pl.when(turn == index)
        def _(index=index):
            for term in range(terms):
                env = envs[index * terms + term][0]
                env_ref[:, :, term * width : (term + 1) * width] = env

    for sector in range(sectors):
        half = sector % 2
        for share in range(depth):
            for place in range(per_sector):
                at = slice(place * extent + share * SHARE, place * extent + (share + 1) * SHARE)
                block = sector * per_sector + place
                moved_ref[half, at, 0:LANES] = slices_ref[share, 0, block, 0:SHARE, :]
                moved_ref[half, at, LANES:] = slices_ref[share, 0, block, SHARE:, :]
        product = jnp.dot(moved_ref[half], env_ref[sector], preferred_element_type=jnp.float32)
        product = product.astype(jnp.bfloat16)
        for place in range(per_sector):
            for term in range(terms):
                owner = targets_ref[turn, term * count + sector * per_sector + place]

                @pl.when(lax.div(owner, group) == place_ref[0])
                def _(place=place, term=term, owner=owner):
                    out_ref[lax.rem(owner, group), 0, term] = product[
                        place * extent : (place + 1) * extent, term * width : (term + 1) * width
                    ]


def right_products(place, targets, slices, envs, group, width):
    depth, layers, blocks, tall, lanes = slices.shape
    terms = len(envs[0])
    sectors, extent = envs[0][0][0].shape[1:3]
    per_sector = (blocks - 1) // sectors
    flat = [pair for layer in envs for pair in layer]
    shape = (group, layers, terms, extent, width)
    return pl.pallas_call(
        right_kernel,
        grid_spec=pltpu.PrefetchScalarGridSpec(
            num_scalar_prefetch=2,
            grid=(layers,),
            in_specs=[pl.BlockSpec((depth, 1, blocks, tall, lanes), lambda i, p, t: (0, i, 0, 0, 0))]
            + [
                pl.BlockSpec((1, sectors, extent, width), lambda i, p, t, at=at: (at(p), 0, 0, 0))
                for _, at in flat
            ],
            out_specs=pl.BlockSpec((group, 1, terms, extent, width), lambda i, p, t: (0, i, 0, 0, 0)),
            scratch_shapes=[
                pltpu.VMEM((2, per_sector * extent, extent), jnp.bfloat16),
                pltpu.VMEM((sectors, extent, terms * width), jnp.bfloat16),
            ],
        ),
        out_shape=pltpu.HBM(shape, jnp.bfloat16),
        compiler_params=pltpu.CompilerParams(vmem_limit_bytes=VMEM_LIMIT),
        name="right_products",
    )(place, targets, in_hbm(slices), *[array for array, _ in flat])


def left_partials(place_ref, from_ref, near_ref, far_ref, env_ref, placed_ref):
    terms, count = from_ref.shape
    group, near, _, extent, width = near_ref.shape
    layers = near + far_ref.shape[1]
    per_sector = count // pl.num_programs(0)
    sector = pl.program_id(0)
    left = jnp.concatenate([env_ref[term, 0] for term in range(terms)], axis=1)
    for place in range(per_sector):
        for term in range(terms):
            device = from_ref[term, sector * per_sector + place]
            peer = lax.rem(device, group)
            step = lax.rem(lax.div(device, group) + layers - place_ref[0], layers)
            rows = slice(term * extent, (term + 1) * extent)
            columns = slice(place * width, (place + 1) * width)

            @pl.when(step < near)
            def _(term=term, peer=peer, step=step, rows=rows, columns=columns):
                placed_ref[rows, columns] = near_ref[peer, jnp.minimum(step, near - 1), term]

            @pl.when(step >= near)
            def _(term=term, peer=peer, step=step, rows=rows, columns=columns):
                placed_ref[rows, columns] = far_ref[peer, jnp.maximum(step - near, 0), term]

    partial = jnp.dot(left, placed_ref[...], preferred_element_type=jnp.float32)
    partial = partial.astype(jnp.bfloat16)
    for place in range(per_sector):
        yield place, partial[:, place * width : (place + 1) * width]


def left_kernel(place_ref, from_ref, near_ref, far_ref, env_ref, out_ref, placed_ref):
    for place, partial in left_partials(place_ref, from_ref, near_ref, far_ref, env_ref, placed_ref):
        out_ref[:, place] = partial.reshape(out_ref.shape[0], SHARE, partial.shape[1])


def left_split_kernel(place_ref, from_ref, near_ref, far_ref, env_ref, keep_ref, send_ref, placed_ref):
    chips = keep_ref.shape[0]
    core = place_ref[2]
    for place, partial in left_partials(place_ref, from_ref, near_ref, far_ref, env_ref, placed_ref):
        halves = [
            jnp.stack(
                [partial[(2 * c + k) * SHARE : (2 * c + k + 1) * SHARE] for c in range(chips)]
            )
            for k in range(2)
        ]
        keep_ref[:, place] = jnp.where(core == 0, halves[0], halves[1])
        send_ref[:, place] = jnp.where(core == 0, halves[1], halves[0])


def left_products(place, source, near, far, left_env, split):
    _, sectors, extent, _ = left_env.shape
    terms, count = source.shape
    width = far.shape[-1]
    per_sector = count // sectors
    pieces = extent // SHARE // (2 if split else 1)
    out_spec = pl.BlockSpec((pieces, per_sector, SHARE, width), lambda i: (0, i, 0, 0))
    shape = jax.ShapeDtypeStruct((pieces, count, SHARE, width), jnp.bfloat16)
    return pl.pallas_call(
        left_split_kernel if split else left_kernel,
        grid=(sectors,),
        in_specs=[
            SMEM,
            SMEM,
            pl.BlockSpec(near.shape, lambda i: (0, 0, 0, 0, 0)),
            pl.BlockSpec(far.shape, lambda i: (0, 0, 0, 0, 0)),
            pl.BlockSpec((terms, 1, extent, extent), lambda i: (0, i, 0, 0)),
        ],
        out_specs=[out_spec, out_spec] if split else out_spec,
        out_shape=[shape, shape] if split else shape,
        scratch_shapes=[pltpu.VMEM((terms * extent, per_sector * width), jnp.bfloat16)],
        compiler_params=pltpu.CompilerParams(vmem_limit_bytes=VMEM_LIMIT),
        name="left_products",
    )(place, source, near, far, left_env)


def shift(array, axis, step):
    size = lax.axis_size(axis)
    return lax.ppermute(array, axis, [(i, (i + step) % size) for i in range(size)])


def local(wavefunction, right_home, term_links, sector_rows, sector_cols, left_env, right_env):
    count, _, width = wavefunction.shape
    per_sector = count // sector_rows.shape[0]
    slots = lax.axis_size(REMAP)
    layers = lax.axis_size("zh")
    group = slots // layers
    terms = term_links.shape[0]
    layer = lax.axis_index("zh")
    core_index = lax.axis_index("core")
    depth_index = lax.axis_index("y") * 2 + core_index
    place = jnp.stack([layer, lax.axis_index("y"), core_index])

    second = right_env[..., LANES:]
    gathered_env = lax.all_gather(right_env[..., :LANES], "zh")
    buffer = spread(depth_index.reshape(1), right_home, term_links, sector_rows, wavefunction, slots)
    arrived = lax.all_to_all(buffer, REMAP, 0, 0, tiled=True)
    labels = arrived[:, 2 * SHARE, : 1 + terms].astype(jnp.int32)
    match = labels.T[:, None, :] == jnp.arange(count, dtype=jnp.int32)[None, :, None]
    source = jnp.sum(jnp.where(match, jnp.arange(slots, dtype=jnp.int32), 0), axis=2)
    ordered = order(source[0], term_links, sector_cols, arrived)

    around = lax.all_gather(ordered, "zh")
    around = lax.dynamic_slice_in_dim(jnp.concatenate([around, around]), layer, layers)
    targets = around[:, count, 0, : terms * count].astype(jnp.int32)
    far = around[NEAR:]
    near, gathered_env = lax.optimization_barrier((around[:NEAR], gathered_env))
    near = lax.all_gather(near, DEPTH)
    far = lax.all_gather(far, DEPTH)

    above, below = shift(second, "zh", -1), shift(second, "zh", 1)
    across = [shift(above[:1], "zh", -1), shift(below[1:], "zh", 1)]
    held = gathered_env.reshape((layers * terms,) + gathered_env.shape[2:])
    first_envs = [
        [
            (held, lambda p, step=step, term=term: lax.rem(p[0] + step, layers) * terms + term)
            for term in range(terms)
        ]
        for step in range(layers)
    ]
    begun = right_products(place, targets[:NEAR], near, first_envs[:NEAR], group, LANES)
    begun, above, below, across = lax.optimization_barrier((begun, above, below, across))
    second_envs = [
        [(second, lambda p: 0), (second, lambda p: 1)],
        [(above, lambda p: 0), (above, lambda p: 1)],
        [(across[0], lambda p: 0), (across[1], lambda p: 0)],
        [(below, lambda p: 0), (below, lambda p: 1)],
    ]
    sent = {("near", 0): lax.all_to_all(begun, GROUP, 0, 0, tiled=True)}
    for key, chunk, slices, envs in (
        ("near", 1, near, second_envs[:NEAR]),
        ("far", 0, far, first_envs[NEAR:]),
        ("far", 1, far, second_envs[NEAR:]),
    ):
        steps = targets[:NEAR] if key == "near" else targets[NEAR:]
        products = right_products(place, steps, slices, envs, group, LANES)
        before = list(sent)[-1]
        products, sent[before] = lax.optimization_barrier((products, sent[before]))
        sent[key, chunk] = lax.all_to_all(products, GROUP, 0, 0, tiled=True)

    partial = left_products(place, source[1:], sent["near", 0], sent["far", 0], left_env, False)
    summed = lax.psum_scatter(partial, DEPTH, scatter_dimension=0, tiled=False)
    pieces = [summed.astype(jnp.float32)]
    keep, send = left_products(place, source[1:], sent["near", 1], sent["far", 1], left_env, True)
    pair = keep.astype(jnp.float32) + shift(send, "core", 1).astype(jnp.float32)
    shares = lax.all_to_all(pair.astype(jnp.bfloat16), "y", 0, 0, tiled=True)
    pieces.append(jnp.sum(shares.astype(jnp.float32), axis=0))
    total = jnp.concatenate(pieces, axis=2)
    row = depth_index * SHARE + jnp.arange(SHARE, dtype=jnp.int32)
    keep_rows = row[None, :] < jnp.repeat(sector_rows, per_sector)[:, None]
    return jnp.where(keep_rows[:, :, None], total, 0.0).astype(jnp.bfloat16)


def solution(mesh):
    slots, depth = mesh.devices.shape
    split = Mesh(
        mesh.devices.reshape(4, 2, slots // 8, depth // 2, 2), ("zh", "zl", "x", "y", "core")
    )
    return jax.shard_map(
        local,
        mesh=split,
        in_specs=(
            P(REMAP, None, None),
            P(REMAP),
            P(DEPTH, REMAP),
            P(REMAP),
            P(REMAP),
            P(DEPTH, REMAP, None, None),
            P(DEPTH, REMAP, None, None),
        ),
        out_specs=P(REMAP, DEPTH, None),
        check_vma=False,
    )
```

```python
import functools

import jax
import jax.numpy as jnp
from jax import lax
from jax.experimental import pallas as pl
from jax.experimental.pallas import tpu as pltpu
from jax.sharding import Mesh, PartitionSpec as P

SHARE = 16
LANES = 128
VMEM_LIMIT = 40 * 1024 * 1024
REMAP = ("zh", "zl", "x")
GROUP = ("zl", "x")
DEPTH = ("y", "core")
SMEM = pl.BlockSpec(memory_space=pltpu.SMEM)


def in_hbm(array):
    return pltpu.with_memory_space_constraint(array, pltpu.HBM)


def spread_kernel(count, depth_ref, home_ref, links_ref, rows_ref, wave_ref, out_ref, label_ref):
    slots = out_ref.shape[0]
    terms = links_ref.shape[0]
    per_sector = count // rows_ref.shape[0]

    def clear(peer, carry):
        for kind in range(1 + terms):
            label_ref[kind, peer] = count
        return carry

    lax.fori_loop(0, slots, clear, 0)

    def fill(block, carry):
        home = home_ref[block]
        label_ref[0, lax.div(home, count)] = lax.rem(home, count)
        for term in range(terms):
            link = links_ref[term, block]
            label_ref[1 + term, lax.div(link, count)] = lax.rem(link, count)
        return carry

    lax.fori_loop(0, count, fill, 0)
    lane = lax.broadcasted_iota(jnp.int32, (SHARE, LANES), 1)

    def mark(peer, carry):
        tile = jnp.full(lane.shape, label_ref[0, peer], jnp.int32)
        for term in range(terms):
            tile = jnp.where(lane == 1 + term, label_ref[1 + term, peer], tile)
        out_ref[peer, 2 * SHARE :, :] = tile.astype(jnp.float32).astype(jnp.bfloat16)
        return carry

    lax.fori_loop(0, slots, mark, 0)
    row = lax.broadcasted_iota(jnp.int32, wave_ref.shape[1:], 0) + depth_ref[0] * SHARE

    def put(block, carry):
        owner = lax.div(home_ref[block], count)
        keep = row < rows_ref[lax.div(block, per_sector)]
        value = wave_ref[block]
        value = jnp.where(keep, value, jnp.zeros_like(value))
        out_ref[owner, 0:SHARE, :] = value[:, :LANES]
        out_ref[owner, SHARE : 2 * SHARE, :] = value[:, LANES:]
        return carry

    lax.fori_loop(0, count, put, 0)


def spread(depth, right_home, term_links, sector_rows, wavefunction, slots):
    count, _, width = wavefunction.shape
    return pl.pallas_call(
        functools.partial(spread_kernel, count),
        grid_spec=pltpu.PrefetchScalarGridSpec(
            num_scalar_prefetch=1,
            grid=(1,),
            in_specs=[
                SMEM,
                SMEM,
                SMEM,
                pl.BlockSpec((count, SHARE, width), lambda i, depth: (0, depth[0], 0)),
            ],
            out_specs=pl.BlockSpec((slots, 3 * SHARE, LANES), lambda i, depth: (0, 0, 0)),
            scratch_shapes=[pltpu.SMEM((1 + term_links.shape[0], slots), jnp.int32)],
        ),
        out_shape=pltpu.HBM((slots, 3 * SHARE, LANES), jnp.bfloat16),
        name="spread_blocks",
    )(depth, right_home, term_links, sector_rows, in_hbm(wavefunction))


def order_kernel(from_ref, links_ref, cols_ref, in_ref, out_ref):
    terms, count = links_ref.shape
    per_sector = count // cols_ref.shape[0]
    lane = lax.broadcasted_iota(jnp.int32, (SHARE, LANES), 1)
    targets = jnp.zeros(lane.shape, jnp.int32)
    for block in range(count):
        slot = from_ref[block]
        cols = cols_ref[block // per_sector]
        for part in range(2):
            value = in_ref[slot, part * SHARE : (part + 1) * SHARE, :]
            out_ref[block, part * SHARE : (part + 1) * SHARE, :] = jnp.where(
                lane + part * LANES < cols, value, jnp.zeros_like(value)
            )
        for term in range(terms):
            owner = lax.div(links_ref[term, block], count)
            targets = jnp.where(lane == term * count + block, owner, targets)
    targets = targets.astype(jnp.float32).astype(jnp.bfloat16)
    out_ref[count, 0:SHARE, :] = targets
    out_ref[count, SHARE:, :] = targets


def order(source, term_links, sector_cols, arrived):
    count = source.shape[0]
    return pl.pallas_call(
        order_kernel,
        in_specs=[SMEM, SMEM, SMEM, pl.BlockSpec(memory_space=pltpu.VMEM)],
        out_specs=pl.BlockSpec(memory_space=pltpu.VMEM),
        out_shape=jax.ShapeDtypeStruct((count + 1, 2 * SHARE, LANES), jnp.bfloat16),
        name="order_blocks",
    )(source, term_links, sector_cols, arrived)


def right_kernel(place_ref, targets_ref, slices_ref, *refs):
    envs, (out_ref, moved_ref, env_ref) = refs[:-3], refs[-3:]
    group, _, terms, extent, width = out_ref.shape
    sectors = env_ref.shape[0]
    depth, count = slices_ref.shape[0], slices_ref.shape[2] - 1
    per_sector = count // sectors
    turn = pl.program_id(0)
    for index in range(len(envs) // terms):

        @pl.when(turn == index)
        def _(index=index):
            for term in range(terms):
                env = envs[index * terms + term][0]
                env_ref[:, :, term * width : (term + 1) * width] = env

    for sector in range(sectors):
        half = sector % 2
        for share in range(depth):
            for place in range(per_sector):
                at = slice(place * extent + share * SHARE, place * extent + (share + 1) * SHARE)
                block = sector * per_sector + place
                moved_ref[half, at, 0:LANES] = slices_ref[share, 0, block, 0:SHARE, :]
                moved_ref[half, at, LANES:] = slices_ref[share, 0, block, SHARE:, :]
        product = jnp.dot(moved_ref[half], env_ref[sector], preferred_element_type=jnp.float32)
        product = product.astype(jnp.bfloat16)
        for place in range(per_sector):
            for term in range(terms):
                owner = targets_ref[turn, term * count + sector * per_sector + place]

                @pl.when(lax.div(owner, group) == place_ref[0])
                def _(place=place, term=term, owner=owner):
                    out_ref[lax.rem(owner, group), 0, term] = product[
                        place * extent : (place + 1) * extent, term * width : (term + 1) * width
                    ]


def right_products(place, targets, slices, envs, group, chunk, width):
    depth, layers, blocks, tall, lanes = slices.shape
    terms = len(envs[0])
    sectors, extent = envs[0][0][0].shape[1:3]
    per_sector = (blocks - 1) // sectors
    flat = [pair for layer in envs for pair in layer]
    shape = (group, layers, terms, extent, width)
    return pl.pallas_call(
        right_kernel,
        grid_spec=pltpu.PrefetchScalarGridSpec(
            num_scalar_prefetch=2,
            grid=(layers,),
            in_specs=[pl.BlockSpec((depth, 1, blocks, tall, lanes), lambda i, p, t: (0, i, 0, 0, 0))]
            + [
                pl.BlockSpec(
                    (1, sectors, extent, width), lambda i, p, t, term=term: (term, 0, 0, chunk)
                )
                for _, term in flat
            ],
            out_specs=pl.BlockSpec((group, 1, terms, extent, width), lambda i, p, t: (0, i, 0, 0, 0)),
            scratch_shapes=[
                pltpu.VMEM((2, per_sector * extent, extent), jnp.bfloat16),
                pltpu.VMEM((sectors, extent, terms * width), jnp.bfloat16),
            ],
        ),
        out_shape=pltpu.HBM(shape, jnp.bfloat16),
        compiler_params=pltpu.CompilerParams(vmem_limit_bytes=VMEM_LIMIT),
        name="right_products",
    )(place, targets, in_hbm(slices), *[array for array, _ in flat])


def left_partials(place_ref, from_ref, near_ref, far_ref, env_ref, placed_ref):
    terms, count = from_ref.shape
    group, near, _, extent, width = near_ref.shape
    layers = near + far_ref.shape[1]
    per_sector = count // pl.num_programs(0)
    sector = pl.program_id(0)
    left = jnp.concatenate([env_ref[term, 0] for term in range(terms)], axis=1)
    for place in range(per_sector):
        for term in range(terms):
            device = from_ref[term, sector * per_sector + place]
            peer = lax.rem(device, group)
            step = lax.rem(lax.div(device, group) + layers - place_ref[0], layers)
            rows = slice(term * extent, (term + 1) * extent)
            columns = slice(place * width, (place + 1) * width)

            @pl.when(step < near)
            def _(term=term, peer=peer, step=step, rows=rows, columns=columns):
                placed_ref[rows, columns] = near_ref[peer, jnp.minimum(step, near - 1), term]

            @pl.when(step >= near)
            def _(term=term, peer=peer, step=step, rows=rows, columns=columns):
                placed_ref[rows, columns] = far_ref[peer, jnp.maximum(step - near, 0), term]

    partial = jnp.dot(left, placed_ref[...], preferred_element_type=jnp.float32)
    partial = partial.astype(jnp.bfloat16)
    for place in range(per_sector):
        yield place, partial[:, place * width : (place + 1) * width]


def left_kernel(place_ref, from_ref, near_ref, far_ref, env_ref, out_ref, placed_ref):
    for place, partial in left_partials(place_ref, from_ref, near_ref, far_ref, env_ref, placed_ref):
        out_ref[:, place] = partial.reshape(out_ref.shape[0], SHARE, partial.shape[1])


def left_split_kernel(place_ref, from_ref, near_ref, far_ref, env_ref, keep_ref, send_ref, placed_ref):
    chips = keep_ref.shape[0]
    core = place_ref[2]
    for place, partial in left_partials(place_ref, from_ref, near_ref, far_ref, env_ref, placed_ref):
        halves = [
            jnp.stack(
                [partial[(2 * c + k) * SHARE : (2 * c + k + 1) * SHARE] for c in range(chips)]
            )
            for k in range(2)
        ]
        keep_ref[:, place] = jnp.where(core == 0, halves[0], halves[1])
        send_ref[:, place] = jnp.where(core == 0, halves[1], halves[0])


def left_products(place, source, near, far, left_env, chunk, split):
    _, sectors, extent, _ = left_env.shape
    terms, count = source.shape
    width = far.shape[-1]
    per_sector = count // sectors
    pieces = extent // SHARE // (2 if split else 1)
    out_spec = pl.BlockSpec((pieces, per_sector, SHARE, width), lambda i: (0, i, 0, 0))
    shape = jax.ShapeDtypeStruct((pieces, count, SHARE, width), jnp.bfloat16)
    return pl.pallas_call(
        left_split_kernel if split else left_kernel,
        grid=(sectors,),
        in_specs=[
            SMEM,
            SMEM,
            pl.BlockSpec(near.shape[:-1] + (width,), lambda i: (0, 0, 0, 0, chunk)),
            pl.BlockSpec(far.shape, lambda i: (0, 0, 0, 0, 0)),
            pl.BlockSpec((terms, 1, extent, extent), lambda i: (0, i, 0, 0)),
        ],
        out_specs=[out_spec, out_spec] if split else out_spec,
        out_shape=[shape, shape] if split else shape,
        scratch_shapes=[pltpu.VMEM((terms * extent, per_sector * width), jnp.bfloat16)],
        compiler_params=pltpu.CompilerParams(vmem_limit_bytes=VMEM_LIMIT),
        name="left_products",
    )(place, source, near, far, left_env)


def shift(array, axis, step):
    size = lax.axis_size(axis)
    return lax.ppermute(array, axis, [(i, (i + step) % size) for i in range(size)])


def local(wavefunction, right_home, term_links, sector_rows, sector_cols, left_env, right_env):
    count, _, width = wavefunction.shape
    per_sector = count // sector_rows.shape[0]
    slots = lax.axis_size(REMAP)
    layers = lax.axis_size("zh")
    group = slots // layers
    terms = term_links.shape[0]
    layer = lax.axis_index("zh")
    core_index = lax.axis_index("core")
    depth_index = lax.axis_index("y") * 2 + core_index
    place = jnp.stack([layer, lax.axis_index("y"), core_index])

    buffer = spread(depth_index.reshape(1), right_home, term_links, sector_rows, wavefunction, slots)
    arrived = lax.all_to_all(buffer, REMAP, 0, 0, tiled=True)
    labels = arrived[:, 2 * SHARE, : 1 + terms].astype(jnp.int32)
    match = labels.T[:, None, :] == jnp.arange(count, dtype=jnp.int32)[None, :, None]
    source = jnp.sum(jnp.where(match, jnp.arange(slots, dtype=jnp.int32), 0), axis=2)
    ordered = order(source[0], term_links, sector_cols, arrived)

    parts = [right_env[..., at : at + LANES] for at in range(0, width, LANES)]
    above = [shift(part, "zh", -1) for part in parts]
    below = [shift(part, "zh", 1) for part in parts]

    slices = lax.all_gather(ordered[None], DEPTH)
    around = lax.all_gather(ordered, "zh")
    around, above[0], below[0] = lax.optimization_barrier((around, above[0], below[0]))
    others = lax.dynamic_slice_in_dim(jnp.concatenate([around, around]), layer + 1, layers - 1)
    far_targets = others[:, count, 0, : terms * count].astype(jnp.int32)
    far_slices = lax.all_gather(others, DEPTH)

    targets = (term_links // count).reshape(1, terms * count)
    envs = [[(right_env, term) for term in range(terms)]]
    products = right_products(place, targets, slices, envs, group, 0, width)
    across = [
        (shift(up[:1], "zh", -1), shift(down[1:], "zh", 1)) for up, down in zip(above, below)
    ]
    products, above, below, across = lax.optimization_barrier((products, above, below, across))
    own = lax.all_to_all(products, GROUP, 0, 0, tiled=True)

    pieces = []
    for chunk in range(len(parts)):
        up, down = above[chunk], below[chunk]
        first, second = across[chunk]
        envs = [[(up, 0), (up, 1)], [(first, 0), (second, 0)], [(down, 0), (down, 1)]]
        products = right_products(place, far_targets, far_slices, envs, group, 0, LANES)
        far_slices, products = lax.optimization_barrier((far_slices, products))
        far = lax.all_to_all(products, GROUP, 0, 0, tiled=True)
        last = chunk + 1 == len(parts)
        partial = left_products(place, source[1:], own, far, left_env, chunk, last)
        if last:
            keep, send = partial
            pair = keep.astype(jnp.float32) + shift(send, "core", 1).astype(jnp.float32)
            gathered = lax.all_to_all(pair.astype(jnp.bfloat16), "y", 0, 0, tiled=True)
            pieces.append(jnp.sum(gathered.astype(jnp.float32), axis=0))
        else:
            summed = lax.psum_scatter(partial, DEPTH, scatter_dimension=0, tiled=False)
            pieces.append(summed.astype(jnp.float32))
    total = jnp.concatenate(pieces, axis=2)
    row = depth_index * SHARE + jnp.arange(SHARE, dtype=jnp.int32)
    keep_rows = row[None, :] < jnp.repeat(sector_rows, per_sector)[:, None]
    return jnp.where(keep_rows[:, :, None], total, 0.0).astype(jnp.bfloat16)


def solution(mesh):
    slots, depth = mesh.devices.shape
    split = Mesh(
        mesh.devices.reshape(4, 2, slots // 8, depth // 2, 2), ("zh", "zl", "x", "y", "core")
    )
    return jax.shard_map(
        local,
        mesh=split,
        in_specs=(
            P(REMAP, None, None),
            P(REMAP),
            P(DEPTH, REMAP),
            P(REMAP),
            P(REMAP),
            P(DEPTH, REMAP, None, None),
            P(DEPTH, REMAP, None, None),
        ),
        out_specs=P(REMAP, DEPTH, None),
        check_vma=False,
    )
```

```python
import functools

import jax
import jax.numpy as jnp
from jax import lax
from jax.experimental import pallas as pl
from jax.experimental.pallas import tpu as pltpu
from jax.sharding import Mesh, PartitionSpec as P

SHARE = 16
LANES = 128
VMEM_LIMIT = 40 * 1024 * 1024
REMAP = ("zh", "zl", "x")
GROUP = ("zl", "x")
DEPTH = ("y", "core")
SMEM = pl.BlockSpec(memory_space=pltpu.SMEM)


def in_hbm(array):
    return pltpu.with_memory_space_constraint(array, pltpu.HBM)


def spread_kernel(count, depth_ref, home_ref, links_ref, rows_ref, wave_ref, out_ref, label_ref):
    slots = out_ref.shape[0]
    terms = links_ref.shape[0]
    per_sector = count // rows_ref.shape[0]

    def clear(peer, carry):
        for kind in range(1 + terms):
            label_ref[kind, peer] = count
        return carry

    lax.fori_loop(0, slots, clear, 0)

    def fill(block, carry):
        home = home_ref[block]
        label_ref[0, lax.div(home, count)] = lax.rem(home, count)
        for term in range(terms):
            link = links_ref[term, block]
            label_ref[1 + term, lax.div(link, count)] = lax.rem(link, count)
        return carry

    lax.fori_loop(0, count, fill, 0)
    lane = lax.broadcasted_iota(jnp.int32, (SHARE, LANES), 1)

    def mark(peer, carry):
        tile = jnp.full(lane.shape, label_ref[0, peer], jnp.int32)
        for term in range(terms):
            tile = jnp.where(lane == 1 + term, label_ref[1 + term, peer], tile)
        out_ref[peer, 2 * SHARE :, :] = tile.astype(jnp.float32).astype(jnp.bfloat16)
        return carry

    lax.fori_loop(0, slots, mark, 0)
    row = lax.broadcasted_iota(jnp.int32, wave_ref.shape[1:], 0) + depth_ref[0] * SHARE

    def put(block, carry):
        owner = lax.div(home_ref[block], count)
        keep = row < rows_ref[lax.div(block, per_sector)]
        value = wave_ref[block]
        value = jnp.where(keep, value, jnp.zeros_like(value))
        out_ref[owner, 0:SHARE, :] = value[:, :LANES]
        out_ref[owner, SHARE : 2 * SHARE, :] = value[:, LANES:]
        return carry

    lax.fori_loop(0, count, put, 0)


def spread(depth, right_home, term_links, sector_rows, wavefunction, slots):
    count, _, width = wavefunction.shape
    return pl.pallas_call(
        functools.partial(spread_kernel, count),
        grid_spec=pltpu.PrefetchScalarGridSpec(
            num_scalar_prefetch=1,
            grid=(1,),
            in_specs=[
                SMEM,
                SMEM,
                SMEM,
                pl.BlockSpec((count, SHARE, width), lambda i, depth: (0, depth[0], 0)),
            ],
            out_specs=pl.BlockSpec((slots, 3 * SHARE, LANES), lambda i, depth: (0, 0, 0)),
            scratch_shapes=[pltpu.SMEM((1 + term_links.shape[0], slots), jnp.int32)],
        ),
        out_shape=pltpu.HBM((slots, 3 * SHARE, LANES), jnp.bfloat16),
        name="spread_blocks",
    )(depth, right_home, term_links, sector_rows, in_hbm(wavefunction))


def order_kernel(from_ref, links_ref, cols_ref, in_ref, out_ref):
    terms, count = links_ref.shape
    per_sector = count // cols_ref.shape[0]
    lane = lax.broadcasted_iota(jnp.int32, (SHARE, LANES), 1)
    targets = jnp.zeros(lane.shape, jnp.int32)
    for block in range(count):
        slot = from_ref[block]
        cols = cols_ref[block // per_sector]
        for part in range(2):
            value = in_ref[slot, part * SHARE : (part + 1) * SHARE, :]
            out_ref[block, part * SHARE : (part + 1) * SHARE, :] = jnp.where(
                lane + part * LANES < cols, value, jnp.zeros_like(value)
            )
        for term in range(terms):
            owner = lax.div(links_ref[term, block], count)
            targets = jnp.where(lane == term * count + block, owner, targets)
    targets = targets.astype(jnp.float32).astype(jnp.bfloat16)
    out_ref[count, 0:SHARE, :] = targets
    out_ref[count, SHARE:, :] = targets


def order(source, term_links, sector_cols, arrived):
    count = source.shape[0]
    return pl.pallas_call(
        order_kernel,
        in_specs=[SMEM, SMEM, SMEM, pl.BlockSpec(memory_space=pltpu.VMEM)],
        out_specs=pl.BlockSpec(memory_space=pltpu.VMEM),
        out_shape=jax.ShapeDtypeStruct((count + 1, 2 * SHARE, LANES), jnp.bfloat16),
        name="order_blocks",
    )(source, term_links, sector_cols, arrived)


def right_kernel(place_ref, targets_ref, slices_ref, *refs):
    envs, (out_ref, moved_ref, env_ref) = refs[:-3], refs[-3:]
    group, _, terms, extent, width = out_ref.shape
    sectors = env_ref.shape[0]
    depth, count = slices_ref.shape[0], slices_ref.shape[2] - 1
    per_sector = count // sectors
    turn = pl.program_id(0)
    for index in range(len(envs) // terms):

        @pl.when(turn == index)
        def _(index=index):
            for term in range(terms):
                env = envs[index * terms + term][0]
                env_ref[:, :, term * width : (term + 1) * width] = env

    for sector in range(sectors):
        half = sector % 2
        for share in range(depth):
            for place in range(per_sector):
                at = slice(place * extent + share * SHARE, place * extent + (share + 1) * SHARE)
                block = sector * per_sector + place
                moved_ref[half, at, 0:LANES] = slices_ref[share, 0, block, 0:SHARE, :]
                moved_ref[half, at, LANES:] = slices_ref[share, 0, block, SHARE:, :]
        product = jnp.dot(moved_ref[half], env_ref[sector], preferred_element_type=jnp.float32)
        product = product.astype(jnp.bfloat16)
        for place in range(per_sector):
            for term in range(terms):
                owner = targets_ref[turn, term * count + sector * per_sector + place]

                @pl.when(lax.div(owner, group) == place_ref[0])
                def _(place=place, term=term, owner=owner):
                    out_ref[lax.rem(owner, group), 0, term] = product[
                        place * extent : (place + 1) * extent, term * width : (term + 1) * width
                    ]


def right_products(place, targets, slices, envs, group, chunk, width):
    depth, layers, blocks, tall, lanes = slices.shape
    terms = len(envs[0])
    sectors, extent = envs[0][0][0].shape[1:3]
    per_sector = (blocks - 1) // sectors
    flat = [pair for layer in envs for pair in layer]
    shape = (group, layers, terms, extent, width)
    return pl.pallas_call(
        right_kernel,
        grid_spec=pltpu.PrefetchScalarGridSpec(
            num_scalar_prefetch=2,
            grid=(layers,),
            in_specs=[pl.BlockSpec((depth, 1, blocks, tall, lanes), lambda i, p, t: (0, i, 0, 0, 0))]
            + [
                pl.BlockSpec(
                    (1, sectors, extent, width), lambda i, p, t, term=term: (term, 0, 0, chunk)
                )
                for _, term in flat
            ],
            out_specs=pl.BlockSpec((group, 1, terms, extent, width), lambda i, p, t: (0, i, 0, 0, 0)),
            scratch_shapes=[
                pltpu.VMEM((2, per_sector * extent, extent), jnp.bfloat16),
                pltpu.VMEM((sectors, extent, terms * width), jnp.bfloat16),
            ],
        ),
        out_shape=pltpu.HBM(shape, jnp.bfloat16),
        compiler_params=pltpu.CompilerParams(vmem_limit_bytes=VMEM_LIMIT),
        name="right_products",
    )(place, targets, in_hbm(slices), *[array for array, _ in flat])


def far_products(place, targets, slices, above, below, across, group):
    envs = [
        [(above, 0), (above, 1)],
        [(across[0], 0), (across[1], 0)],
        [(below, 0), (below, 1)],
    ]
    return right_products(place, targets, slices, envs, group, 0, LANES)


def left_partials(place_ref, from_ref, near_ref, far_ref, env_ref, placed_ref):
    terms, count = from_ref.shape
    group, near, _, extent, width = near_ref.shape
    layers = near + far_ref.shape[1]
    per_sector = count // pl.num_programs(0)
    sector = pl.program_id(0)
    left = jnp.concatenate([env_ref[term, 0] for term in range(terms)], axis=1)
    for place in range(per_sector):
        for term in range(terms):
            device = from_ref[term, sector * per_sector + place]
            peer = lax.rem(device, group)
            step = lax.rem(lax.div(device, group) + layers - place_ref[0], layers)
            rows = slice(term * extent, (term + 1) * extent)
            columns = slice(place * width, (place + 1) * width)

            @pl.when(step < near)
            def _(term=term, peer=peer, step=step, rows=rows, columns=columns):
                placed_ref[rows, columns] = near_ref[peer, jnp.minimum(step, near - 1), term]

            @pl.when(step >= near)
            def _(term=term, peer=peer, step=step, rows=rows, columns=columns):
                placed_ref[rows, columns] = far_ref[peer, jnp.maximum(step - near, 0), term]

    partial = jnp.dot(left, placed_ref[...], preferred_element_type=jnp.float32)
    partial = partial.astype(jnp.bfloat16)
    for place in range(per_sector):
        yield place, partial[:, place * width : (place + 1) * width]


def left_kernel(place_ref, from_ref, near_ref, far_ref, env_ref, out_ref, placed_ref):
    for place, partial in left_partials(place_ref, from_ref, near_ref, far_ref, env_ref, placed_ref):
        out_ref[:, place] = partial.reshape(out_ref.shape[0], SHARE, partial.shape[1])


def left_split_kernel(place_ref, from_ref, near_ref, far_ref, env_ref, keep_ref, send_ref, placed_ref):
    chips = keep_ref.shape[0]
    core = place_ref[2]
    for place, partial in left_partials(place_ref, from_ref, near_ref, far_ref, env_ref, placed_ref):
        halves = [
            jnp.stack(
                [partial[(2 * c + k) * SHARE : (2 * c + k + 1) * SHARE] for c in range(chips)]
            )
            for k in range(2)
        ]
        keep_ref[:, place] = jnp.where(core == 0, halves[0], halves[1])
        send_ref[:, place] = jnp.where(core == 0, halves[1], halves[0])


def left_products(place, source, near, far, left_env, chunk, split):
    _, sectors, extent, _ = left_env.shape
    terms, count = source.shape
    width = far.shape[-1]
    per_sector = count // sectors
    pieces = extent // SHARE // (2 if split else 1)
    out_spec = pl.BlockSpec((pieces, per_sector, SHARE, width), lambda i: (0, i, 0, 0))
    shape = jax.ShapeDtypeStruct((pieces, count, SHARE, width), jnp.bfloat16)
    return pl.pallas_call(
        left_split_kernel if split else left_kernel,
        grid=(sectors,),
        in_specs=[
            SMEM,
            SMEM,
            pl.BlockSpec(near.shape[:-1] + (width,), lambda i: (0, 0, 0, 0, chunk)),
            pl.BlockSpec(far.shape, lambda i: (0, 0, 0, 0, 0)),
            pl.BlockSpec((terms, 1, extent, extent), lambda i: (0, i, 0, 0)),
        ],
        out_specs=[out_spec, out_spec] if split else out_spec,
        out_shape=[shape, shape] if split else shape,
        scratch_shapes=[pltpu.VMEM((terms * extent, per_sector * width), jnp.bfloat16)],
        compiler_params=pltpu.CompilerParams(vmem_limit_bytes=VMEM_LIMIT),
        name="left_products",
    )(place, source, near, far, left_env)


def shift(array, axis, step):
    size = lax.axis_size(axis)
    return lax.ppermute(array, axis, [(i, (i + step) % size) for i in range(size)])


def local(wavefunction, right_home, term_links, sector_rows, sector_cols, left_env, right_env):
    count, _, width = wavefunction.shape
    per_sector = count // sector_rows.shape[0]
    slots = lax.axis_size(REMAP)
    layers = lax.axis_size("zh")
    group = slots // layers
    terms = term_links.shape[0]
    layer = lax.axis_index("zh")
    core_index = lax.axis_index("core")
    depth_index = lax.axis_index("y") * 2 + core_index
    place = jnp.stack([layer, lax.axis_index("y"), core_index])

    buffer = spread(depth_index.reshape(1), right_home, term_links, sector_rows, wavefunction, slots)
    arrived = lax.all_to_all(buffer, REMAP, 0, 0, tiled=True)
    labels = arrived[:, 2 * SHARE, : 1 + terms].astype(jnp.int32)
    match = labels.T[:, None, :] == jnp.arange(count, dtype=jnp.int32)[None, :, None]
    source = jnp.sum(jnp.where(match, jnp.arange(slots, dtype=jnp.int32), 0), axis=2)
    ordered = order(source[0], term_links, sector_cols, arrived)

    parts = [right_env[..., at : at + LANES] for at in range(0, width, LANES)]
    above, below = shift(parts[0], "zh", -1), shift(parts[0], "zh", 1)
    across = shift(above[:1], "zh", -1), shift(below[1:], "zh", 1)

    slices = lax.all_gather(ordered[None], DEPTH)
    around = lax.all_gather(ordered, "zh")
    others = lax.dynamic_slice_in_dim(jnp.concatenate([around, around]), layer + 1, layers - 1)
    far_targets = others[:, count, 0, : terms * count].astype(jnp.int32)
    far_slices = lax.all_gather(others, DEPTH)

    targets = (term_links // count).reshape(1, terms * count)
    envs = [[(right_env, term) for term in range(terms)]]
    products = right_products(place, targets, slices, envs, group, 0, width)
    products, above, below, across = lax.optimization_barrier((products, above, below, across))
    own = lax.all_to_all(products, GROUP, 0, 0, tiled=True)

    own, second = lax.optimization_barrier((own, parts[1]))
    next_above, next_below = shift(second, "zh", -1), shift(second, "zh", 1)
    next_across = shift(next_above[:1], "zh", -1), shift(next_below[1:], "zh", 1)

    products = far_products(place, far_targets, far_slices, above, below, across, group)
    after = products, far_slices, next_above, next_below, next_across
    products, far_slices, next_above, next_below, next_across = lax.optimization_barrier(after)
    far = lax.all_to_all(products, GROUP, 0, 0, tiled=True)
    partial = left_products(place, source[1:], own, far, left_env, 0, False)
    partial = partial.reshape((-1, 2) + partial.shape[1:])
    summed = lax.psum_scatter(partial, "y", scatter_dimension=0, tiled=False)
    received = shift(lax.dynamic_index_in_dim(summed, 1 - core_index, 0, False), "core", 1)
    kept = lax.dynamic_index_in_dim(summed, core_index, 0, False)
    pieces = [kept.astype(jnp.float32) + received.astype(jnp.float32)]

    products = far_products(
        place, far_targets, far_slices, next_above, next_below, next_across, group
    )
    far = lax.all_to_all(products, GROUP, 0, 0, tiled=True)
    keep, send = left_products(place, source[1:], own, far, left_env, 1, True)
    pair = keep.astype(jnp.float32) + shift(send, "core", 1).astype(jnp.float32)
    shares = lax.all_to_all(pair.astype(jnp.bfloat16), "y", 0, 0, tiled=True)
    pieces.append(jnp.sum(shares.astype(jnp.float32), axis=0))
    total = jnp.concatenate(pieces, axis=2)
    row = depth_index * SHARE + jnp.arange(SHARE, dtype=jnp.int32)
    keep_rows = row[None, :] < jnp.repeat(sector_rows, per_sector)[:, None]
    return jnp.where(keep_rows[:, :, None], total, 0.0).astype(jnp.bfloat16)


def solution(mesh):
    slots, depth = mesh.devices.shape
    split = Mesh(
        mesh.devices.reshape(4, 2, slots // 8, depth // 2, 2), ("zh", "zl", "x", "y", "core")
    )
    return jax.shard_map(
        local,
        mesh=split,
        in_specs=(
            P(REMAP, None, None),
            P(REMAP),
            P(DEPTH, REMAP),
            P(REMAP),
            P(REMAP),
            P(DEPTH, REMAP, None, None),
            P(DEPTH, REMAP, None, None),
        ),
        out_specs=P(REMAP, DEPTH, None),
        check_vma=False,
    )
```

```python
import functools

import jax
import jax.numpy as jnp
from jax import lax
from jax.experimental import pallas as pl
from jax.experimental.pallas import tpu as pltpu
from jax.sharding import Mesh, PartitionSpec as P

SHARE = 16
LANES = 128
VMEM_LIMIT = 40 * 1024 * 1024
REMAP = ("zh", "zl", "x")
DEPTH = ("y", "core")
SMEM = pl.BlockSpec(memory_space=pltpu.SMEM)


def in_hbm(array):
    return pltpu.with_memory_space_constraint(array, pltpu.HBM)


def spread_kernel(count, depth_ref, home_ref, links_ref, rows_ref, wave_ref, out_ref, label_ref):
    slots = out_ref.shape[0]
    terms = links_ref.shape[0]
    per_sector = count // rows_ref.shape[0]

    def clear(peer, carry):
        for kind in range(1 + terms):
            label_ref[kind, peer] = count
        return carry

    lax.fori_loop(0, slots, clear, 0)

    def fill(block, carry):
        home = home_ref[block]
        label_ref[0, lax.div(home, count)] = lax.rem(home, count)
        for term in range(terms):
            link = links_ref[term, block]
            label_ref[1 + term, lax.div(link, count)] = lax.rem(link, count)
        return carry

    lax.fori_loop(0, count, fill, 0)
    lane = lax.broadcasted_iota(jnp.int32, (SHARE, LANES), 1)

    def mark(peer, carry):
        tile = jnp.full(lane.shape, label_ref[0, peer], jnp.int32)
        for term in range(terms):
            tile = jnp.where(lane == 1 + term, label_ref[1 + term, peer], tile)
        out_ref[peer, 2 * SHARE :, :] = tile.astype(jnp.float32).astype(jnp.bfloat16)
        return carry

    lax.fori_loop(0, slots, mark, 0)
    row = lax.broadcasted_iota(jnp.int32, wave_ref.shape[1:], 0) + depth_ref[0] * SHARE

    def put(block, carry):
        owner = lax.div(home_ref[block], count)
        keep = row < rows_ref[lax.div(block, per_sector)]
        value = wave_ref[block]
        value = jnp.where(keep, value, jnp.zeros_like(value))
        out_ref[owner, 0:SHARE, :] = value[:, :LANES]
        out_ref[owner, SHARE : 2 * SHARE, :] = value[:, LANES:]
        return carry

    lax.fori_loop(0, count, put, 0)


def spread(depth, right_home, term_links, sector_rows, wavefunction, slots):
    count, _, width = wavefunction.shape
    return pl.pallas_call(
        functools.partial(spread_kernel, count),
        grid_spec=pltpu.PrefetchScalarGridSpec(
            num_scalar_prefetch=1,
            grid=(1,),
            in_specs=[
                SMEM,
                SMEM,
                SMEM,
                pl.BlockSpec((count, SHARE, width), lambda i, depth: (0, depth[0], 0)),
            ],
            out_specs=pl.BlockSpec((slots, 3 * SHARE, LANES), lambda i, depth: (0, 0, 0)),
            scratch_shapes=[pltpu.SMEM((1 + term_links.shape[0], slots), jnp.int32)],
        ),
        out_shape=pltpu.HBM((slots, 3 * SHARE, LANES), jnp.bfloat16),
        name="spread_blocks",
    )(depth, right_home, term_links, sector_rows, in_hbm(wavefunction))


def order_kernel(from_ref, links_ref, cols_ref, in_ref, out_ref):
    terms, count = links_ref.shape
    per_sector = count // cols_ref.shape[0]
    lane = lax.broadcasted_iota(jnp.int32, (SHARE, LANES), 1)
    targets = jnp.zeros(lane.shape, jnp.int32)
    for block in range(count):
        slot = from_ref[block]
        cols = cols_ref[block // per_sector]
        for part in range(2):
            value = in_ref[slot, part * SHARE : (part + 1) * SHARE, :]
            out_ref[block, part * SHARE : (part + 1) * SHARE, :] = jnp.where(
                lane + part * LANES < cols, value, jnp.zeros_like(value)
            )
        for term in range(terms):
            owner = lax.div(links_ref[term, block], count)
            targets = jnp.where(lane == term * count + block, owner, targets)
    targets = targets.astype(jnp.float32).astype(jnp.bfloat16)
    out_ref[count, 0:SHARE, :] = targets
    out_ref[count, SHARE:, :] = targets


def order(source, term_links, sector_cols, arrived):
    count = source.shape[0]
    return pl.pallas_call(
        order_kernel,
        in_specs=[SMEM, SMEM, SMEM, pl.BlockSpec(memory_space=pltpu.VMEM)],
        out_specs=pl.BlockSpec(memory_space=pltpu.VMEM),
        out_shape=jax.ShapeDtypeStruct((count + 1, 2 * SHARE, LANES), jnp.bfloat16),
        name="order_blocks",
    )(source, term_links, sector_cols, arrived)


def right_kernel(place_ref, targets_ref, slices_ref, *refs):
    envs, (out_ref, moved_ref, env_ref) = refs[:-3], refs[-3:]
    group, _, terms, extent, width = out_ref.shape
    sectors = env_ref.shape[0]
    depth, count = slices_ref.shape[0], slices_ref.shape[2] - 1
    per_sector = count // sectors
    turn = pl.program_id(0)
    for index in range(len(envs) // terms):

        @pl.when(turn == index)
        def _(index=index):
            for term in range(terms):
                env = envs[index * terms + term][0]
                env_ref[:, :, term * width : (term + 1) * width] = env

    for sector in range(sectors):
        half = sector % 2
        for share in range(depth):
            for place in range(per_sector):
                at = slice(place * extent + share * SHARE, place * extent + (share + 1) * SHARE)
                block = sector * per_sector + place
                moved_ref[half, at, 0:LANES] = slices_ref[share, 0, block, 0:SHARE, :]
                moved_ref[half, at, LANES:] = slices_ref[share, 0, block, SHARE:, :]
        product = jnp.dot(moved_ref[half], env_ref[sector], preferred_element_type=jnp.float32)
        product = product.astype(jnp.bfloat16)
        for place in range(per_sector):
            for term in range(terms):
                owner = targets_ref[turn, term * count + sector * per_sector + place]

                @pl.when(lax.div(owner, group) == place_ref[0])
                def _(place=place, term=term, owner=owner):
                    out_ref[lax.rem(owner, group), 0, term] = product[
                        place * extent : (place + 1) * extent, term * width : (term + 1) * width
                    ]


def right_products(place, targets, slices, envs, group, chunk, width):
    depth, layers, blocks, tall, lanes = slices.shape
    terms = len(envs[0])
    sectors, extent = envs[0][0][0].shape[1:3]
    per_sector = (blocks - 1) // sectors
    flat = [pair for layer in envs for pair in layer]
    shape = (group, layers, terms, extent, width)
    return pl.pallas_call(
        right_kernel,
        grid_spec=pltpu.PrefetchScalarGridSpec(
            num_scalar_prefetch=2,
            grid=(layers,),
            in_specs=[pl.BlockSpec((depth, 1, blocks, tall, lanes), lambda i, p, t: (0, i, 0, 0, 0))]
            + [
                pl.BlockSpec(
                    (1, sectors, extent, width), lambda i, p, t, term=term: (term, 0, 0, chunk)
                )
                for _, term in flat
            ],
            out_specs=pl.BlockSpec((group, 1, terms, extent, width), lambda i, p, t: (0, i, 0, 0, 0)),
            scratch_shapes=[
                pltpu.VMEM((2, per_sector * extent, extent), jnp.bfloat16),
                pltpu.VMEM((sectors, extent, terms * width), jnp.bfloat16),
            ],
        ),
        out_shape=pltpu.HBM(shape, jnp.bfloat16),
        compiler_params=pltpu.CompilerParams(vmem_limit_bytes=VMEM_LIMIT),
        name="right_products",
    )(place, targets, in_hbm(slices), *[array for array, _ in flat])


def far_products(place, targets, slices, above, below, across, group):
    envs = [
        [(above, 0), (above, 1)],
        [(across[0], 0), (across[1], 0)],
        [(below, 0), (below, 1)],
    ]
    return right_products(place, targets, slices, envs, group, 0, LANES)


def left_partials(place_ref, from_ref, near_ref, far_ref, env_ref, placed_ref):
    terms, count = from_ref.shape
    group, near, _, extent, width = near_ref.shape
    layers = near + far_ref.shape[1]
    per_sector = count // pl.num_programs(0)
    sector = pl.program_id(0)
    left = jnp.concatenate([env_ref[term, 0] for term in range(terms)], axis=1)
    for place in range(per_sector):
        for term in range(terms):
            device = from_ref[term, sector * per_sector + place]
            peer = lax.rem(device, group)
            step = lax.rem(lax.div(device, group) + layers - place_ref[0], layers)
            rows = slice(term * extent, (term + 1) * extent)
            columns = slice(place * width, (place + 1) * width)

            @pl.when(step < near)
            def _(term=term, peer=peer, step=step, rows=rows, columns=columns):
                placed_ref[rows, columns] = near_ref[peer, jnp.minimum(step, near - 1), term]

            @pl.when(step >= near)
            def _(term=term, peer=peer, step=step, rows=rows, columns=columns):
                placed_ref[rows, columns] = far_ref[peer, jnp.maximum(step - near, 0), term]

    partial = jnp.dot(left, placed_ref[...], preferred_element_type=jnp.float32)
    partial = partial.astype(jnp.bfloat16)
    for place in range(per_sector):
        yield place, partial[:, place * width : (place + 1) * width]


def left_kernel(place_ref, from_ref, near_ref, far_ref, env_ref, out_ref, placed_ref):
    for place, partial in left_partials(place_ref, from_ref, near_ref, far_ref, env_ref, placed_ref):
        out_ref[:, place] = partial.reshape(out_ref.shape[0], SHARE, partial.shape[1])


def left_split_kernel(place_ref, from_ref, near_ref, far_ref, env_ref, keep_ref, send_ref, placed_ref):
    chips = keep_ref.shape[0]
    core = place_ref[2]
    for place, partial in left_partials(place_ref, from_ref, near_ref, far_ref, env_ref, placed_ref):
        halves = [
            jnp.stack(
                [partial[(2 * c + k) * SHARE : (2 * c + k + 1) * SHARE] for c in range(chips)]
            )
            for k in range(2)
        ]
        keep_ref[:, place] = jnp.where(core == 0, halves[0], halves[1])
        send_ref[:, place] = jnp.where(core == 0, halves[1], halves[0])


def left_products(place, source, near, far, left_env, chunk, split):
    _, sectors, extent, _ = left_env.shape
    terms, count = source.shape
    width = far.shape[-1]
    per_sector = count // sectors
    pieces = extent // SHARE // (2 if split else 1)
    out_spec = pl.BlockSpec((pieces, per_sector, SHARE, width), lambda i: (0, i, 0, 0))
    shape = jax.ShapeDtypeStruct((pieces, count, SHARE, width), jnp.bfloat16)
    return pl.pallas_call(
        left_split_kernel if split else left_kernel,
        grid=(sectors,),
        in_specs=[
            SMEM,
            SMEM,
            pl.BlockSpec(near.shape[:-1] + (width,), lambda i: (0, 0, 0, 0, chunk)),
            pl.BlockSpec(far.shape, lambda i: (0, 0, 0, 0, 0)),
            pl.BlockSpec((terms, 1, extent, extent), lambda i: (0, i, 0, 0)),
        ],
        out_specs=[out_spec, out_spec] if split else out_spec,
        out_shape=[shape, shape] if split else shape,
        scratch_shapes=[pltpu.VMEM((terms * extent, per_sector * width), jnp.bfloat16)],
        compiler_params=pltpu.CompilerParams(vmem_limit_bytes=VMEM_LIMIT),
        name="left_products",
    )(place, source, near, far, left_env)


def shift(array, axis, step):
    size = lax.axis_size(axis)
    return lax.ppermute(array, axis, [(i, (i + step) % size) for i in range(size)])


def exchange(products):
    axes = ("zh", "zl", "x", "core")
    along_x, cores = lax.axis_size("x"), lax.axis_size("core")
    along_z = lax.axis_size("zh") * lax.axis_size("zl")
    groups = [
        [
            (((2 * pair + core + step) % along_z) * along_x + x) * cores + core
            for step in range(2)
            for x in range(along_x)
        ]
        for core in range(cores)
        for pair in range(along_z // 2)
    ]
    return lax.all_to_all(products, axes, 0, 0, axis_index_groups=groups, tiled=True)


def local(wavefunction, right_home, term_links, sector_rows, sector_cols, left_env, right_env):
    count, _, width = wavefunction.shape
    per_sector = count // sector_rows.shape[0]
    slots = lax.axis_size(REMAP)
    layers = lax.axis_size("zh")
    group = slots // layers
    terms = term_links.shape[0]
    layer = lax.axis_index("zh")
    core_index = lax.axis_index("core")
    depth_index = lax.axis_index("y") * 2 + core_index
    scheme_index = lax.rem(lax.axis_index(REMAP) + slots - core_index * (group // 2), slots)
    place = jnp.stack([scheme_index // group, lax.axis_index("y"), core_index])

    buffer = spread(depth_index.reshape(1), right_home, term_links, sector_rows, wavefunction, slots)
    arrived = lax.all_to_all(buffer, REMAP, 0, 0, tiled=True)
    labels = arrived[:, 2 * SHARE, : 1 + terms].astype(jnp.int32)
    match = labels.T[:, None, :] == jnp.arange(count, dtype=jnp.int32)[None, :, None]
    source = jnp.sum(jnp.where(match, jnp.arange(slots, dtype=jnp.int32), 0), axis=2)
    moved_by = slots - core_index * (group // 2)
    peers = lax.rem(source[1:] + moved_by, slots)
    ordered = order(source[0], term_links, sector_cols, arrived)

    parts = [right_env[..., at : at + LANES] for at in range(0, width, LANES)]
    above, below = shift(parts[0], "zh", -1), shift(parts[0], "zh", 1)
    across = shift(above[:1], "zh", -1), shift(below[1:], "zh", 1)

    slices = lax.all_gather(ordered[None], DEPTH)
    around = lax.all_gather(ordered, "zh")
    others = lax.dynamic_slice_in_dim(jnp.concatenate([around, around]), layer + 1, layers - 1)
    far_targets = others[:, count, 0, : terms * count].astype(jnp.int32)
    far_targets = lax.rem(far_targets + moved_by, slots)
    far_slices = lax.all_gather(others, DEPTH)

    targets = lax.rem((term_links // count).reshape(1, terms * count) + moved_by, slots)
    envs = [[(right_env, term) for term in range(terms)]]
    products = right_products(place, targets, slices, envs, group, 0, width)
    products, above, below = lax.optimization_barrier((products, above, below))
    own = exchange(products)

    across, second = lax.optimization_barrier((across, parts[1]))
    next_above, next_below = shift(second, "zh", -1), shift(second, "zh", 1)
    next_across = shift(next_above[:1], "zh", -1), shift(next_below[1:], "zh", 1)

    products = far_products(place, far_targets, far_slices, above, below, across, group)
    after = products, far_slices, next_above, next_below
    products, far_slices, next_above, next_below = lax.optimization_barrier(after)
    far = exchange(products)
    partial = left_products(place, peers, own, far, left_env, 0, False)
    partial = partial.reshape((-1, 2) + partial.shape[1:])
    summed = lax.psum_scatter(partial, "y", scatter_dimension=0, tiled=False)
    received = shift(lax.dynamic_index_in_dim(summed, 1 - core_index, 0, False), "core", 1)
    kept = lax.dynamic_index_in_dim(summed, core_index, 0, False)
    pieces = [kept.astype(jnp.float32) + received.astype(jnp.float32)]

    products = far_products(
        place, far_targets, far_slices, next_above, next_below, next_across, group
    )
    far = exchange(products)
    keep, send = left_products(place, peers, own, far, left_env, 1, True)
    pair = keep.astype(jnp.float32) + shift(send, "core", 1).astype(jnp.float32)
    shares = lax.all_to_all(pair.astype(jnp.bfloat16), "y", 0, 0, tiled=True)
    pieces.append(jnp.sum(shares.astype(jnp.float32), axis=0))
    total = jnp.concatenate(pieces, axis=2)
    row = depth_index * SHARE + jnp.arange(SHARE, dtype=jnp.int32)
    keep_rows = row[None, :] < jnp.repeat(sector_rows, per_sector)[:, None]
    return jnp.where(keep_rows[:, :, None], total, 0.0).astype(jnp.bfloat16)


def solution(mesh):
    slots, depth = mesh.devices.shape
    split = Mesh(
        mesh.devices.reshape(4, 2, slots // 8, depth // 2, 2), ("zh", "zl", "x", "y", "core")
    )
    return jax.shard_map(
        local,
        mesh=split,
        in_specs=(
            P(REMAP, None, None),
            P(REMAP),
            P(DEPTH, REMAP),
            P(REMAP),
            P(REMAP),
            P(DEPTH, REMAP, None, None),
            P(DEPTH, REMAP, None, None),
        ),
        out_specs=P(REMAP, DEPTH, None),
        check_vma=False,
    )
```

```python
import functools

import jax
import jax.numpy as jnp
from jax import lax
from jax.experimental import pallas as pl
from jax.experimental.pallas import tpu as pltpu
from jax.sharding import Mesh, PartitionSpec as P

SHARE = 16
LANES = 128
VMEM_LIMIT = 40 * 1024 * 1024
REMAP = ("zh", "zl", "x")
DEPTH = ("y", "core")
SMEM = pl.BlockSpec(memory_space=pltpu.SMEM)


def in_hbm(array):
    return pltpu.with_memory_space_constraint(array, pltpu.HBM)


def spread_kernel(count, depth_ref, home_ref, links_ref, rows_ref, wave_ref, out_ref, label_ref):
    slots = out_ref.shape[0]
    terms = links_ref.shape[0]
    per_sector = count // rows_ref.shape[0]

    def clear(peer, carry):
        for kind in range(1 + terms):
            label_ref[kind, peer] = count
        return carry

    lax.fori_loop(0, slots, clear, 0)

    def fill(block, carry):
        home = home_ref[block]
        label_ref[0, lax.div(home, count)] = lax.rem(home, count)
        for term in range(terms):
            link = links_ref[term, block]
            label_ref[1 + term, lax.div(link, count)] = lax.rem(link, count)
        return carry

    lax.fori_loop(0, count, fill, 0)
    lane = lax.broadcasted_iota(jnp.int32, (SHARE, LANES), 1)

    def mark(peer, carry):
        tile = jnp.full(lane.shape, label_ref[0, peer], jnp.int32)
        for term in range(terms):
            tile = jnp.where(lane == 1 + term, label_ref[1 + term, peer], tile)
        out_ref[peer, 2 * SHARE :, :] = tile.astype(jnp.float32).astype(jnp.bfloat16)
        return carry

    lax.fori_loop(0, slots, mark, 0)
    row = lax.broadcasted_iota(jnp.int32, wave_ref.shape[1:], 0) + depth_ref[0] * SHARE

    def put(block, carry):
        owner = lax.div(home_ref[block], count)
        keep = row < rows_ref[lax.div(block, per_sector)]
        value = wave_ref[block]
        value = jnp.where(keep, value, jnp.zeros_like(value))
        out_ref[owner, 0:SHARE, :] = value[:, :LANES]
        out_ref[owner, SHARE : 2 * SHARE, :] = value[:, LANES:]
        return carry

    lax.fori_loop(0, count, put, 0)


def spread(depth, right_home, term_links, sector_rows, wavefunction, slots):
    count, _, width = wavefunction.shape
    return pl.pallas_call(
        functools.partial(spread_kernel, count),
        grid_spec=pltpu.PrefetchScalarGridSpec(
            num_scalar_prefetch=1,
            grid=(1,),
            in_specs=[
                SMEM,
                SMEM,
                SMEM,
                pl.BlockSpec((count, SHARE, width), lambda i, depth: (0, depth[0], 0)),
            ],
            out_specs=pl.BlockSpec((slots, 3 * SHARE, LANES), lambda i, depth: (0, 0, 0)),
            scratch_shapes=[pltpu.SMEM((1 + term_links.shape[0], slots), jnp.int32)],
        ),
        out_shape=pltpu.HBM((slots, 3 * SHARE, LANES), jnp.bfloat16),
        name="spread_blocks",
    )(depth, right_home, term_links, sector_rows, in_hbm(wavefunction))


def order_kernel(from_ref, links_ref, cols_ref, in_ref, out_ref):
    terms, count = links_ref.shape
    per_sector = count // cols_ref.shape[0]
    lane = lax.broadcasted_iota(jnp.int32, (SHARE, LANES), 1)
    targets = jnp.zeros(lane.shape, jnp.int32)
    for block in range(count):
        slot = from_ref[block]
        cols = cols_ref[block // per_sector]
        for part in range(2):
            value = in_ref[slot, part * SHARE : (part + 1) * SHARE, :]
            out_ref[block, part * SHARE : (part + 1) * SHARE, :] = jnp.where(
                lane + part * LANES < cols, value, jnp.zeros_like(value)
            )
        for term in range(terms):
            owner = lax.div(links_ref[term, block], count)
            targets = jnp.where(lane == term * count + block, owner, targets)
    targets = targets.astype(jnp.float32).astype(jnp.bfloat16)
    out_ref[count, 0:SHARE, :] = targets
    out_ref[count, SHARE:, :] = targets


def order(source, term_links, sector_cols, arrived):
    count = source.shape[0]
    return pl.pallas_call(
        order_kernel,
        in_specs=[SMEM, SMEM, SMEM, pl.BlockSpec(memory_space=pltpu.VMEM)],
        out_specs=pl.BlockSpec(memory_space=pltpu.VMEM),
        out_shape=jax.ShapeDtypeStruct((count + 1, 2 * SHARE, LANES), jnp.bfloat16),
        name="order_blocks",
    )(source, term_links, sector_cols, arrived)


def right_kernel(place_ref, targets_ref, slices_ref, *refs):
    envs, (out_ref, moved_ref, env_ref) = refs[:-3], refs[-3:]
    group, _, terms, extent, width = out_ref.shape
    sectors = env_ref.shape[0]
    depth, count = slices_ref.shape[0], slices_ref.shape[2] - 1
    per_sector = count // sectors
    turn = pl.program_id(0)
    for index in range(len(envs) // terms):

        @pl.when(turn == index)
        def _(index=index):
            for term in range(terms):
                env = envs[index * terms + term][0]
                env_ref[:, :, term * width : (term + 1) * width] = env

    for sector in range(sectors):
        half = sector % 2
        for share in range(depth):
            for place in range(per_sector):
                at = slice(place * extent + share * SHARE, place * extent + (share + 1) * SHARE)
                block = sector * per_sector + place
                moved_ref[half, at, 0:LANES] = slices_ref[share, 0, block, 0:SHARE, :]
                moved_ref[half, at, LANES:] = slices_ref[share, 0, block, SHARE:, :]
        product = jnp.dot(moved_ref[half], env_ref[sector], preferred_element_type=jnp.float32)
        product = product.astype(jnp.bfloat16)
        for place in range(per_sector):
            for term in range(terms):
                owner = targets_ref[turn, term * count + sector * per_sector + place]

                @pl.when(lax.div(owner, group) == place_ref[0])
                def _(place=place, term=term, owner=owner):
                    out_ref[lax.rem(owner, group), 0, term] = product[
                        place * extent : (place + 1) * extent, term * width : (term + 1) * width
                    ]


def right_products(place, targets, slices, envs, group, chunk, width):
    depth, layers, blocks, tall, lanes = slices.shape
    terms = len(envs[0])
    sectors, extent = envs[0][0][0].shape[1:3]
    per_sector = (blocks - 1) // sectors
    flat = [pair for layer in envs for pair in layer]
    shape = (group, layers, terms, extent, width)
    return pl.pallas_call(
        right_kernel,
        grid_spec=pltpu.PrefetchScalarGridSpec(
            num_scalar_prefetch=2,
            grid=(layers,),
            in_specs=[pl.BlockSpec((depth, 1, blocks, tall, lanes), lambda i, p, t: (0, i, 0, 0, 0))]
            + [
                pl.BlockSpec(
                    (1, sectors, extent, width), lambda i, p, t, term=term: (term, 0, 0, chunk)
                )
                for _, term in flat
            ],
            out_specs=pl.BlockSpec((group, 1, terms, extent, width), lambda i, p, t: (0, i, 0, 0, 0)),
            scratch_shapes=[
                pltpu.VMEM((2, per_sector * extent, extent), jnp.bfloat16),
                pltpu.VMEM((sectors, extent, terms * width), jnp.bfloat16),
            ],
        ),
        out_shape=pltpu.HBM(shape, jnp.bfloat16),
        compiler_params=pltpu.CompilerParams(vmem_limit_bytes=VMEM_LIMIT),
        name="right_products",
    )(place, targets, in_hbm(slices), *[array for array, _ in flat])


def left_partials(place_ref, from_ref, own_ref, side_ref, back_ref, env_ref, placed_ref):
    terms, count = from_ref.shape
    group, _, _, extent, width = own_ref.shape
    layers = 2 + side_ref.shape[1]
    per_sector = count // pl.num_programs(0)
    sector = pl.program_id(0)
    left = jnp.concatenate([env_ref[term, 0] for term in range(terms)], axis=1)
    for place in range(per_sector):
        for term in range(terms):
            device = from_ref[term, sector * per_sector + place]
            peer = lax.rem(device, group)
            step = lax.rem(lax.div(device, group) + layers - place_ref[0], layers)
            rows = slice(term * extent, (term + 1) * extent)
            columns = slice(place * width, (place + 1) * width)

            @pl.when(step == 0)
            def _(term=term, peer=peer, rows=rows, columns=columns):
                placed_ref[rows, columns] = own_ref[peer, 0, term]

            @pl.when(step == layers // 2)
            def _(term=term, peer=peer, rows=rows, columns=columns):
                placed_ref[rows, columns] = back_ref[peer, 0, term]

            @pl.when(lax.rem(step, 2) == 1)
            def _(term=term, peer=peer, step=step, rows=rows, columns=columns):
                placed_ref[rows, columns] = side_ref[peer, lax.div(step, 2), term]

    partial = jnp.dot(left, placed_ref[...], preferred_element_type=jnp.float32)
    partial = partial.astype(jnp.bfloat16)
    for place in range(per_sector):
        yield place, partial[:, place * width : (place + 1) * width]


def left_kernel(place_ref, from_ref, own_ref, side_ref, back_ref, env_ref, out_ref, placed_ref):
    for place, partial in left_partials(place_ref, from_ref, own_ref, side_ref, back_ref, env_ref, placed_ref):
        out_ref[:, place] = partial.reshape(out_ref.shape[0], SHARE, partial.shape[1])


def left_split_kernel(place_ref, from_ref, own_ref, side_ref, back_ref, env_ref, keep_ref, send_ref, placed_ref):
    chips = keep_ref.shape[0]
    core = place_ref[2]
    for place, partial in left_partials(place_ref, from_ref, own_ref, side_ref, back_ref, env_ref, placed_ref):
        halves = [
            jnp.stack(
                [partial[(2 * c + k) * SHARE : (2 * c + k + 1) * SHARE] for c in range(chips)]
            )
            for k in range(2)
        ]
        keep_ref[:, place] = jnp.where(core == 0, halves[0], halves[1])
        send_ref[:, place] = jnp.where(core == 0, halves[1], halves[0])


def left_products(place, source, own, side, back, left_env, chunk, split):
    _, sectors, extent, _ = left_env.shape
    terms, count = source.shape
    width = side.shape[-1]
    per_sector = count // sectors
    pieces = extent // SHARE // (2 if split else 1)
    out_spec = pl.BlockSpec((pieces, per_sector, SHARE, width), lambda i: (0, i, 0, 0))
    shape = jax.ShapeDtypeStruct((pieces, count, SHARE, width), jnp.bfloat16)
    return pl.pallas_call(
        left_split_kernel if split else left_kernel,
        grid=(sectors,),
        in_specs=[
            SMEM,
            SMEM,
            pl.BlockSpec(own.shape[:-1] + (width,), lambda i: (0, 0, 0, 0, chunk)),
            pl.BlockSpec(side.shape, lambda i: (0, 0, 0, 0, 0)),
            pl.BlockSpec(back.shape, lambda i: (0, 0, 0, 0, 0)),
            pl.BlockSpec((terms, 1, extent, extent), lambda i: (0, i, 0, 0)),
        ],
        out_specs=[out_spec, out_spec] if split else out_spec,
        out_shape=[shape, shape] if split else shape,
        scratch_shapes=[pltpu.VMEM((terms * extent, per_sector * width), jnp.bfloat16)],
        compiler_params=pltpu.CompilerParams(vmem_limit_bytes=VMEM_LIMIT),
        name="left_products",
    )(place, source, own, side, back, left_env)


def shift(array, axis, step):
    size = lax.axis_size(axis)
    return lax.ppermute(array, axis, [(i, (i + step) % size) for i in range(size)])


def exchange(products):
    axes = ("zh", "zl", "x", "core")
    along_x, cores = lax.axis_size("x"), lax.axis_size("core")
    along_z = lax.axis_size("zh") * lax.axis_size("zl")
    groups = [
        [
            (((2 * pair + core + step) % along_z) * along_x + x) * cores + core
            for step in range(2)
            for x in range(along_x)
        ]
        for core in range(cores)
        for pair in range(along_z // 2)
    ]
    return lax.all_to_all(products, axes, 0, 0, axis_index_groups=groups, tiled=True)


def local(wavefunction, right_home, term_links, sector_rows, sector_cols, left_env, right_env):
    count, _, width = wavefunction.shape
    per_sector = count // sector_rows.shape[0]
    slots = lax.axis_size(REMAP)
    layers = lax.axis_size("zh")
    group = slots // layers
    terms = term_links.shape[0]
    layer = lax.axis_index("zh")
    core_index = lax.axis_index("core")
    depth_index = lax.axis_index("y") * 2 + core_index
    scheme_index = lax.rem(lax.axis_index(REMAP) + slots - core_index * (group // 2), slots)
    place = jnp.stack([scheme_index // group, lax.axis_index("y"), core_index])

    buffer = spread(depth_index.reshape(1), right_home, term_links, sector_rows, wavefunction, slots)
    arrived = lax.all_to_all(buffer, REMAP, 0, 0, tiled=True)
    labels = arrived[:, 2 * SHARE, : 1 + terms].astype(jnp.int32)
    match = labels.T[:, None, :] == jnp.arange(count, dtype=jnp.int32)[None, :, None]
    source = jnp.sum(jnp.where(match, jnp.arange(slots, dtype=jnp.int32), 0), axis=2)
    moved_by = slots - core_index * (group // 2)
    peers = lax.rem(source[1:] + moved_by, slots)
    ordered = order(source[0], term_links, sector_cols, arrived)

    above, below = shift(right_env, "zh", -1), shift(right_env, "zh", 1)
    across = shift(above[:1], "zh", -1), shift(below[1:], "zh", 1)

    slices = lax.all_gather(ordered[None], DEPTH)
    around = lax.all_gather(ordered, "zh")
    others = lax.dynamic_slice_in_dim(jnp.concatenate([around, around]), layer + 1, layers - 1)
    far_targets = others[:, count, 0, : terms * count].astype(jnp.int32)
    far_targets = lax.rem(far_targets + moved_by, slots)
    side_slices = lax.all_gather(jnp.stack([others[0], others[2]]), DEPTH)
    back_slices = lax.all_gather(others[1:2], DEPTH)

    targets = lax.rem((term_links // count).reshape(1, terms * count) + moved_by, slots)
    envs = [[(right_env, term) for term in range(terms)]]
    products = right_products(place, targets, slices, envs, group, 0, width)
    products, above, below = lax.optimization_barrier((products, above, below))
    own = exchange(products)

    sides, backs = [], []
    targets = jnp.stack([far_targets[0], far_targets[2]])
    envs = [[(above, 0), (above, 1)], [(below, 0), (below, 1)]]
    for chunk in range(width // LANES):
        products = right_products(place, targets, side_slices, envs, group, chunk, LANES)
        if sides:
            after = products, sides[-1], across
            products, sides[-1], across = lax.optimization_barrier(after)
        else:
            products, own = lax.optimization_barrier((products, own))
        sides.append(exchange(products))
    envs = [[(across[0], 0), (across[1], 0)]]
    for chunk in range(width // LANES):
        products = right_products(place, far_targets[1:2], back_slices, envs, group, chunk, LANES)
        if backs:
            products, backs[-1] = lax.optimization_barrier((products, backs[-1]))
        else:
            products, sides[-1] = lax.optimization_barrier((products, sides[-1]))
        backs.append(exchange(products))

    partial = left_products(place, peers, own, sides[0], backs[0], left_env, 0, False)
    partial = partial.reshape((-1, 2) + partial.shape[1:])
    summed = lax.psum_scatter(partial, "y", scatter_dimension=0, tiled=False)
    received = shift(lax.dynamic_index_in_dim(summed, 1 - core_index, 0, False), "core", 1)
    kept = lax.dynamic_index_in_dim(summed, core_index, 0, False)
    pieces = [kept.astype(jnp.float32) + received.astype(jnp.float32)]

    keep, send = left_products(place, peers, own, sides[1], backs[1], left_env, 1, True)
    pair = keep.astype(jnp.float32) + shift(send, "core", 1).astype(jnp.float32)
    shares = lax.all_to_all(pair.astype(jnp.bfloat16), "y", 0, 0, tiled=True)
    pieces.append(jnp.sum(shares.astype(jnp.float32), axis=0))
    total = jnp.concatenate(pieces, axis=2)
    row = depth_index * SHARE + jnp.arange(SHARE, dtype=jnp.int32)
    keep_rows = row[None, :] < jnp.repeat(sector_rows, per_sector)[:, None]
    return jnp.where(keep_rows[:, :, None], total, 0.0).astype(jnp.bfloat16)


def solution(mesh):
    slots, depth = mesh.devices.shape
    split = Mesh(
        mesh.devices.reshape(4, 2, slots // 8, depth // 2, 2), ("zh", "zl", "x", "y", "core")
    )
    return jax.shard_map(
        local,
        mesh=split,
        in_specs=(
            P(REMAP, None, None),
            P(REMAP),
            P(DEPTH, REMAP),
            P(REMAP),
            P(REMAP),
            P(DEPTH, REMAP, None, None),
            P(DEPTH, REMAP, None, None),
        ),
        out_specs=P(REMAP, DEPTH, None),
        check_vma=False,
    )
```

```python
import functools

import jax
import jax.numpy as jnp
from jax import lax
from jax.experimental import pallas as pl
from jax.experimental.pallas import tpu as pltpu
from jax.sharding import Mesh, PartitionSpec as P

SHARE = 16
LANES = 128
VMEM_LIMIT = 40 * 1024 * 1024
REMAP = ("zh", "zl", "x")
DEPTH = ("y", "core")
SMEM = pl.BlockSpec(memory_space=pltpu.SMEM)


def in_hbm(array):
    return pltpu.with_memory_space_constraint(array, pltpu.HBM)


def spread_kernel(count, depth_ref, home_ref, links_ref, rows_ref, wave_ref, out_ref, label_ref):
    slots = out_ref.shape[0]
    terms = links_ref.shape[0]
    per_sector = count // rows_ref.shape[0]

    def clear(peer, carry):
        for kind in range(1 + terms):
            label_ref[kind, peer] = count
        return carry

    lax.fori_loop(0, slots, clear, 0)

    def fill(block, carry):
        home = home_ref[block]
        label_ref[0, lax.div(home, count)] = lax.rem(home, count)
        for term in range(terms):
            link = links_ref[term, block]
            label_ref[1 + term, lax.div(link, count)] = lax.rem(link, count)
        return carry

    lax.fori_loop(0, count, fill, 0)
    lane = lax.broadcasted_iota(jnp.int32, (SHARE, LANES), 1)

    def mark(peer, carry):
        tile = jnp.full(lane.shape, label_ref[0, peer], jnp.int32)
        for term in range(terms):
            tile = jnp.where(lane == 1 + term, label_ref[1 + term, peer], tile)
        out_ref[peer, 2 * SHARE :, :] = tile.astype(jnp.float32).astype(jnp.bfloat16)
        return carry

    lax.fori_loop(0, slots, mark, 0)
    row = lax.broadcasted_iota(jnp.int32, wave_ref.shape[1:], 0) + depth_ref[0] * SHARE

    def put(block, carry):
        owner = lax.div(home_ref[block], count)
        keep = row < rows_ref[lax.div(block, per_sector)]
        value = wave_ref[block]
        value = jnp.where(keep, value, jnp.zeros_like(value))
        out_ref[owner, 0:SHARE, :] = value[:, :LANES]
        out_ref[owner, SHARE : 2 * SHARE, :] = value[:, LANES:]
        return carry

    lax.fori_loop(0, count, put, 0)


def spread(depth, right_home, term_links, sector_rows, wavefunction, slots):
    count, _, width = wavefunction.shape
    return pl.pallas_call(
        functools.partial(spread_kernel, count),
        grid_spec=pltpu.PrefetchScalarGridSpec(
            num_scalar_prefetch=1,
            grid=(1,),
            in_specs=[
                SMEM,
                SMEM,
                SMEM,
                pl.BlockSpec((count, SHARE, width), lambda i, depth: (0, depth[0], 0)),
            ],
            out_specs=pl.BlockSpec((slots, 3 * SHARE, LANES), lambda i, depth: (0, 0, 0)),
            scratch_shapes=[pltpu.SMEM((1 + term_links.shape[0], slots), jnp.int32)],
        ),
        out_shape=pltpu.HBM((slots, 3 * SHARE, LANES), jnp.bfloat16),
        name="spread_blocks",
    )(depth, right_home, term_links, sector_rows, in_hbm(wavefunction))


def order_kernel(from_ref, links_ref, cols_ref, in_ref, out_ref):
    terms, count = links_ref.shape
    per_sector = count // cols_ref.shape[0]
    lane = lax.broadcasted_iota(jnp.int32, (SHARE, LANES), 1)
    targets = jnp.zeros(lane.shape, jnp.int32)
    for block in range(count):
        slot = from_ref[block]
        cols = cols_ref[block // per_sector]
        for part in range(2):
            value = in_ref[slot, part * SHARE : (part + 1) * SHARE, :]
            out_ref[block, part * SHARE : (part + 1) * SHARE, :] = jnp.where(
                lane + part * LANES < cols, value, jnp.zeros_like(value)
            )
        for term in range(terms):
            owner = lax.div(links_ref[term, block], count)
            targets = jnp.where(lane == term * count + block, owner, targets)
    targets = targets.astype(jnp.float32).astype(jnp.bfloat16)
    out_ref[count, 0:SHARE, :] = targets
    out_ref[count, SHARE:, :] = targets


def order(source, term_links, sector_cols, arrived):
    count = source.shape[0]
    return pl.pallas_call(
        order_kernel,
        in_specs=[SMEM, SMEM, SMEM, pl.BlockSpec(memory_space=pltpu.VMEM)],
        out_specs=pl.BlockSpec(memory_space=pltpu.VMEM),
        out_shape=jax.ShapeDtypeStruct((count + 1, 2 * SHARE, LANES), jnp.bfloat16),
        name="order_blocks",
    )(source, term_links, sector_cols, arrived)


def right_kernel(place_ref, targets_ref, slices_ref, *refs):
    envs, (out_ref, moved_ref, env_ref, slot_ref) = refs[:-4], refs[-4:]
    group, _, terms, extent, width = out_ref.shape
    sectors = env_ref.shape[0]
    depth, count = slices_ref.shape[0], slices_ref.shape[2] - 1
    per_sector = count // sectors
    turn = pl.program_id(0)
    for index in range(len(envs) // terms):

        @pl.when(turn == index)
        def _(index=index):
            for term in range(terms):
                env = envs[index * terms + term][0]
                env_ref[:, :, term * width : (term + 1) * width] = env

    for sector in range(sectors):
        half = sector % 2
        for share in range(depth):
            for place in range(per_sector):
                at = slice(place * extent + share * SHARE, place * extent + (share + 1) * SHARE)
                block = sector * per_sector + place
                moved_ref[half, at, 0:LANES] = slices_ref[share, 0, block, 0:SHARE, :]
                moved_ref[half, at, LANES:] = slices_ref[share, 0, block, SHARE:, :]
        product = jnp.dot(moved_ref[half], env_ref[sector], preferred_element_type=jnp.float32)
        product = product.astype(jnp.bfloat16)
        for place in range(per_sector):
            for term in range(terms):
                owner = targets_ref[turn, term * count + sector * per_sector + place]

                here = lax.div(owner, group) == place_ref[0]
                slot_ref[jnp.where(here, lax.rem(owner, group), group), term] = product[
                    place * extent : (place + 1) * extent, term * width : (term + 1) * width
                ]
    out_ref[:, 0] = slot_ref[:group]


def right_products(place, targets, slices, envs, group, chunk, width):
    depth, layers, blocks, tall, lanes = slices.shape
    terms = len(envs[0])
    sectors, extent = envs[0][0][0].shape[1:3]
    per_sector = (blocks - 1) // sectors
    flat = [pair for layer in envs for pair in layer]
    shape = (group, layers, terms, extent, width)
    return pl.pallas_call(
        right_kernel,
        grid_spec=pltpu.PrefetchScalarGridSpec(
            num_scalar_prefetch=2,
            grid=(layers,),
            in_specs=[pl.BlockSpec((depth, 1, blocks, tall, lanes), lambda i, p, t: (0, i, 0, 0, 0))]
            + [
                pl.BlockSpec(
                    (1, sectors, extent, width), lambda i, p, t, term=term: (term, 0, 0, chunk)
                )
                for _, term in flat
            ],
            out_specs=pl.BlockSpec((group, 1, terms, extent, width), lambda i, p, t: (0, i, 0, 0, 0)),
            scratch_shapes=[
                pltpu.VMEM((2, per_sector * extent, extent), jnp.bfloat16),
                pltpu.VMEM((sectors, extent, terms * width), jnp.bfloat16),
                pltpu.VMEM((group + 1, terms, extent, width), jnp.bfloat16),
            ],
        ),
        out_shape=pltpu.HBM(shape, jnp.bfloat16),
        compiler_params=pltpu.CompilerParams(vmem_limit_bytes=VMEM_LIMIT),
        name="right_products",
    )(place, targets, in_hbm(slices), *[array for array, _ in flat])


def far_products(place, targets, slices, above, below, across, group):
    envs = [
        [(above, 0), (above, 1)],
        [(across[0], 0), (across[1], 0)],
        [(below, 0), (below, 1)],
    ]
    return right_products(place, targets, slices, envs, group, 0, LANES)


def left_partials(place_ref, from_ref, near_ref, far_ref, env_ref, placed_ref):
    terms, count = from_ref.shape
    group, near, _, extent, width = near_ref.shape
    layers = near + far_ref.shape[1]
    per_sector = count // pl.num_programs(0)
    sector = pl.program_id(0)
    left = jnp.concatenate([env_ref[term, 0] for term in range(terms)], axis=1)
    for place in range(per_sector):
        for term in range(terms):
            device = from_ref[term, sector * per_sector + place]
            peer = lax.rem(device, group)
            step = lax.rem(lax.div(device, group) + layers - place_ref[0], layers)
            rows = slice(term * extent, (term + 1) * extent)
            columns = slice(place * width, (place + 1) * width)

            @pl.when(step < near)
            def _(term=term, peer=peer, step=step, rows=rows, columns=columns):
                placed_ref[rows, columns] = near_ref[peer, jnp.minimum(step, near - 1), term]

            @pl.when(step >= near)
            def _(term=term, peer=peer, step=step, rows=rows, columns=columns):
                placed_ref[rows, columns] = far_ref[peer, jnp.maximum(step - near, 0), term]

    partial = jnp.dot(left, placed_ref[...], preferred_element_type=jnp.float32)
    partial = partial.astype(jnp.bfloat16)
    for place in range(per_sector):
        yield place, partial[:, place * width : (place + 1) * width]


def left_kernel(place_ref, from_ref, near_ref, far_ref, env_ref, out_ref, placed_ref):
    for place, partial in left_partials(place_ref, from_ref, near_ref, far_ref, env_ref, placed_ref):
        out_ref[:, place] = partial.reshape(out_ref.shape[0], SHARE, partial.shape[1])


def left_split_kernel(place_ref, from_ref, near_ref, far_ref, env_ref, keep_ref, send_ref, placed_ref):
    chips = keep_ref.shape[0]
    core = place_ref[2]
    for place, partial in left_partials(place_ref, from_ref, near_ref, far_ref, env_ref, placed_ref):
        halves = [
            jnp.stack(
                [partial[(2 * c + k) * SHARE : (2 * c + k + 1) * SHARE] for c in range(chips)]
            )
            for k in range(2)
        ]
        keep_ref[:, place] = jnp.where(core == 0, halves[0], halves[1])
        send_ref[:, place] = jnp.where(core == 0, halves[1], halves[0])


def left_products(place, source, near, far, left_env, chunk, split):
    _, sectors, extent, _ = left_env.shape
    terms, count = source.shape
    width = far.shape[-1]
    per_sector = count // sectors
    pieces = extent // SHARE // (2 if split else 1)
    out_spec = pl.BlockSpec((pieces, per_sector, SHARE, width), lambda i: (0, i, 0, 0))
    shape = jax.ShapeDtypeStruct((pieces, count, SHARE, width), jnp.bfloat16)
    return pl.pallas_call(
        left_split_kernel if split else left_kernel,
        grid=(sectors,),
        in_specs=[
            SMEM,
            SMEM,
            pl.BlockSpec(near.shape[:-1] + (width,), lambda i: (0, 0, 0, 0, chunk)),
            pl.BlockSpec(far.shape, lambda i: (0, 0, 0, 0, 0)),
            pl.BlockSpec((terms, 1, extent, extent), lambda i: (0, i, 0, 0)),
        ],
        out_specs=[out_spec, out_spec] if split else out_spec,
        out_shape=[shape, shape] if split else shape,
        scratch_shapes=[pltpu.VMEM((terms * extent, per_sector * width), jnp.bfloat16)],
        compiler_params=pltpu.CompilerParams(vmem_limit_bytes=VMEM_LIMIT),
        name="left_products",
    )(place, source, near, far, left_env)


def shift(array, axis, step):
    size = lax.axis_size(axis)
    return lax.ppermute(array, axis, [(i, (i + step) % size) for i in range(size)])


def exchange(products):
    axes = ("zh", "zl", "x", "core")
    along_x, cores = lax.axis_size("x"), lax.axis_size("core")
    along_z = lax.axis_size("zh") * lax.axis_size("zl")
    groups = [
        [
            (((2 * pair + core + step) % along_z) * along_x + x) * cores + core
            for step in range(2)
            for x in range(along_x)
        ]
        for core in range(cores)
        for pair in range(along_z // 2)
    ]
    return lax.all_to_all(products, axes, 0, 0, axis_index_groups=groups, tiled=True)


def local(wavefunction, right_home, term_links, sector_rows, sector_cols, left_env, right_env):
    count, _, width = wavefunction.shape
    per_sector = count // sector_rows.shape[0]
    slots = lax.axis_size(REMAP)
    layers = lax.axis_size("zh")
    group = slots // layers
    terms = term_links.shape[0]
    layer = lax.axis_index("zh")
    core_index = lax.axis_index("core")
    depth_index = lax.axis_index("y") * 2 + core_index
    scheme_index = lax.rem(lax.axis_index(REMAP) + slots - core_index * (group // 2), slots)
    place = jnp.stack([scheme_index // group, lax.axis_index("y"), core_index])

    buffer = spread(depth_index.reshape(1), right_home, term_links, sector_rows, wavefunction, slots)
    arrived = lax.all_to_all(buffer, REMAP, 0, 0, tiled=True)
    parts = [right_env[..., at : at + LANES] for at in range(0, width, LANES)]
    above, below = shift(parts[0], "zh", -1), shift(parts[0], "zh", 1)
    arrived, above, below = lax.optimization_barrier((arrived, above, below))
    across = shift(above[:1], "zh", -1), shift(below[1:], "zh", 1)
    labels = arrived[:, 2 * SHARE, : 1 + terms].astype(jnp.int32)
    match = labels.T[:, None, :] == jnp.arange(count, dtype=jnp.int32)[None, :, None]
    source = jnp.sum(jnp.where(match, jnp.arange(slots, dtype=jnp.int32), 0), axis=2)
    moved_by = slots - core_index * (group // 2)
    peers = lax.rem(source[1:] + moved_by, slots)
    ordered = order(source[0], term_links, sector_cols, arrived)

    slices = lax.all_gather(ordered[None], DEPTH)
    around = lax.all_gather(ordered, "zh")
    around, second = lax.optimization_barrier((around, parts[1]))
    next_above, next_below = shift(second, "zh", -1), shift(second, "zh", 1)
    next_across = shift(next_above[:1], "zh", -1), shift(next_below[1:], "zh", 1)
    others = lax.dynamic_slice_in_dim(jnp.concatenate([around, around]), layer + 1, layers - 1)
    far_targets = others[:, count, 0, : terms * count].astype(jnp.int32)
    far_targets = lax.rem(far_targets + moved_by, slots)
    far_slices = lax.all_gather(others, DEPTH)

    targets = lax.rem((term_links // count).reshape(1, terms * count) + moved_by, slots)
    envs = [[(right_env, term) for term in range(terms)]]
    products = right_products(place, targets, slices, envs, group, 0, width)
    after = products, next_above, next_below
    products, next_above, next_below = lax.optimization_barrier(after)
    own = exchange(products)

    products = far_products(place, far_targets, far_slices, above, below, across, group)
    after = products, far_slices, next_across
    products, far_slices, next_across = lax.optimization_barrier(after)
    far = exchange(products)
    partial = left_products(place, peers, own, far, left_env, 0, False)
    partial = partial.reshape((-1, 2) + partial.shape[1:])
    summed = lax.psum_scatter(partial, "y", scatter_dimension=0, tiled=False)
    received = shift(lax.dynamic_index_in_dim(summed, 1 - core_index, 0, False), "core", 1)
    kept = lax.dynamic_index_in_dim(summed, core_index, 0, False)
    pieces = [kept.astype(jnp.float32) + received.astype(jnp.float32)]

    products = far_products(
        place, far_targets, far_slices, next_above, next_below, next_across, group
    )
    far = exchange(products)
    keep, send = left_products(place, peers, own, far, left_env, 1, True)
    pair = keep.astype(jnp.float32) + shift(send, "core", 1).astype(jnp.float32)
    shares = lax.all_to_all(pair.astype(jnp.bfloat16), "y", 0, 0, tiled=True)
    pieces.append(jnp.sum(shares.astype(jnp.float32), axis=0))
    total = jnp.concatenate(pieces, axis=2)
    row = depth_index * SHARE + jnp.arange(SHARE, dtype=jnp.int32)
    keep_rows = row[None, :] < jnp.repeat(sector_rows, per_sector)[:, None]
    return jnp.where(keep_rows[:, :, None], total, 0.0).astype(jnp.bfloat16)


def solution(mesh):
    slots, depth = mesh.devices.shape
    split = Mesh(
        mesh.devices.reshape(4, 2, slots // 8, depth // 2, 2), ("zh", "zl", "x", "y", "core")
    )
    return jax.shard_map(
        local,
        mesh=split,
        in_specs=(
            P(REMAP, None, None),
            P(REMAP),
            P(DEPTH, REMAP),
            P(REMAP),
            P(REMAP),
            P(DEPTH, REMAP, None, None),
            P(DEPTH, REMAP, None, None),
        ),
        out_specs=P(REMAP, DEPTH, None),
        check_vma=False,
    )
```

```python
import functools

import jax
import jax.numpy as jnp
from jax import lax
from jax.experimental import pallas as pl
from jax.experimental.pallas import tpu as pltpu
from jax.sharding import Mesh, PartitionSpec as P

SHARE = 16
LANES = 128
VMEM_LIMIT = 40 * 1024 * 1024
REMAP = ("zh", "zl", "x")
DEPTH = ("y", "core")
SMEM = pl.BlockSpec(memory_space=pltpu.SMEM)


def in_hbm(array):
    return pltpu.with_memory_space_constraint(array, pltpu.HBM)


def spread_kernel(count, depth_ref, home_ref, links_ref, rows_ref, wave_ref, out_ref, label_ref):
    slots = out_ref.shape[0]
    terms = links_ref.shape[0]
    per_sector = count // rows_ref.shape[0]

    def clear(peer, carry):
        for kind in range(1 + terms):
            label_ref[kind, peer] = count
        return carry

    lax.fori_loop(0, slots, clear, 0)

    def fill(block, carry):
        home = home_ref[block]
        label_ref[0, lax.div(home, count)] = lax.rem(home, count)
        for term in range(terms):
            link = links_ref[term, block]
            label_ref[1 + term, lax.div(link, count)] = lax.rem(link, count)
        return carry

    lax.fori_loop(0, count, fill, 0)
    lane = lax.broadcasted_iota(jnp.int32, (SHARE, LANES), 1)

    def mark(peer, carry):
        tile = jnp.full(lane.shape, label_ref[0, peer], jnp.int32)
        for term in range(terms):
            tile = jnp.where(lane == 1 + term, label_ref[1 + term, peer], tile)
        out_ref[peer, 2 * SHARE :, :] = tile.astype(jnp.float32).astype(jnp.bfloat16)
        return carry

    lax.fori_loop(0, slots, mark, 0)
    row = lax.broadcasted_iota(jnp.int32, wave_ref.shape[1:], 0) + depth_ref[0] * SHARE

    def put(block, carry):
        owner = lax.div(home_ref[block], count)
        keep = row < rows_ref[lax.div(block, per_sector)]
        value = wave_ref[block]
        value = jnp.where(keep, value, jnp.zeros_like(value))
        out_ref[owner, 0:SHARE, :] = value[:, :LANES]
        out_ref[owner, SHARE : 2 * SHARE, :] = value[:, LANES:]
        return carry

    lax.fori_loop(0, count, put, 0)


def spread(depth, right_home, term_links, sector_rows, wavefunction, slots):
    count, _, width = wavefunction.shape
    return pl.pallas_call(
        functools.partial(spread_kernel, count),
        grid_spec=pltpu.PrefetchScalarGridSpec(
            num_scalar_prefetch=1,
            grid=(1,),
            in_specs=[
                SMEM,
                SMEM,
                SMEM,
                pl.BlockSpec((count, SHARE, width), lambda i, depth: (0, depth[0], 0)),
            ],
            out_specs=pl.BlockSpec((slots, 3 * SHARE, LANES), lambda i, depth: (0, 0, 0)),
            scratch_shapes=[pltpu.SMEM((1 + term_links.shape[0], slots), jnp.int32)],
        ),
        out_shape=pltpu.HBM((slots, 3 * SHARE, LANES), jnp.bfloat16),
        name="spread_blocks",
    )(depth, right_home, term_links, sector_rows, in_hbm(wavefunction))


def order_kernel(from_ref, links_ref, cols_ref, in_ref, out_ref):
    terms, count = links_ref.shape
    per_sector = count // cols_ref.shape[0]
    lane = lax.broadcasted_iota(jnp.int32, (SHARE, LANES), 1)
    targets = jnp.zeros(lane.shape, jnp.int32)
    for block in range(count):
        slot = from_ref[block]
        cols = cols_ref[block // per_sector]
        for part in range(2):
            value = in_ref[slot, part * SHARE : (part + 1) * SHARE, :]
            out_ref[block, part * SHARE : (part + 1) * SHARE, :] = jnp.where(
                lane + part * LANES < cols, value, jnp.zeros_like(value)
            )
        for term in range(terms):
            owner = lax.div(links_ref[term, block], count)
            targets = jnp.where(lane == term * count + block, owner, targets)
    targets = targets.astype(jnp.float32).astype(jnp.bfloat16)
    out_ref[count, 0:SHARE, :] = targets
    out_ref[count, SHARE:, :] = targets


def order(source, term_links, sector_cols, arrived):
    count = source.shape[0]
    return pl.pallas_call(
        order_kernel,
        in_specs=[SMEM, SMEM, SMEM, pl.BlockSpec(memory_space=pltpu.VMEM)],
        out_specs=pl.BlockSpec(memory_space=pltpu.VMEM),
        out_shape=jax.ShapeDtypeStruct((count + 1, 2 * SHARE, LANES), jnp.bfloat16),
        name="order_blocks",
    )(source, term_links, sector_cols, arrived)


def right_kernel(place_ref, targets_ref, slices_ref, *refs):
    envs, (out_ref, moved_ref, env_ref, slot_ref) = refs[:-4], refs[-4:]
    group, _, terms, extent, width = out_ref.shape
    sectors = env_ref.shape[0]
    depth, count = slices_ref.shape[0], slices_ref.shape[2] - 1
    per_sector = count // sectors
    turn = pl.program_id(0)
    for index in range(len(envs) // terms):

        @pl.when(turn == index)
        def _(index=index):
            for term in range(terms):
                env = envs[index * terms + term][0]
                env_ref[:, :, term * width : (term + 1) * width] = env

    for sector in range(sectors):
        half = sector % 2
        for share in range(depth):
            for place in range(per_sector):
                at = slice(place * extent + share * SHARE, place * extent + (share + 1) * SHARE)
                block = sector * per_sector + place
                moved_ref[half, at, 0:LANES] = slices_ref[share, 0, block, 0:SHARE, :]
                moved_ref[half, at, LANES:] = slices_ref[share, 0, block, SHARE:, :]
        product = jnp.dot(moved_ref[half], env_ref[sector], preferred_element_type=jnp.float32)
        product = product.astype(jnp.bfloat16)
        for place in range(per_sector):
            for term in range(terms):
                owner = targets_ref[turn, term * count + sector * per_sector + place]

                here = lax.div(owner, group) == place_ref[0]
                slot_ref[jnp.where(here, lax.rem(owner, group), group), term] = product[
                    place * extent : (place + 1) * extent, term * width : (term + 1) * width
                ]
    out_ref[:, 0] = slot_ref[:group]


def right_products(place, targets, slices, envs, group, chunk, width):
    depth, layers, blocks, tall, lanes = slices.shape
    terms = len(envs[0])
    sectors, extent = envs[0][0][0].shape[1:3]
    per_sector = (blocks - 1) // sectors
    flat = [pair for layer in envs for pair in layer]
    shape = (group, layers, terms, extent, width)
    return pl.pallas_call(
        right_kernel,
        grid_spec=pltpu.PrefetchScalarGridSpec(
            num_scalar_prefetch=2,
            grid=(layers,),
            in_specs=[pl.BlockSpec((depth, 1, blocks, tall, lanes), lambda i, p, t: (0, i, 0, 0, 0))]
            + [
                pl.BlockSpec(
                    (1, sectors, extent, width), lambda i, p, t, term=term: (term, 0, 0, chunk)
                )
                for _, term in flat
            ],
            out_specs=pl.BlockSpec((group, 1, terms, extent, width), lambda i, p, t: (0, i, 0, 0, 0)),
            scratch_shapes=[
                pltpu.VMEM((2, per_sector * extent, extent), jnp.bfloat16),
                pltpu.VMEM((sectors, extent, terms * width), jnp.bfloat16),
                pltpu.VMEM((group + 1, terms, extent, width), jnp.bfloat16),
            ],
        ),
        out_shape=pltpu.HBM(shape, jnp.bfloat16),
        compiler_params=pltpu.CompilerParams(vmem_limit_bytes=VMEM_LIMIT),
        name="right_products",
    )(place, targets, in_hbm(slices), *[array for array, _ in flat])


def left_partials(place_ref, from_ref, near_ref, far_ref, env_ref, placed_ref):
    terms, count = from_ref.shape
    group, near, _, extent, width = near_ref.shape
    layers = near + far_ref.shape[1]
    per_sector = count // pl.num_programs(0)
    sector = pl.program_id(0)
    left = jnp.concatenate([env_ref[term, 0] for term in range(terms)], axis=1)
    for place in range(per_sector):
        for term in range(terms):
            device = from_ref[term, sector * per_sector + place]
            peer = lax.rem(device, group)
            step = lax.rem(lax.div(device, group) + layers - place_ref[0], layers)
            rows = slice(term * extent, (term + 1) * extent)
            columns = slice(place * width, (place + 1) * width)

            @pl.when(step < near)
            def _(term=term, peer=peer, step=step, rows=rows, columns=columns):
                placed_ref[rows, columns] = near_ref[peer, jnp.minimum(step, near - 1), term]

            @pl.when(step >= near)
            def _(term=term, peer=peer, step=step, rows=rows, columns=columns):
                placed_ref[rows, columns] = far_ref[peer, jnp.maximum(step - near, 0), term]

    partial = jnp.dot(left, placed_ref[...], preferred_element_type=jnp.float32)
    partial = partial.astype(jnp.bfloat16)
    for place in range(per_sector):
        yield place, partial[:, place * width : (place + 1) * width]


def left_kernel(place_ref, from_ref, near_ref, far_ref, env_ref, out_ref, placed_ref):
    for place, partial in left_partials(place_ref, from_ref, near_ref, far_ref, env_ref, placed_ref):
        out_ref[:, place] = partial.reshape(out_ref.shape[0], SHARE, partial.shape[1])


def left_split_kernel(place_ref, from_ref, near_ref, far_ref, env_ref, keep_ref, send_ref, placed_ref):
    chips = keep_ref.shape[0]
    core = place_ref[2]
    for place, partial in left_partials(place_ref, from_ref, near_ref, far_ref, env_ref, placed_ref):
        halves = [
            jnp.stack(
                [partial[(2 * c + k) * SHARE : (2 * c + k + 1) * SHARE] for c in range(chips)]
            )
            for k in range(2)
        ]
        keep_ref[:, place] = jnp.where(core == 0, halves[0], halves[1])
        send_ref[:, place] = jnp.where(core == 0, halves[1], halves[0])


def left_products(place, source, near, far, left_env, chunk, split):
    _, sectors, extent, _ = left_env.shape
    terms, count = source.shape
    width = far.shape[-1]
    per_sector = count // sectors
    pieces = extent // SHARE // (2 if split else 1)
    out_spec = pl.BlockSpec((pieces, per_sector, SHARE, width), lambda i: (0, i, 0, 0))
    shape = jax.ShapeDtypeStruct((pieces, count, SHARE, width), jnp.bfloat16)
    return pl.pallas_call(
        left_split_kernel if split else left_kernel,
        grid=(sectors,),
        in_specs=[
            SMEM,
            SMEM,
            pl.BlockSpec(near.shape[:-1] + (width,), lambda i: (0, 0, 0, 0, chunk)),
            pl.BlockSpec(far.shape, lambda i: (0, 0, 0, 0, 0)),
            pl.BlockSpec((terms, 1, extent, extent), lambda i: (0, i, 0, 0)),
        ],
        out_specs=[out_spec, out_spec] if split else out_spec,
        out_shape=[shape, shape] if split else shape,
        scratch_shapes=[pltpu.VMEM((terms * extent, per_sector * width), jnp.bfloat16)],
        compiler_params=pltpu.CompilerParams(vmem_limit_bytes=VMEM_LIMIT),
        name="left_products",
    )(place, source, near, far, left_env)


def shift(array, axis, step):
    size = lax.axis_size(axis)
    return lax.ppermute(array, axis, [(i, (i + step) % size) for i in range(size)])


def exchange(products):
    axes = ("zh", "zl", "x", "core")
    along_x, cores = lax.axis_size("x"), lax.axis_size("core")
    along_z = lax.axis_size("zh") * lax.axis_size("zl")
    groups = [
        [
            (((2 * pair + core + step) % along_z) * along_x + x) * cores + core
            for step in range(2)
            for x in range(along_x)
        ]
        for core in range(cores)
        for pair in range(along_z // 2)
    ]
    return lax.all_to_all(products, axes, 0, 0, axis_index_groups=groups, tiled=True)


def local(wavefunction, right_home, term_links, sector_rows, sector_cols, left_env, right_env):
    count, _, width = wavefunction.shape
    per_sector = count // sector_rows.shape[0]
    slots = lax.axis_size(REMAP)
    layers = lax.axis_size("zh")
    group = slots // layers
    terms = term_links.shape[0]
    layer = lax.axis_index("zh")
    core_index = lax.axis_index("core")
    depth_index = lax.axis_index("y") * 2 + core_index
    scheme_index = lax.rem(lax.axis_index(REMAP) + slots - core_index * (group // 2), slots)
    place = jnp.stack([scheme_index // group, lax.axis_index("y"), core_index])

    buffer = spread(depth_index.reshape(1), right_home, term_links, sector_rows, wavefunction, slots)
    arrived = lax.all_to_all(buffer, REMAP, 0, 0, tiled=True)
    first, second = right_env[..., :LANES], right_env[..., LANES:]
    early, rest = first[:1], jnp.concatenate([first[1:], second])
    above, below = shift(early, "zh", -1), shift(early, "zh", 1)
    arrived, above, below = lax.optimization_barrier((arrived, above, below))
    labels = arrived[:, 2 * SHARE, : 1 + terms].astype(jnp.int32)
    match = labels.T[:, None, :] == jnp.arange(count, dtype=jnp.int32)[None, :, None]
    source = jnp.sum(jnp.where(match, jnp.arange(slots, dtype=jnp.int32), 0), axis=2)
    moved_by = slots - core_index * (group // 2)
    peers = lax.rem(source[1:] + moved_by, slots)
    ordered = order(source[0], term_links, sector_cols, arrived)

    slices = lax.all_gather(ordered[None], DEPTH)
    around = lax.all_gather(ordered, "zh")
    around, rest = lax.optimization_barrier((around, rest))
    rest_above, rest_below = shift(rest, "zh", -1), shift(rest, "zh", 1)
    across = (
        shift(jnp.concatenate([above, rest_above[1:2]]), "zh", -1),
        shift(jnp.concatenate([rest_below[:1], rest_below[2:]]), "zh", 1),
    )
    others = lax.dynamic_slice_in_dim(jnp.concatenate([around, around]), layer + 1, layers - 1)
    far_targets = others[:, count, 0, : terms * count].astype(jnp.int32)
    far_targets = lax.rem(far_targets + moved_by, slots)
    far_slices = lax.all_gather(others, DEPTH)

    targets = lax.rem((term_links // count).reshape(1, terms * count) + moved_by, slots)
    envs = [[(right_env, term) for term in range(terms)]]
    products = right_products(place, targets, slices, envs, group, 0, width)
    after = products, rest_above, rest_below
    products, rest_above, rest_below = lax.optimization_barrier(after)
    own = exchange(products)

    envs = [
        [(above, 0), (rest_above, 0)],
        [(across[0], 0), (across[1], 0)],
        [(below, 0), (rest_below, 0)],
    ]
    products = right_products(place, far_targets, far_slices, envs, group, 0, LANES)
    far_slices, products = lax.optimization_barrier((far_slices, products))
    far = exchange(products)
    partial = left_products(place, peers, own, far, left_env, 0, False)
    partial = partial.reshape((-1, 2) + partial.shape[1:])
    summed = lax.psum_scatter(partial, "y", scatter_dimension=0, tiled=False)
    received = shift(lax.dynamic_index_in_dim(summed, 1 - core_index, 0, False), "core", 1)
    kept = lax.dynamic_index_in_dim(summed, core_index, 0, False)
    pieces = [kept.astype(jnp.float32) + received.astype(jnp.float32)]

    envs = [
        [(rest_above, 1), (rest_above, 2)],
        [(across[0], 1), (across[1], 1)],
        [(rest_below, 1), (rest_below, 2)],
    ]
    products = right_products(place, far_targets, far_slices, envs, group, 0, LANES)
    far = exchange(products)
    keep, send = left_products(place, peers, own, far, left_env, 1, True)
    pair = keep.astype(jnp.float32) + shift(send, "core", 1).astype(jnp.float32)
    shares = lax.all_to_all(pair.astype(jnp.bfloat16), "y", 0, 0, tiled=True)
    pieces.append(jnp.sum(shares.astype(jnp.float32), axis=0))
    total = jnp.concatenate(pieces, axis=2)
    row = depth_index * SHARE + jnp.arange(SHARE, dtype=jnp.int32)
    keep_rows = row[None, :] < jnp.repeat(sector_rows, per_sector)[:, None]
    return jnp.where(keep_rows[:, :, None], total, 0.0).astype(jnp.bfloat16)


def solution(mesh):
    slots, depth = mesh.devices.shape
    split = Mesh(
        mesh.devices.reshape(4, 2, slots // 8, depth // 2, 2), ("zh", "zl", "x", "y", "core")
    )
    return jax.shard_map(
        local,
        mesh=split,
        in_specs=(
            P(REMAP, None, None),
            P(REMAP),
            P(DEPTH, REMAP),
            P(REMAP),
            P(REMAP),
            P(DEPTH, REMAP, None, None),
            P(DEPTH, REMAP, None, None),
        ),
        out_specs=P(REMAP, DEPTH, None),
        check_vma=False,
    )
```

```python
import functools

import jax
import jax.numpy as jnp
from jax import lax
from jax.experimental import pallas as pl
from jax.experimental.pallas import tpu as pltpu
from jax.sharding import Mesh, PartitionSpec as P

SHARE = 16
LANES = 128
VMEM_LIMIT = 40 * 1024 * 1024
REMAP = ("zh", "zl", "x")
DEPTH = ("y", "core")
SMEM = pl.BlockSpec(memory_space=pltpu.SMEM)


def in_hbm(array):
    return pltpu.with_memory_space_constraint(array, pltpu.HBM)


def spread_kernel(count, depth_ref, home_ref, links_ref, rows_ref, wave_ref, out_ref, label_ref):
    slots = out_ref.shape[0]
    terms = links_ref.shape[0]
    per_sector = count // rows_ref.shape[0]

    def clear(peer, carry):
        for kind in range(1 + terms):
            label_ref[kind, peer] = count
        return carry

    lax.fori_loop(0, slots, clear, 0)

    def fill(block, carry):
        home = home_ref[block]
        label_ref[0, lax.div(home, count)] = lax.rem(home, count)
        for term in range(terms):
            link = links_ref[term, block]
            label_ref[1 + term, lax.div(link, count)] = lax.rem(link, count)
        return carry

    lax.fori_loop(0, count, fill, 0)
    lane = lax.broadcasted_iota(jnp.int32, (SHARE, LANES), 1)

    def mark(peer, carry):
        tile = jnp.full(lane.shape, label_ref[0, peer], jnp.int32)
        for term in range(terms):
            tile = jnp.where(lane == 1 + term, label_ref[1 + term, peer], tile)
        out_ref[peer, 2 * SHARE :, :] = tile.astype(jnp.float32).astype(jnp.bfloat16)
        return carry

    lax.fori_loop(0, slots, mark, 0)
    row = lax.broadcasted_iota(jnp.int32, wave_ref.shape[1:], 0) + depth_ref[0] * SHARE

    def put(block, carry):
        owner = lax.div(home_ref[block], count)
        keep = row < rows_ref[lax.div(block, per_sector)]
        value = wave_ref[block]
        value = jnp.where(keep, value, jnp.zeros_like(value))
        out_ref[owner, 0:SHARE, :] = value[:, :LANES]
        out_ref[owner, SHARE : 2 * SHARE, :] = value[:, LANES:]
        return carry

    lax.fori_loop(0, count, put, 0)


def spread(depth, right_home, term_links, sector_rows, wavefunction, slots):
    count, _, width = wavefunction.shape
    return pl.pallas_call(
        functools.partial(spread_kernel, count),
        grid_spec=pltpu.PrefetchScalarGridSpec(
            num_scalar_prefetch=1,
            grid=(1,),
            in_specs=[
                SMEM,
                SMEM,
                SMEM,
                pl.BlockSpec((count, SHARE, width), lambda i, depth: (0, depth[0], 0)),
            ],
            out_specs=pl.BlockSpec((slots, 3 * SHARE, LANES), lambda i, depth: (0, 0, 0)),
            scratch_shapes=[pltpu.SMEM((1 + term_links.shape[0], slots), jnp.int32)],
        ),
        out_shape=pltpu.HBM((slots, 3 * SHARE, LANES), jnp.bfloat16),
        name="spread_blocks",
    )(depth, right_home, term_links, sector_rows, in_hbm(wavefunction))


def order_kernel(from_ref, links_ref, cols_ref, in_ref, out_ref):
    terms, count = links_ref.shape
    per_sector = count // cols_ref.shape[0]
    lane = lax.broadcasted_iota(jnp.int32, (SHARE, LANES), 1)
    targets = jnp.zeros(lane.shape, jnp.int32)
    for block in range(count):
        slot = from_ref[block]
        cols = cols_ref[block // per_sector]
        for part in range(2):
            value = in_ref[slot, part * SHARE : (part + 1) * SHARE, :]
            out_ref[block, part * SHARE : (part + 1) * SHARE, :] = jnp.where(
                lane + part * LANES < cols, value, jnp.zeros_like(value)
            )
        for term in range(terms):
            owner = lax.div(links_ref[term, block], count)
            targets = jnp.where(lane == term * count + block, owner, targets)
    targets = targets.astype(jnp.float32).astype(jnp.bfloat16)
    out_ref[count, 0:SHARE, :] = targets
    out_ref[count, SHARE:, :] = targets


def order(source, term_links, sector_cols, arrived):
    count = source.shape[0]
    return pl.pallas_call(
        order_kernel,
        in_specs=[SMEM, SMEM, SMEM, pl.BlockSpec(memory_space=pltpu.VMEM)],
        out_specs=pl.BlockSpec(memory_space=pltpu.VMEM),
        out_shape=jax.ShapeDtypeStruct((count + 1, 2 * SHARE, LANES), jnp.bfloat16),
        name="order_blocks",
    )(source, term_links, sector_cols, arrived)


def right_kernel(aliased, place_ref, targets_ref, slices_ref, *refs):
    envs, (out_ref, moved_ref, env_ref, slot_ref) = refs[: -4 - aliased], refs[-4:]
    group, _, terms, extent, width = out_ref.shape
    sectors = env_ref.shape[0]
    depth, count = slices_ref.shape[0], slices_ref.shape[2] - 1
    per_sector = count // sectors
    turn = pl.program_id(0)
    for index in range(len(envs) // terms):

        @pl.when(turn == index)
        def _(index=index):
            for term in range(terms):
                env = envs[index * terms + term][0]
                env_ref[:, :, term * width : (term + 1) * width] = env

    for sector in range(sectors):
        half = sector % 2
        for share in range(depth):
            for place in range(per_sector):
                at = slice(place * extent + share * SHARE, place * extent + (share + 1) * SHARE)
                block = sector * per_sector + place
                moved_ref[half, at, 0:LANES] = slices_ref[share, 0, block, 0:SHARE, :]
                moved_ref[half, at, LANES:] = slices_ref[share, 0, block, SHARE:, :]
        product = jnp.dot(moved_ref[half], env_ref[sector], preferred_element_type=jnp.float32)
        product = product.astype(jnp.bfloat16)
        for place in range(per_sector):
            for term in range(terms):
                owner = targets_ref[turn, term * count + sector * per_sector + place]

                here = lax.div(owner, group) == place_ref[0]
                slot_ref[jnp.where(here, lax.rem(owner, group), group), term] = product[
                    place * extent : (place + 1) * extent, term * width : (term + 1) * width
                ]
    out_ref[:, 0] = slot_ref[:group]


def right_products(place, targets, slices, envs, group, width, first=0, stride=1, into=None):
    depth, layers, blocks, tall, lanes = slices.shape
    terms = len(envs[0])
    sectors, extent = envs[0][0][0].shape[1:3]
    per_sector = (blocks - 1) // sectors
    flat = [pair for layer in envs for pair in layer]
    extra = [] if into is None else [into]
    return pl.pallas_call(
        functools.partial(right_kernel, len(extra)),
        grid_spec=pltpu.PrefetchScalarGridSpec(
            num_scalar_prefetch=2,
            grid=(len(envs),),
            in_specs=[
                pl.BlockSpec(
                    (depth, 1, blocks, tall, lanes),
                    lambda i, p, t: (0, first + stride * i, 0, 0, 0),
                )
            ]
            + [
                pl.BlockSpec((1, sectors, extent, width), lambda i, p, t, term=term: (term, 0, 0, 0))
                for _, term in flat
            ]
            + [pl.BlockSpec(memory_space=pl.ANY)] * len(extra),
            out_specs=pl.BlockSpec(
                (group, 1, terms, extent, width), lambda i, p, t: (0, first + stride * i, 0, 0, 0)
            ),
            scratch_shapes=[
                pltpu.VMEM((2, per_sector * extent, extent), jnp.bfloat16),
                pltpu.VMEM((sectors, extent, terms * width), jnp.bfloat16),
                pltpu.VMEM((group + 1, terms, extent, width), jnp.bfloat16),
            ],
        ),
        out_shape=pltpu.HBM((group, layers, terms, extent, width), jnp.bfloat16),
        input_output_aliases={3 + len(flat): 0} if extra else {},
        compiler_params=pltpu.CompilerParams(vmem_limit_bytes=VMEM_LIMIT),
        name="right_products",
    )(place, targets, in_hbm(slices), *[array for array, _ in flat], *extra)


def left_partials(place_ref, from_ref, near_ref, far_ref, env_ref, placed_ref):
    terms, count = from_ref.shape
    group, near, _, extent, width = near_ref.shape
    layers = near + far_ref.shape[1]
    per_sector = count // pl.num_programs(0)
    sector = pl.program_id(0)
    left = jnp.concatenate([env_ref[term, 0] for term in range(terms)], axis=1)
    for place in range(per_sector):
        for term in range(terms):
            device = from_ref[term, sector * per_sector + place]
            peer = lax.rem(device, group)
            step = lax.rem(lax.div(device, group) + layers - place_ref[0], layers)
            rows = slice(term * extent, (term + 1) * extent)
            columns = slice(place * width, (place + 1) * width)

            @pl.when(step < near)
            def _(term=term, peer=peer, step=step, rows=rows, columns=columns):
                placed_ref[rows, columns] = near_ref[peer, jnp.minimum(step, near - 1), term]

            @pl.when(step >= near)
            def _(term=term, peer=peer, step=step, rows=rows, columns=columns):
                placed_ref[rows, columns] = far_ref[peer, jnp.maximum(step - near, 0), term]

    partial = jnp.dot(left, placed_ref[...], preferred_element_type=jnp.float32)
    partial = partial.astype(jnp.bfloat16)
    for place in range(per_sector):
        yield place, partial[:, place * width : (place + 1) * width]


def left_kernel(place_ref, from_ref, near_ref, far_ref, env_ref, out_ref, placed_ref):
    for place, partial in left_partials(place_ref, from_ref, near_ref, far_ref, env_ref, placed_ref):
        out_ref[:, place] = partial.reshape(out_ref.shape[0], SHARE, partial.shape[1])


def left_split_kernel(place_ref, from_ref, near_ref, far_ref, env_ref, keep_ref, send_ref, placed_ref):
    chips = keep_ref.shape[0]
    core = place_ref[2]
    for place, partial in left_partials(place_ref, from_ref, near_ref, far_ref, env_ref, placed_ref):
        halves = [
            jnp.stack(
                [partial[(2 * c + k) * SHARE : (2 * c + k + 1) * SHARE] for c in range(chips)]
            )
            for k in range(2)
        ]
        keep_ref[:, place] = jnp.where(core == 0, halves[0], halves[1])
        send_ref[:, place] = jnp.where(core == 0, halves[1], halves[0])


def left_products(place, source, near, far, left_env, chunk, split):
    _, sectors, extent, _ = left_env.shape
    terms, count = source.shape
    width = far.shape[-1]
    per_sector = count // sectors
    pieces = extent // SHARE // (2 if split else 1)
    out_spec = pl.BlockSpec((pieces, per_sector, SHARE, width), lambda i: (0, i, 0, 0))
    shape = jax.ShapeDtypeStruct((pieces, count, SHARE, width), jnp.bfloat16)
    return pl.pallas_call(
        left_split_kernel if split else left_kernel,
        grid=(sectors,),
        in_specs=[
            SMEM,
            SMEM,
            pl.BlockSpec(near.shape[:-1] + (width,), lambda i: (0, 0, 0, 0, chunk)),
            pl.BlockSpec(far.shape, lambda i: (0, 0, 0, 0, 0)),
            pl.BlockSpec((terms, 1, extent, extent), lambda i: (0, i, 0, 0)),
        ],
        out_specs=[out_spec, out_spec] if split else out_spec,
        out_shape=[shape, shape] if split else shape,
        scratch_shapes=[pltpu.VMEM((terms * extent, per_sector * width), jnp.bfloat16)],
        compiler_params=pltpu.CompilerParams(vmem_limit_bytes=VMEM_LIMIT),
        name="left_products",
    )(place, source, near, far, left_env)


def shift(array, axis, step):
    size = lax.axis_size(axis)
    return lax.ppermute(array, axis, [(i, (i + step) % size) for i in range(size)])


def exchange(products):
    axes = ("zh", "zl", "x", "core")
    along_x, cores = lax.axis_size("x"), lax.axis_size("core")
    along_z = lax.axis_size("zh") * lax.axis_size("zl")
    groups = [
        [
            (((2 * pair + core + step) % along_z) * along_x + x) * cores + core
            for step in range(2)
            for x in range(along_x)
        ]
        for core in range(cores)
        for pair in range(along_z // 2)
    ]
    return lax.all_to_all(products, axes, 0, 0, axis_index_groups=groups, tiled=True)


def local(wavefunction, right_home, term_links, sector_rows, sector_cols, left_env, right_env):
    count, _, width = wavefunction.shape
    per_sector = count // sector_rows.shape[0]
    slots = lax.axis_size(REMAP)
    layers = lax.axis_size("zh")
    group = slots // layers
    terms = term_links.shape[0]
    layer = lax.axis_index("zh")
    core_index = lax.axis_index("core")
    depth_index = lax.axis_index("y") * 2 + core_index
    scheme_index = lax.rem(lax.axis_index(REMAP) + slots - core_index * (group // 2), slots)
    place = jnp.stack([scheme_index // group, lax.axis_index("y"), core_index])

    buffer = spread(depth_index.reshape(1), right_home, term_links, sector_rows, wavefunction, slots)
    arrived = lax.all_to_all(buffer, REMAP, 0, 0, tiled=True)
    labels = arrived[:, 2 * SHARE, : 1 + terms].astype(jnp.int32)
    match = labels.T[:, None, :] == jnp.arange(count, dtype=jnp.int32)[None, :, None]
    source = jnp.sum(jnp.where(match, jnp.arange(slots, dtype=jnp.int32), 0), axis=2)
    moved_by = slots - core_index * (group // 2)
    peers = lax.rem(source[1:] + moved_by, slots)
    ordered = order(source[0], term_links, sector_cols, arrived)

    parts = [right_env[..., at : at + LANES] for at in range(0, width, LANES)]
    above, below = shift(parts[0], "zh", -1), shift(parts[0], "zh", 1)
    across = shift(above[:1], "zh", -1), shift(below[1:], "zh", 1)

    slices = lax.all_gather(ordered[None], DEPTH)
    around = lax.all_gather(ordered, "zh")
    others = lax.dynamic_slice_in_dim(jnp.concatenate([around, around]), layer + 1, layers - 1)
    far_targets = others[:, count, 0, : terms * count].astype(jnp.int32)
    far_targets = lax.rem(far_targets + moved_by, slots)
    far_slices = lax.all_gather(others, DEPTH)

    targets = lax.rem((term_links // count).reshape(1, terms * count) + moved_by, slots)
    envs = [[(right_env, term) for term in range(terms)]]
    products = right_products(place, targets, slices, envs, group, width)
    products, above, below = lax.optimization_barrier((products, above, below))
    own = exchange(products)

    across, second = lax.optimization_barrier((across, parts[1]))
    next_above, next_below = shift(second, "zh", -1), shift(second, "zh", 1)
    next_across = shift(next_above[:1], "zh", -1), shift(next_below[1:], "zh", 1)

    envs = [
        [(above, 0), (above, 1)],
        [(across[0], 0), (across[1], 0)],
        [(below, 0), (below, 1)],
    ]
    products = right_products(place, far_targets, far_slices, envs, group, LANES)
    after = products, far_slices, next_above, next_below
    products, far_slices, next_above, next_below = lax.optimization_barrier(after)
    far = exchange(products)
    partial = left_products(place, peers, own, far, left_env, 0, False)
    partial = partial.reshape((-1, 2) + partial.shape[1:])
    summed = lax.psum_scatter(partial, "y", scatter_dimension=0, tiled=False)
    received = shift(lax.dynamic_index_in_dim(summed, 1 - core_index, 0, False), "core", 1)
    kept = lax.dynamic_index_in_dim(summed, core_index, 0, False)
    pieces = [kept.astype(jnp.float32) + received.astype(jnp.float32)]

    sides = jnp.stack([far_targets[0], far_targets[2]])
    envs = [[(next_above, 0), (next_above, 1)], [(next_below, 0), (next_below, 1)]]
    products = right_products(place, sides, far_slices, envs, group, LANES, 0, 2)
    envs = [[(next_across[0], 0), (next_across[1], 0)]]
    products = right_products(
        place, far_targets[1:2], far_slices, envs, group, LANES, 1, 1, products
    )
    far = exchange(products)
    keep, send = left_products(place, peers, own, far, left_env, 1, True)
    pair = keep.astype(jnp.float32) + shift(send, "core", 1).astype(jnp.float32)
    shares = lax.all_to_all(pair.astype(jnp.bfloat16), "y", 0, 0, tiled=True)
    pieces.append(jnp.sum(shares.astype(jnp.float32), axis=0))
    total = jnp.concatenate(pieces, axis=2)
    row = depth_index * SHARE + jnp.arange(SHARE, dtype=jnp.int32)
    keep_rows = row[None, :] < jnp.repeat(sector_rows, per_sector)[:, None]
    return jnp.where(keep_rows[:, :, None], total, 0.0).astype(jnp.bfloat16)


def solution(mesh):
    slots, depth = mesh.devices.shape
    split = Mesh(
        mesh.devices.reshape(4, 2, slots // 8, depth // 2, 2), ("zh", "zl", "x", "y", "core")
    )
    return jax.shard_map(
        local,
        mesh=split,
        in_specs=(
            P(REMAP, None, None),
            P(REMAP),
            P(DEPTH, REMAP),
            P(REMAP),
            P(REMAP),
            P(DEPTH, REMAP, None, None),
            P(DEPTH, REMAP, None, None),
        ),
        out_specs=P(REMAP, DEPTH, None),
        check_vma=False,
    )
```

```python
import functools

import jax
import jax.numpy as jnp
from jax import lax
from jax.experimental import pallas as pl
from jax.experimental.pallas import tpu as pltpu
from jax.sharding import Mesh, PartitionSpec as P

SHARE = 16
LANES = 128
VMEM_LIMIT = 40 * 1024 * 1024
REMAP = ("zh", "zl", "x")
DEPTH = ("y", "core")
SMEM = pl.BlockSpec(memory_space=pltpu.SMEM)


def in_hbm(array):
    return pltpu.with_memory_space_constraint(array, pltpu.HBM)


def spread_kernel(count, depth_ref, home_ref, links_ref, rows_ref, wave_ref, out_ref, label_ref):
    slots = out_ref.shape[0]
    terms = links_ref.shape[0]
    per_sector = count // rows_ref.shape[0]

    def clear(peer, carry):
        for kind in range(1 + terms):
            label_ref[kind, peer] = count
        return carry

    lax.fori_loop(0, slots, clear, 0)

    def fill(block, carry):
        home = home_ref[block]
        label_ref[0, lax.div(home, count)] = lax.rem(home, count)
        for term in range(terms):
            link = links_ref[term, block]
            label_ref[1 + term, lax.div(link, count)] = lax.rem(link, count)
        return carry

    lax.fori_loop(0, count, fill, 0)
    lane = lax.broadcasted_iota(jnp.int32, (SHARE, LANES), 1)

    def mark(peer, carry):
        tile = jnp.full(lane.shape, label_ref[0, peer], jnp.int32)
        for term in range(terms):
            tile = jnp.where(lane == 1 + term, label_ref[1 + term, peer], tile)
        out_ref[peer, 2 * SHARE :, :] = tile.astype(jnp.float32).astype(jnp.bfloat16)
        return carry

    lax.fori_loop(0, slots, mark, 0)
    row = lax.broadcasted_iota(jnp.int32, wave_ref.shape[1:], 0) + depth_ref[0] * SHARE

    def put(block, carry):
        owner = lax.div(home_ref[block], count)
        keep = row < rows_ref[lax.div(block, per_sector)]
        value = wave_ref[block]
        value = jnp.where(keep, value, jnp.zeros_like(value))
        out_ref[owner, 0:SHARE, :] = value[:, :LANES]
        out_ref[owner, SHARE : 2 * SHARE, :] = value[:, LANES:]
        return carry

    lax.fori_loop(0, count, put, 0)


def spread(depth, right_home, term_links, sector_rows, wavefunction, slots):
    count, _, width = wavefunction.shape
    return pl.pallas_call(
        functools.partial(spread_kernel, count),
        grid_spec=pltpu.PrefetchScalarGridSpec(
            num_scalar_prefetch=1,
            grid=(1,),
            in_specs=[
                SMEM,
                SMEM,
                SMEM,
                pl.BlockSpec((count, SHARE, width), lambda i, depth: (0, depth[0], 0)),
            ],
            out_specs=pl.BlockSpec((slots, 3 * SHARE, LANES), lambda i, depth: (0, 0, 0)),
            scratch_shapes=[pltpu.SMEM((1 + term_links.shape[0], slots), jnp.int32)],
        ),
        out_shape=pltpu.HBM((slots, 3 * SHARE, LANES), jnp.bfloat16),
        name="spread_blocks",
    )(depth, right_home, term_links, sector_rows, in_hbm(wavefunction))


def order_kernel(from_ref, links_ref, cols_ref, in_ref, out_ref):
    terms, count = links_ref.shape
    per_sector = count // cols_ref.shape[0]
    lane = lax.broadcasted_iota(jnp.int32, (SHARE, LANES), 1)
    targets = jnp.zeros(lane.shape, jnp.int32)
    for block in range(count):
        slot = from_ref[block]
        cols = cols_ref[block // per_sector]
        for part in range(2):
            value = in_ref[slot, part * SHARE : (part + 1) * SHARE, :]
            out_ref[block, part * SHARE : (part + 1) * SHARE, :] = jnp.where(
                lane + part * LANES < cols, value, jnp.zeros_like(value)
            )
        for term in range(terms):
            owner = lax.div(links_ref[term, block], count)
            targets = jnp.where(lane == term * count + block, owner, targets)
    targets = targets.astype(jnp.float32).astype(jnp.bfloat16)
    out_ref[count, 0:SHARE, :] = targets
    out_ref[count, SHARE:, :] = targets


def order(source, term_links, sector_cols, arrived):
    count = source.shape[0]
    return pl.pallas_call(
        order_kernel,
        in_specs=[SMEM, SMEM, SMEM, pl.BlockSpec(memory_space=pltpu.VMEM)],
        out_specs=pl.BlockSpec(memory_space=pltpu.VMEM),
        out_shape=jax.ShapeDtypeStruct((count + 1, 2 * SHARE, LANES), jnp.bfloat16),
        name="order_blocks",
    )(source, term_links, sector_cols, arrived)


def right_kernel(aliased, place_ref, targets_ref, slices_ref, *refs):
    envs, (out_ref, moved_ref, env_ref, slot_ref) = refs[: -4 - aliased], refs[-4:]
    group, _, terms, extent, width = out_ref.shape
    sectors = env_ref.shape[0]
    depth, count = slices_ref.shape[0], slices_ref.shape[2] - 1
    per_sector = count // sectors
    turn = pl.program_id(0)
    for index in range(len(envs) // terms):

        @pl.when(turn == index)
        def _(index=index):
            for term in range(terms):
                env = envs[index * terms + term][0]
                env_ref[:, :, term * width : (term + 1) * width] = env

    for sector in range(sectors):
        half = sector % 2
        for share in range(depth):
            for place in range(per_sector):
                at = slice(place * extent + share * SHARE, place * extent + (share + 1) * SHARE)
                block = sector * per_sector + place
                moved_ref[half, at, 0:LANES] = slices_ref[share, 0, block, 0:SHARE, :]
                moved_ref[half, at, LANES:] = slices_ref[share, 0, block, SHARE:, :]
        product = jnp.dot(moved_ref[half], env_ref[sector], preferred_element_type=jnp.float32)
        product = product.astype(jnp.bfloat16)
        for place in range(per_sector):
            for term in range(terms):
                owner = targets_ref[turn, term * count + sector * per_sector + place]

                here = lax.div(owner, group) == place_ref[0]
                slot_ref[jnp.where(here, lax.rem(owner, group), group), term] = product[
                    place * extent : (place + 1) * extent, term * width : (term + 1) * width
                ]
    out_ref[:, 0] = slot_ref[:group]


def right_products(place, targets, slices, envs, group, width, first=0, stride=1, into=None):
    depth, layers, blocks, tall, lanes = slices.shape
    terms = len(envs[0])
    sectors, extent = envs[0][0][0].shape[1:3]
    per_sector = (blocks - 1) // sectors
    flat = [pair for layer in envs for pair in layer]
    extra = [] if into is None else [into]
    return pl.pallas_call(
        functools.partial(right_kernel, len(extra)),
        grid_spec=pltpu.PrefetchScalarGridSpec(
            num_scalar_prefetch=2,
            grid=(len(envs),),
            in_specs=[
                pl.BlockSpec(
                    (depth, 1, blocks, tall, lanes),
                    lambda i, p, t: (0, first + stride * i, 0, 0, 0),
                )
            ]
            + [
                pl.BlockSpec((1, sectors, extent, width), lambda i, p, t, term=term: (term, 0, 0, 0))
                for _, term in flat
            ]
            + [pl.BlockSpec(memory_space=pl.ANY)] * len(extra),
            out_specs=pl.BlockSpec(
                (group, 1, terms, extent, width), lambda i, p, t: (0, first + stride * i, 0, 0, 0)
            ),
            scratch_shapes=[
                pltpu.VMEM((2, per_sector * extent, extent), jnp.bfloat16),
                pltpu.VMEM((sectors, extent, terms * width), jnp.bfloat16),
                pltpu.VMEM((group + 1, terms, extent, width), jnp.bfloat16),
            ],
        ),
        out_shape=pltpu.HBM((group, layers, terms, extent, width), jnp.bfloat16),
        input_output_aliases={3 + len(flat): 0} if extra else {},
        compiler_params=pltpu.CompilerParams(vmem_limit_bytes=VMEM_LIMIT),
        name="right_products",
    )(place, targets, in_hbm(slices), *[array for array, _ in flat], *extra)


def left_partials(place_ref, from_ref, near_ref, far_ref, env_ref, placed_ref):
    terms, count = from_ref.shape
    group, near, _, extent, width = near_ref.shape
    layers = near + far_ref.shape[1]
    per_sector = count // pl.num_programs(0)
    sector = pl.program_id(0)
    left = jnp.concatenate([env_ref[term, 0] for term in range(terms)], axis=1)
    for place in range(per_sector):
        for term in range(terms):
            device = from_ref[term, sector * per_sector + place]
            peer = lax.rem(device, group)
            step = lax.rem(lax.div(device, group) + layers - place_ref[0], layers)
            rows = slice(term * extent, (term + 1) * extent)
            columns = slice(place * width, (place + 1) * width)

            @pl.when(step < near)
            def _(term=term, peer=peer, step=step, rows=rows, columns=columns):
                placed_ref[rows, columns] = near_ref[peer, jnp.minimum(step, near - 1), term]

            @pl.when(step >= near)
            def _(term=term, peer=peer, step=step, rows=rows, columns=columns):
                placed_ref[rows, columns] = far_ref[peer, jnp.maximum(step - near, 0), term]

    partial = jnp.dot(left, placed_ref[...], preferred_element_type=jnp.float32)
    partial = partial.astype(jnp.bfloat16)
    for place in range(per_sector):
        yield place, partial[:, place * width : (place + 1) * width]


def left_kernel(place_ref, from_ref, near_ref, far_ref, env_ref, out_ref, placed_ref):
    for place, partial in left_partials(place_ref, from_ref, near_ref, far_ref, env_ref, placed_ref):
        out_ref[:, place] = partial.reshape(out_ref.shape[0], SHARE, partial.shape[1])


def left_split_kernel(place_ref, from_ref, near_ref, far_ref, env_ref, keep_ref, send_ref, placed_ref):
    chips = keep_ref.shape[0]
    core = place_ref[2]
    for place, partial in left_partials(place_ref, from_ref, near_ref, far_ref, env_ref, placed_ref):
        halves = [
            jnp.stack(
                [partial[(2 * c + k) * SHARE : (2 * c + k + 1) * SHARE] for c in range(chips)]
            )
            for k in range(2)
        ]
        keep_ref[:, place] = jnp.where(core == 0, halves[0], halves[1])
        send_ref[:, place] = jnp.where(core == 0, halves[1], halves[0])


def left_products(place, source, near, far, left_env, chunk, split):
    _, sectors, extent, _ = left_env.shape
    terms, count = source.shape
    width = far.shape[-1]
    per_sector = count // sectors
    pieces = extent // SHARE // (2 if split else 1)
    out_spec = pl.BlockSpec((pieces, per_sector, SHARE, width), lambda i: (0, i, 0, 0))
    shape = jax.ShapeDtypeStruct((pieces, count, SHARE, width), jnp.bfloat16)
    return pl.pallas_call(
        left_split_kernel if split else left_kernel,
        grid=(sectors,),
        in_specs=[
            SMEM,
            SMEM,
            pl.BlockSpec(near.shape[:-1] + (width,), lambda i: (0, 0, 0, 0, chunk)),
            pl.BlockSpec(far.shape, lambda i: (0, 0, 0, 0, 0)),
            pl.BlockSpec((terms, 1, extent, extent), lambda i: (0, i, 0, 0)),
        ],
        out_specs=[out_spec, out_spec] if split else out_spec,
        out_shape=[shape, shape] if split else shape,
        scratch_shapes=[pltpu.VMEM((terms * extent, per_sector * width), jnp.bfloat16)],
        compiler_params=pltpu.CompilerParams(vmem_limit_bytes=VMEM_LIMIT),
        name="left_products",
    )(place, source, near, far, left_env)


def shift(array, axis, step):
    size = lax.axis_size(axis)
    return lax.ppermute(array, axis, [(i, (i + step) % size) for i in range(size)])


def exchange(products):
    axes = ("zh", "zl", "x", "core")
    along_x, cores = lax.axis_size("x"), lax.axis_size("core")
    along_z = lax.axis_size("zh") * lax.axis_size("zl")
    groups = [
        [
            (((2 * pair + core + step) % along_z) * along_x + x) * cores + core
            for step in range(2)
            for x in range(along_x)
        ]
        for core in range(cores)
        for pair in range(along_z // 2)
    ]
    return lax.all_to_all(products, axes, 0, 0, axis_index_groups=groups, tiled=True)


def local(wavefunction, right_home, term_links, sector_rows, sector_cols, left_env, right_env):
    count, _, width = wavefunction.shape
    per_sector = count // sector_rows.shape[0]
    slots = lax.axis_size(REMAP)
    layers = lax.axis_size("zh")
    group = slots // layers
    terms = term_links.shape[0]
    layer = lax.axis_index("zh")
    core_index = lax.axis_index("core")
    depth_index = lax.axis_index("y") * 2 + core_index
    scheme_index = lax.rem(lax.axis_index(REMAP) + slots - core_index * (group // 2), slots)
    place = jnp.stack([scheme_index // group, lax.axis_index("y"), core_index])

    buffer = spread(depth_index.reshape(1), right_home, term_links, sector_rows, wavefunction, slots)
    arrived = lax.all_to_all(buffer, REMAP, 0, 0, tiled=True)
    labels = arrived[:, 2 * SHARE, : 1 + terms].astype(jnp.int32)
    match = labels.T[:, None, :] == jnp.arange(count, dtype=jnp.int32)[None, :, None]
    source = jnp.sum(jnp.where(match, jnp.arange(slots, dtype=jnp.int32), 0), axis=2)
    moved_by = slots - core_index * (group // 2)
    peers = lax.rem(source[1:] + moved_by, slots)
    ordered = order(source[0], term_links, sector_cols, arrived)

    parts = [right_env[..., at : at + LANES] for at in range(0, width, LANES)]
    above, below = shift(parts[0], "zh", -1), shift(parts[0], "zh", 1)
    across = shift(above[:1], "zh", -1), shift(below[1:], "zh", 1)

    slices = lax.all_gather(ordered[None], DEPTH)
    around = lax.all_gather(ordered, "zh")
    others = lax.dynamic_slice_in_dim(jnp.concatenate([around, around]), layer + 1, layers - 1)
    far_targets = others[:, count, 0, : terms * count].astype(jnp.int32)
    far_targets = lax.rem(far_targets + moved_by, slots)
    far_slices = lax.all_gather(others, DEPTH)

    targets = lax.rem((term_links // count).reshape(1, terms * count) + moved_by, slots)
    envs = [[(right_env, term) for term in range(terms)]]
    products = right_products(place, targets, slices, envs, group, width)
    after = products, above, below, parts[1]
    products, above, below, second = lax.optimization_barrier(after)
    own = exchange(products)

    next_above, next_below = shift(second, "zh", -1), shift(second, "zh", 1)
    next_across = shift(next_above[:1], "zh", -1), shift(next_below[1:], "zh", 1)

    envs = [
        [(above, 0), (above, 1)],
        [(across[0], 0), (across[1], 0)],
        [(below, 0), (below, 1)],
    ]
    products = right_products(place, far_targets, far_slices, envs, group, LANES)
    after = products, far_slices, next_above, next_below
    products, far_slices, next_above, next_below = lax.optimization_barrier(after)
    far = exchange(products)
    partial = left_products(place, peers, own, far, left_env, 0, False)
    partial = partial.reshape((-1, 2) + partial.shape[1:])
    summed = lax.psum_scatter(partial, "y", scatter_dimension=0, tiled=False)
    received = shift(lax.dynamic_index_in_dim(summed, 1 - core_index, 0, False), "core", 1)
    kept = lax.dynamic_index_in_dim(summed, core_index, 0, False)
    pieces = [kept.astype(jnp.float32) + received.astype(jnp.float32)]

    sides = jnp.stack([far_targets[0], far_targets[2]])
    envs = [[(next_above, 0), (next_above, 1)], [(next_below, 0), (next_below, 1)]]
    products = right_products(place, sides, far_slices, envs, group, LANES, 0, 2)
    envs = [[(next_across[0], 0), (next_across[1], 0)]]
    products = right_products(
        place, far_targets[1:2], far_slices, envs, group, LANES, 1, 1, products
    )
    far = exchange(products)
    keep, send = left_products(place, peers, own, far, left_env, 1, True)
    pair = keep.astype(jnp.float32) + shift(send, "core", 1).astype(jnp.float32)
    shares = lax.all_to_all(pair.astype(jnp.bfloat16), "y", 0, 0, tiled=True)
    pieces.append(jnp.sum(shares.astype(jnp.float32), axis=0))
    total = jnp.concatenate(pieces, axis=2)
    row = depth_index * SHARE + jnp.arange(SHARE, dtype=jnp.int32)
    keep_rows = row[None, :] < jnp.repeat(sector_rows, per_sector)[:, None]
    return jnp.where(keep_rows[:, :, None], total, 0.0).astype(jnp.bfloat16)


def solution(mesh):
    slots, depth = mesh.devices.shape
    split = Mesh(
        mesh.devices.reshape(4, 2, slots // 8, depth // 2, 2), ("zh", "zl", "x", "y", "core")
    )
    return jax.shard_map(
        local,
        mesh=split,
        in_specs=(
            P(REMAP, None, None),
            P(REMAP),
            P(DEPTH, REMAP),
            P(REMAP),
            P(REMAP),
            P(DEPTH, REMAP, None, None),
            P(DEPTH, REMAP, None, None),
        ),
        out_specs=P(REMAP, DEPTH, None),
        check_vma=False,
    )
```

```python
import functools

import jax
import jax.numpy as jnp
from jax import lax
from jax.experimental import pallas as pl
from jax.experimental.pallas import tpu as pltpu
from jax.sharding import Mesh, PartitionSpec as P

SHARE = 16
LANES = 128
VMEM_LIMIT = 40 * 1024 * 1024
REMAP = ("zh", "zl", "x")
DEPTH = ("y", "core")
SMEM = pl.BlockSpec(memory_space=pltpu.SMEM)


def in_hbm(array):
    return pltpu.with_memory_space_constraint(array, pltpu.HBM)


def spread_kernel(count, depth_ref, home_ref, links_ref, rows_ref, wave_ref, out_ref, label_ref):
    slots = out_ref.shape[0]
    terms = links_ref.shape[0]
    per_sector = count // rows_ref.shape[0]

    def clear(peer, carry):
        for kind in range(1 + terms):
            label_ref[kind, peer] = count
        return carry

    lax.fori_loop(0, slots, clear, 0)

    def fill(block, carry):
        home = home_ref[block]
        label_ref[0, lax.div(home, count)] = lax.rem(home, count)
        for term in range(terms):
            link = links_ref[term, block]
            label_ref[1 + term, lax.div(link, count)] = lax.rem(link, count)
        return carry

    lax.fori_loop(0, count, fill, 0)
    lane = lax.broadcasted_iota(jnp.int32, (SHARE, LANES), 1)

    def mark(peer, carry):
        tile = jnp.full(lane.shape, label_ref[0, peer], jnp.int32)
        for term in range(terms):
            tile = jnp.where(lane == 1 + term, label_ref[1 + term, peer], tile)
        out_ref[peer, 2 * SHARE :, :] = tile.astype(jnp.float32).astype(jnp.bfloat16)
        return carry

    lax.fori_loop(0, slots, mark, 0)
    row = lax.broadcasted_iota(jnp.int32, wave_ref.shape[1:], 0) + depth_ref[0] * SHARE

    def put(block, carry):
        owner = lax.div(home_ref[block], count)
        keep = row < rows_ref[lax.div(block, per_sector)]
        value = wave_ref[block]
        value = jnp.where(keep, value, jnp.zeros_like(value))
        out_ref[owner, 0:SHARE, :] = value[:, :LANES]
        out_ref[owner, SHARE : 2 * SHARE, :] = value[:, LANES:]
        return carry

    lax.fori_loop(0, count, put, 0)


def spread(depth, right_home, term_links, sector_rows, wavefunction, slots):
    count, _, width = wavefunction.shape
    return pl.pallas_call(
        functools.partial(spread_kernel, count),
        grid_spec=pltpu.PrefetchScalarGridSpec(
            num_scalar_prefetch=1,
            grid=(1,),
            in_specs=[
                SMEM,
                SMEM,
                SMEM,
                pl.BlockSpec((count, SHARE, width), lambda i, depth: (0, depth[0], 0)),
            ],
            out_specs=pl.BlockSpec((slots, 3 * SHARE, LANES), lambda i, depth: (0, 0, 0)),
            scratch_shapes=[pltpu.SMEM((1 + term_links.shape[0], slots), jnp.int32)],
        ),
        out_shape=pltpu.HBM((slots, 3 * SHARE, LANES), jnp.bfloat16),
        name="spread_blocks",
    )(depth, right_home, term_links, sector_rows, in_hbm(wavefunction))


def order_kernel(from_ref, links_ref, cols_ref, in_ref, out_ref):
    terms, count = links_ref.shape
    per_sector = count // cols_ref.shape[0]
    lane = lax.broadcasted_iota(jnp.int32, (SHARE, LANES), 1)
    targets = jnp.zeros(lane.shape, jnp.int32)
    for block in range(count):
        slot = from_ref[block]
        cols = cols_ref[block // per_sector]
        for part in range(2):
            value = in_ref[slot, part * SHARE : (part + 1) * SHARE, :]
            out_ref[block, part * SHARE : (part + 1) * SHARE, :] = jnp.where(
                lane + part * LANES < cols, value, jnp.zeros_like(value)
            )
        for term in range(terms):
            owner = lax.div(links_ref[term, block], count)
            targets = jnp.where(lane == term * count + block, owner, targets)
    targets = targets.astype(jnp.float32).astype(jnp.bfloat16)
    out_ref[count, 0:SHARE, :] = targets
    out_ref[count, SHARE:, :] = targets


def order(source, term_links, sector_cols, arrived):
    count = source.shape[0]
    return pl.pallas_call(
        order_kernel,
        in_specs=[SMEM, SMEM, SMEM, pl.BlockSpec(memory_space=pltpu.VMEM)],
        out_specs=pl.BlockSpec(memory_space=pltpu.VMEM),
        out_shape=jax.ShapeDtypeStruct((count + 1, 2 * SHARE, LANES), jnp.bfloat16),
        name="order_blocks",
    )(source, term_links, sector_cols, arrived)


def right_kernel(aliased, place_ref, targets_ref, slices_ref, *refs):
    envs, (out_ref, moved_ref, env_ref, slot_ref) = refs[: -4 - aliased], refs[-4:]
    group, _, terms, extent, width = out_ref.shape
    sectors = env_ref.shape[0]
    depth, count = slices_ref.shape[0], slices_ref.shape[2] - 1
    per_sector = count // sectors
    turn = pl.program_id(0)
    for index in range(len(envs) // terms):

        @pl.when(turn == index)
        def _(index=index):
            for term in range(terms):
                env = envs[index * terms + term][0]
                env_ref[:, :, term * width : (term + 1) * width] = env

    for sector in range(sectors):
        half = sector % 2
        for share in range(depth):
            for place in range(per_sector):
                at = slice(place * extent + share * SHARE, place * extent + (share + 1) * SHARE)
                block = sector * per_sector + place
                moved_ref[half, at, 0:LANES] = slices_ref[share, 0, block, 0:SHARE, :]
                moved_ref[half, at, LANES:] = slices_ref[share, 0, block, SHARE:, :]
        product = jnp.dot(moved_ref[half], env_ref[sector], preferred_element_type=jnp.float32)
        product = product.astype(jnp.bfloat16)
        for place in range(per_sector):
            for term in range(terms):
                owner = targets_ref[turn, term * count + sector * per_sector + place]

                here = lax.div(owner, group) == place_ref[0]
                slot_ref[jnp.where(here, lax.rem(owner, group), group), term] = product[
                    place * extent : (place + 1) * extent, term * width : (term + 1) * width
                ]
    out_ref[:, 0] = slot_ref[:group]


def right_products(place, targets, slices, envs, group, width, first=0, stride=1, into=None):
    depth, layers, blocks, tall, lanes = slices.shape
    terms = len(envs[0])
    sectors, extent = envs[0][0][0].shape[1:3]
    per_sector = (blocks - 1) // sectors
    flat = [pair for layer in envs for pair in layer]
    extra = [] if into is None else [into]
    return pl.pallas_call(
        functools.partial(right_kernel, len(extra)),
        grid_spec=pltpu.PrefetchScalarGridSpec(
            num_scalar_prefetch=2,
            grid=(len(envs),),
            in_specs=[
                pl.BlockSpec(
                    (depth, 1, blocks, tall, lanes),
                    lambda i, p, t: (0, first + stride * i, 0, 0, 0),
                )
            ]
            + [
                pl.BlockSpec((1, sectors, extent, width), lambda i, p, t, term=term: (term, 0, 0, 0))
                for _, term in flat
            ]
            + [pl.BlockSpec(memory_space=pl.ANY)] * len(extra),
            out_specs=pl.BlockSpec(
                (group, 1, terms, extent, width), lambda i, p, t: (0, first + stride * i, 0, 0, 0)
            ),
            scratch_shapes=[
                pltpu.VMEM((2, per_sector * extent, extent), jnp.bfloat16),
                pltpu.VMEM((sectors, extent, terms * width), jnp.bfloat16),
                pltpu.VMEM((group + 1, terms, extent, width), jnp.bfloat16),
            ],
        ),
        out_shape=pltpu.HBM((group, layers, terms, extent, width), jnp.bfloat16),
        input_output_aliases={3 + len(flat): 0} if extra else {},
        compiler_params=pltpu.CompilerParams(vmem_limit_bytes=VMEM_LIMIT),
        name="right_products",
    )(place, targets, in_hbm(slices), *[array for array, _ in flat], *extra)


def left_partials(place_ref, from_ref, near_ref, far_ref, env_ref, placed_ref):
    terms, count = from_ref.shape
    group, near, _, extent, width = near_ref.shape
    layers = near + far_ref.shape[1]
    per_sector = count // pl.num_programs(0)
    sector = pl.program_id(0)
    left = jnp.concatenate([env_ref[term, 0] for term in range(terms)], axis=1)
    for place in range(per_sector):
        for term in range(terms):
            device = from_ref[term, sector * per_sector + place]
            peer = lax.rem(device, group)
            step = lax.rem(lax.div(device, group) + layers - place_ref[0], layers)
            rows = slice(term * extent, (term + 1) * extent)
            columns = slice(place * width, (place + 1) * width)

            @pl.when(step < near)
            def _(term=term, peer=peer, step=step, rows=rows, columns=columns):
                placed_ref[rows, columns] = near_ref[peer, jnp.minimum(step, near - 1), term]

            @pl.when(step >= near)
            def _(term=term, peer=peer, step=step, rows=rows, columns=columns):
                placed_ref[rows, columns] = far_ref[peer, jnp.maximum(step - near, 0), term]

    partial = jnp.dot(left, placed_ref[...], preferred_element_type=jnp.float32)
    partial = partial.astype(jnp.bfloat16)
    for place in range(per_sector):
        yield place, partial[:, place * width : (place + 1) * width]


def left_kernel(place_ref, from_ref, near_ref, far_ref, env_ref, out_ref, placed_ref):
    for place, partial in left_partials(place_ref, from_ref, near_ref, far_ref, env_ref, placed_ref):
        out_ref[:, place] = partial.reshape(out_ref.shape[0], SHARE, partial.shape[1])


def left_split_kernel(place_ref, from_ref, near_ref, far_ref, env_ref, keep_ref, send_ref, placed_ref):
    chips = keep_ref.shape[0]
    core = place_ref[2]
    for place, partial in left_partials(place_ref, from_ref, near_ref, far_ref, env_ref, placed_ref):
        halves = [
            jnp.stack(
                [partial[(2 * c + k) * SHARE : (2 * c + k + 1) * SHARE] for c in range(chips)]
            )
            for k in range(2)
        ]
        keep_ref[:, place] = jnp.where(core == 0, halves[0], halves[1])
        send_ref[:, place] = jnp.where(core == 0, halves[1], halves[0])


def left_products(place, source, near, far, left_env, chunk, split):
    _, sectors, extent, _ = left_env.shape
    terms, count = source.shape
    width = far.shape[-1]
    per_sector = count // sectors
    pieces = extent // SHARE // (2 if split else 1)
    out_spec = pl.BlockSpec((pieces, per_sector, SHARE, width), lambda i: (0, i, 0, 0))
    shape = jax.ShapeDtypeStruct((pieces, count, SHARE, width), jnp.bfloat16)
    return pl.pallas_call(
        left_split_kernel if split else left_kernel,
        grid=(sectors,),
        in_specs=[
            SMEM,
            SMEM,
            pl.BlockSpec(near.shape[:-1] + (width,), lambda i: (0, 0, 0, 0, chunk)),
            pl.BlockSpec(far.shape, lambda i: (0, 0, 0, 0, 0)),
            pl.BlockSpec((terms, 1, extent, extent), lambda i: (0, i, 0, 0)),
        ],
        out_specs=[out_spec, out_spec] if split else out_spec,
        out_shape=[shape, shape] if split else shape,
        scratch_shapes=[pltpu.VMEM((terms * extent, per_sector * width), jnp.bfloat16)],
        compiler_params=pltpu.CompilerParams(vmem_limit_bytes=VMEM_LIMIT),
        name="left_products",
    )(place, source, near, far, left_env)


def shift(array, axis, step):
    size = lax.axis_size(axis)
    return lax.ppermute(array, axis, [(i, (i + step) % size) for i in range(size)])


def exchange(products):
    axes = ("zh", "zl", "x", "core")
    along_x, cores = lax.axis_size("x"), lax.axis_size("core")
    along_z = lax.axis_size("zh") * lax.axis_size("zl")
    groups = [
        [
            (((2 * pair + core + step) % along_z) * along_x + x) * cores + core
            for step in range(2)
            for x in range(along_x)
        ]
        for core in range(cores)
        for pair in range(along_z // 2)
    ]
    return lax.all_to_all(products, axes, 0, 0, axis_index_groups=groups, tiled=True)


def local(wavefunction, right_home, term_links, sector_rows, sector_cols, left_env, right_env):
    count, _, width = wavefunction.shape
    per_sector = count // sector_rows.shape[0]
    slots = lax.axis_size(REMAP)
    layers = lax.axis_size("zh")
    group = slots // layers
    terms = term_links.shape[0]
    layer = lax.axis_index("zh")
    core_index = lax.axis_index("core")
    depth_index = lax.axis_index("y") * 2 + core_index
    scheme_index = lax.rem(lax.axis_index(REMAP) + slots - core_index * (group // 2), slots)
    place = jnp.stack([scheme_index // group, lax.axis_index("y"), core_index])

    buffer = spread(depth_index.reshape(1), right_home, term_links, sector_rows, wavefunction, slots)
    arrived = lax.all_to_all(buffer, REMAP, 0, 0, tiled=True)
    labels = arrived[:, 2 * SHARE, : 1 + terms].astype(jnp.int32)
    match = labels.T[:, None, :] == jnp.arange(count, dtype=jnp.int32)[None, :, None]
    source = jnp.sum(jnp.where(match, jnp.arange(slots, dtype=jnp.int32), 0), axis=2)
    moved_by = slots - core_index * (group // 2)
    peers = lax.rem(source[1:] + moved_by, slots)
    ordered = order(source[0], term_links, sector_cols, arrived)

    parts = [right_env[..., at : at + LANES] for at in range(0, width, LANES)]
    above, below = shift(parts[0], "zh", -1), shift(parts[0], "zh", 1)
    across = shift(above[:1], "zh", -1), shift(below[1:], "zh", 1)

    slices = lax.all_gather(ordered[None], DEPTH)
    around = lax.all_gather(ordered, "zh")
    others = lax.dynamic_slice_in_dim(jnp.concatenate([around, around]), layer + 1, layers - 1)
    far_targets = others[:, count, 0, : terms * count].astype(jnp.int32)
    far_targets = lax.rem(far_targets + moved_by, slots)
    far_slices = lax.all_gather(others, DEPTH)

    targets = lax.rem((term_links // count).reshape(1, terms * count) + moved_by, slots)
    envs = [[(right_env, term) for term in range(terms)]]
    products = right_products(place, targets, slices, envs, group, width)
    products, above, below = lax.optimization_barrier((products, above, below))
    own = exchange(products)

    across, second = lax.optimization_barrier((across, parts[1]))
    next_above, next_below = shift(second[:1], "zh", -1), shift(second[:1], "zh", 1)
    late_above, late_below = shift(second[1:], "zh", -1), shift(second[1:], "zh", 1)
    next_across = shift(next_above, "zh", -1), shift(late_below, "zh", 1)

    envs = [
        [(above, 0), (above, 1)],
        [(across[0], 0), (across[1], 0)],
        [(below, 0), (below, 1)],
    ]
    products = right_products(place, far_targets, far_slices, envs, group, LANES)
    after = products, far_slices, next_above, next_below
    products, far_slices, next_above, next_below = lax.optimization_barrier(after)
    far = exchange(products)
    partial = left_products(place, peers, own, far, left_env, 0, False)
    partial = partial.reshape((-1, 2) + partial.shape[1:])
    summed = lax.psum_scatter(partial, "y", scatter_dimension=0, tiled=False)
    received = shift(lax.dynamic_index_in_dim(summed, 1 - core_index, 0, False), "core", 1)
    kept = lax.dynamic_index_in_dim(summed, core_index, 0, False)
    pieces = [kept.astype(jnp.float32) + received.astype(jnp.float32)]

    sides = jnp.stack([far_targets[0], far_targets[2]])
    envs = [[(next_above, 0), (late_above, 0)], [(next_below, 0), (late_below, 0)]]
    products = right_products(place, sides, far_slices, envs, group, LANES, 0, 2)
    envs = [[(next_across[0], 0), (next_across[1], 0)]]
    products = right_products(
        place, far_targets[1:2], far_slices, envs, group, LANES, 1, 1, products
    )
    far = exchange(products)
    keep, send = left_products(place, peers, own, far, left_env, 1, True)
    pair = keep.astype(jnp.float32) + shift(send, "core", 1).astype(jnp.float32)
    shares = lax.all_to_all(pair.astype(jnp.bfloat16), "y", 0, 0, tiled=True)
    pieces.append(jnp.sum(shares.astype(jnp.float32), axis=0))
    total = jnp.concatenate(pieces, axis=2)
    row = depth_index * SHARE + jnp.arange(SHARE, dtype=jnp.int32)
    keep_rows = row[None, :] < jnp.repeat(sector_rows, per_sector)[:, None]
    return jnp.where(keep_rows[:, :, None], total, 0.0).astype(jnp.bfloat16)


def solution(mesh):
    slots, depth = mesh.devices.shape
    split = Mesh(
        mesh.devices.reshape(4, 2, slots // 8, depth // 2, 2), ("zh", "zl", "x", "y", "core")
    )
    return jax.shard_map(
        local,
        mesh=split,
        in_specs=(
            P(REMAP, None, None),
            P(REMAP),
            P(DEPTH, REMAP),
            P(REMAP),
            P(REMAP),
            P(DEPTH, REMAP, None, None),
            P(DEPTH, REMAP, None, None),
        ),
        out_specs=P(REMAP, DEPTH, None),
        check_vma=False,
    )
```
